512 devices in a mesh: gauss: 64 (over z, y), cam: 8 (over x, core).
Axes of the slice: x: 4, y: 8, z: 8, core: 2. Of those that a mesh axis runs over, the one named last changes fastest.
Arguments:
- attributes: float32 [59, 65536], P(None, 'gauss'), may hold values from -6 to 1.5, as said below
- cameras: float32 [8, 8], P('cam'), may hold values from -0.5 to 5, as said below
- tile_ids: int32 [8, 64, 8, 128], P('cam', 'gauss'), may hold values from -1 to 65535, as said below
- depth_order: int32 [8, 64, 8, 128], P('cam', 'gauss'), may hold values from 0 to 127, each once within a row
- target: float32 [8, 3, 1024, 128], P('cam', None, 'gauss'), may hold values from 0 to 1
Outputs:
- rendered: float32 [8, 3, 1024, 128], P('cam', None, 'gauss')
- grad_attributes: float32 [59, 65536], P(None, ('gauss', 'cam'))
The draws below stay inside these ranges and needn't reach their ends.
Inputs may be any that keep to these rules, and one draw needn't show every extreme that they name: `tile_ids`: -1 marks an empty slot; of the 1024 slots of one view's row of tiles at most 16 name Gaussians of one block (ids o * 1024 to o * 1024 + 1023), and in every view one block is named by exactly 16 slots of every row of tiles. `attributes`: rows 0-2 lie in [-1, 1], rows 3-5 in [log 0.08, log 0.4], row 6 in [0.5, 1.5], rows 7-9 in [-0.5, 0.5], row 10 in [-6, -2], rows 11 to 13 in [-0.5, 1.5], the rest in [-1, 1]. `cameras`: column 0 lies in [0.5, 1.5], columns 1-3 in [-0.5, 0.5], columns 4-5 in [-0.3, 0.3], column 6 in [3, 5], column 7 in [2, 3].
All inputs are finite; a program needn't handle non-finite values.
Results may differ from the reference program's by a relative error of at most 0.0003.
Values sent between devices are 32-bit elements; how exact they have to be, the bound alone decides.
A program may use at most 64 MiB of HBM per device.

```python
import math
import jax
import jax.numpy as jnp
from jax import lax

GL = 1024
TCOLS = 8
LIST = 128
OWNERS = 64
TROWS = 64
CAMS = 8
G = 65536
W = 128
H = 1024
CAP = 16


def draw_attributes(key, part):
    key = jax.random.fold_in(key, 3)
    sub_keys = jax.random.split(key, 7)
    position = jax.random.uniform(sub_keys[0], (3, G), minval=-1.0, maxval=1.0)
    higher = jnp.clip(0.3 * jax.random.normal(sub_keys[6], (45, G)), -1.0, 1.0)
    log_scale = jax.random.uniform(sub_keys[1], (3, G), minval=math.log(0.08), maxval=math.log(0.4))
    quat_first = jax.random.uniform(sub_keys[2], (1, G), minval=0.5, maxval=1.5)
    quat_rest = jax.random.uniform(sub_keys[3], (3, G), minval=-0.5, maxval=0.5)
    opacity = jax.random.uniform(sub_keys[4], (1, G), minval=-6.0, maxval=-2.0)
    base_colour = jax.random.uniform(sub_keys[5], (3, G), minval=-0.5, maxval=1.5)
    return jnp.concatenate([position, log_scale, quat_first, quat_rest, opacity, base_colour, higher], 0).astype(jnp.float32)


def draw_cameras(key, part):
    key = jax.random.fold_in(key, 5)
    sub_keys = jax.random.split(key, 5)
    quat_first = jax.random.uniform(sub_keys[0], (CAMS, 1), minval=0.5, maxval=1.5)
    quat_rest = jax.random.uniform(sub_keys[1], (CAMS, 3), minval=-0.5, maxval=0.5)
    sideways = jax.random.uniform(sub_keys[2], (CAMS, 2), minval=-0.3, maxval=0.3)
    distance = jax.random.uniform(sub_keys[3], (CAMS, 1), minval=3.0, maxval=5.0)
    focal = jax.random.uniform(sub_keys[4], (CAMS, 1), minval=2.0, maxval=3.0)
    return jnp.concatenate([quat_first, quat_rest, sideways, distance, focal], 1).astype(jnp.float32)


def draw_tile_ids(key, part):
    key = jax.random.fold_in(key, 7)
    sub_keys = jax.random.split(key, 5)
    grid_shape = (CAMS, TROWS, TCOLS, LIST)
    hot_owner = jax.random.randint(sub_keys[0], (CAMS, 1, 1, 1), 0, OWNERS)
    lengths = jax.random.randint(sub_keys[1], (CAMS, TROWS, TCOLS, 1), LIST // 4, LIST + 1)
    present = jnp.arange(LIST, dtype=jnp.int32) < lengths
    is_hot = jax.random.randint(sub_keys[2], grid_shape, 0, 4) == 0
    owner_ids = jnp.where(is_hot, hot_owner, jax.random.randint(sub_keys[3], grid_shape, 0, OWNERS))
    local_ids = jax.random.randint(sub_keys[4], grid_shape, 0, GL)
    flat_owner = owner_ids.reshape(CAMS * TROWS, TCOLS * LIST)
    flat_present = present.reshape(CAMS * TROWS, TCOLS * LIST)

    def ranks(row_in):
        member = ((row_in[0][None, :] == jnp.arange(OWNERS, dtype=jnp.int32)[:, None]) & row_in[1][None, :]).astype(jnp.int32)
        return jnp.sum(member * jnp.cumsum(member, axis=1), axis=0) - 1
    slot_order = lax.map(ranks, (flat_owner, flat_present)).reshape(grid_shape)
    keep = present & (slot_order < CAP)
    return jnp.where(keep, owner_ids * GL + local_ids, -1).astype(jnp.int32)


def steps_of(stream_key, extent, shards, low, largest):
    gain = 1.0
    for axis_at, blocks in shards:
        draws = jax.random.uniform(jax.random.fold_in(jax.random.fold_in(stream_key, 6), axis_at), (blocks,), jnp.float32, low / len(shards), largest / len(shards))
        gain = gain * jnp.repeat(jnp.exp(draws), extent[axis_at] // blocks).reshape((-1,) + (1,) * (len(extent) - 1 - axis_at))
    return gain


def setup_inputs(seed: int = 0) -> dict:
    key_of = jax.random.split(jax.random.key(seed), 6)
    attributes = draw_attributes(jax.random.fold_in(key_of[5], 71), 0)
    cameras = draw_cameras(jax.random.fold_in(key_of[5], 71), 0)
    tile_ids = draw_tile_ids(jax.random.fold_in(key_of[5], 71), 0)
    depth_order = jax.vmap(lambda own: jax.random.permutation(own, LIST))(jax.random.split(key_of[3], CAMS * TROWS * TCOLS)).reshape((CAMS, TROWS, TCOLS, LIST)).astype(jnp.int32)
    target = jnp.clip(1.0 * jax.random.uniform(key_of[4], (CAMS, 3, H, W), jnp.float32) ** steps_of(key_of[4], (CAMS, 3, H, W), ((0, 8), (2, 64)), -0.2, 0.2), 0.0, 1.0)
    return {"attributes": attributes, "cameras": cameras, "tile_ids": tile_ids, "depth_order": depth_order, "target": target}


tile_side = 16
window_raw = [math.exp(-(offset - 5) ** 2 / 4.5) for offset in range(11)]
window = [weight / sum(window_raw) for weight in window_raw]
sh_consts = [0.0, -0.4886025119029199, 0.4886025119029199, -0.4886025119029199, 1.0925484305920792, -1.0925484305920792, 0.31539156525252005, -1.0925484305920792, 0.5462742152960396, -0.5900435899266435, 2.890611442640554, -0.4570457994644658, 0.3731763325901154, -0.4570457994644658, 1.445305721320277, -0.5900435899266435]

def unit_quat(parts):
    length_q = jnp.sqrt(parts[0] * parts[0] + parts[1] * parts[1] + parts[2] * parts[2] + parts[3] * parts[3])
    return [part / length_q for part in parts]

def quat_matrix(quaternion):
    q_w, q_x, q_y, q_z = quaternion
    return [[1.0 - 2.0 * (q_y * q_y + q_z * q_z), 2.0 * (q_x * q_y - q_w * q_z), 2.0 * (q_x * q_z + q_w * q_y)], [2.0 * (q_x * q_y + q_w * q_z), 1.0 - 2.0 * (q_x * q_x + q_z * q_z), 2.0 * (q_y * q_z - q_w * q_x)], [2.0 * (q_x * q_z - q_w * q_y), 2.0 * (q_y * q_z + q_w * q_x), 1.0 - 2.0 * (q_x * q_x + q_y * q_y)]]

def project(attr_rows, camera, image_width, height):
    cam_rot = quat_matrix(unit_quat([camera[0], camera[1], camera[2], camera[3]]))
    shift_vec = [camera[4], camera[5], camera[6]]
    horizontal_focal = camera[7] * image_width
    focal_y = camera[7] * height
    position = [attr_rows[0], attr_rows[1], attr_rows[2]]
    view_pos = [cam_rot[axis_row][0] * position[0] + cam_rot[axis_row][1] * position[1] + cam_rot[axis_row][2] * position[2] + shift_vec[axis_row] for axis_row in range(3)]
    inv_z = 1.0 / view_pos[2]
    mean_u = 0.5 * image_width + horizontal_focal * view_pos[0] * inv_z
    mean_v = 0.5 * height + focal_y * view_pos[1] * inv_z
    gauss_rot = quat_matrix(unit_quat([attr_rows[6], attr_rows[7], attr_rows[8], attr_rows[9]]))
    scales = [jnp.exp(attr_rows[3]), jnp.exp(attr_rows[4]), jnp.exp(attr_rows[5])]
    factor = [[gauss_rot[axis_row][axis_col] * scales[axis_col] for axis_col in range(3)] for axis_row in range(3)]
    sigma = [[factor[axis_row][0] * factor[axis_col][0] + factor[axis_row][1] * factor[axis_col][1] + factor[axis_row][2] * factor[axis_col][2] for axis_col in range(3)] for axis_row in range(3)]
    jacobian = [[horizontal_focal * inv_z, 0.0, -horizontal_focal * view_pos[0] * inv_z * inv_z], [0.0, focal_y * inv_z, -focal_y * view_pos[1] * inv_z * inv_z]]
    project_mat = [[jacobian[axis_row][0] * cam_rot[0][axis_col] + jacobian[axis_row][1] * cam_rot[1][axis_col] + jacobian[axis_row][2] * cam_rot[2][axis_col] for axis_col in range(3)] for axis_row in range(2)]
    screen_covariance = [[sum([project_mat[axis_row][inner_idx] * sigma[inner_idx][outer_idx] * project_mat[axis_col][outer_idx] for inner_idx in range(3) for outer_idx in range(3)]) for axis_col in range(2)] for axis_row in range(2)]
    cov_a = screen_covariance[0][0] + 0.3
    cov_b = screen_covariance[0][1]
    cov_c = screen_covariance[1][1] + 0.3
    determinant = cov_a * cov_c - cov_b * cov_b
    opacity = jax.nn.sigmoid(attr_rows[10])
    centre = [-(cam_rot[0][axis_col] * shift_vec[0] + cam_rot[1][axis_col] * shift_vec[1] + cam_rot[2][axis_col] * shift_vec[2]) for axis_col in range(3)]
    offsets = [position[axis_col] - centre[axis_col] for axis_col in range(3)]
    distance = jnp.sqrt(offsets[0] * offsets[0] + offsets[1] * offsets[1] + offsets[2] * offsets[2])
    dir_x, dir_y, dir_z = (offsets[0] / distance, offsets[1] / distance, offsets[2] / distance)
    sq_x, sq_y, sq_z = (dir_x * dir_x, dir_y * dir_y, dir_z * dir_z)
    sh_basis = [None, dir_y, dir_z, dir_x, dir_x * dir_y, dir_y * dir_z, 2.0 * sq_z - sq_x - sq_y, dir_x * dir_z, sq_x - sq_y, dir_y * (3.0 * sq_x - sq_y), dir_x * dir_y * dir_z, dir_y * (4.0 * sq_z - sq_x - sq_y), dir_z * (2.0 * sq_z - 3.0 * sq_x - 3.0 * sq_y), dir_x * (4.0 * sq_z - sq_x - sq_y), dir_z * (sq_x - sq_y), dir_x * (sq_x - 3.0 * sq_y)]
    colours = []
    for channel in range(3):
        colour = 0.5 + 0.28209479177387814 * attr_rows[11 + channel]
        for degree in range(1, 16):
            colour = colour + sh_consts[degree] * sh_basis[degree] * attr_rows[11 + 3 * degree + channel]
        colours.append(colour)
    return jnp.stack([mean_u, mean_v, cov_c / determinant, -cov_b / determinant, cov_a / determinant, opacity, colours[0], colours[1], colours[2]])

def tile_colours(colour_features, first_row, leading_columns):
    pixel = jnp.arange(tile_side * tile_side, dtype=jnp.int32)
    pix_row = (first_row + pixel // tile_side).astype(jnp.float32) + 0.5
    pix_col = (leading_columns[:, None] + pixel[None, :] % tile_side).astype(jnp.float32) + 0.5
    off_u = pix_col[:, :, None] - colour_features[0][:, None, :]
    off_v = pix_row[None, :, None] - colour_features[1][:, None, :]
    exponent = -0.5 * (colour_features[2][:, None, :] * off_u * off_u + colour_features[4][:, None, :] * off_v * off_v) - colour_features[3][:, None, :] * off_u * off_v
    alphas = colour_features[5][:, None, :] * jnp.exp(exponent)
    retained_log_scales = jnp.log1p(-alphas)
    transmit = jnp.exp(jnp.cumsum(retained_log_scales, axis=-1) - retained_log_scales)
    blend_weights = alphas * transmit
    return jnp.einsum('nui,vni->nvu', blend_weights, colour_features[6:9], precision=lax.Precision.HIGHEST)

def to_image(colours):
    tile_rows, tile_cols = (colours.shape[0], colours.shape[1])
    blocks = colours.reshape(tile_rows, tile_cols, 3, tile_side, tile_side)
    return blocks.transpose(2, 0, 3, 1, 4).reshape(3, tile_rows * tile_side, tile_cols * tile_side)

def to_tiles(picture):
    tile_rows, tile_cols = (picture.shape[1] // tile_side, picture.shape[2] // tile_side)
    blocks = picture.reshape(3, tile_rows, tile_side, tile_cols, tile_side)
    return blocks.transpose(1, 3, 0, 2, 4).reshape(tile_rows, tile_cols, 3, tile_side * tile_side)

def gauss_blur(grid_in):
    col_count = grid_in.shape[-1]
    row_count = grid_in.shape[-2] - 10
    padded = jnp.pad(grid_in, [(0, 0)] * (grid_in.ndim - 1) + [(5, 5)])
    across = window[0] * padded[..., 0:col_count]
    for offset in range(1, 11):
        across = across + window[offset] * padded[..., offset:offset + col_count]
    result = window[0] * across[..., 0:row_count, :]
    for offset in range(1, 11):
        result = result + window[offset] * across[..., offset:offset + row_count, :]
    return result

def ssim_loss(ext_image, ext_target):
    mean_x = gauss_blur(ext_image)
    mean_y = gauss_blur(ext_target)
    var_x = gauss_blur(ext_image * ext_image) - mean_x * mean_x
    var_y = gauss_blur(ext_target * ext_target) - mean_y * mean_y
    cov_xy = gauss_blur(ext_image * ext_target) - mean_x * mean_y
    ssim_map = (2.0 * mean_x * mean_y + 0.0001) * (2.0 * cov_xy + 0.0009) / ((mean_x * mean_x + mean_y * mean_y + 0.0001) * (var_x + var_y + 0.0009))
    own_diff = ext_image[..., 5:-5, :] - ext_target[..., 5:-5, :]
    return jnp.sum(0.8 * jnp.sqrt(own_diff * own_diff + 0.0025) + 0.2 * (1.0 - ssim_map)) / 256.0

def reference(attributes, cameras, tile_ids, depth_order, target):
    tile_rows = tile_ids.shape[1]
    tile_cols = tile_ids.shape[2]
    image_width = tile_side * tile_cols
    height = tile_side * tile_rows
    ordered = jnp.take_along_axis(tile_ids, depth_order, axis=3)
    leading_columns = jnp.arange(tile_cols, dtype=jnp.int32) * tile_side
    row_starts = jnp.arange(tile_rows, dtype=jnp.int32) * tile_side

    def one_view(grad_total, view_in):
        camera, view_ids, view_target = view_in
        feature_table, project_back = jax.vjp(lambda values: project(values, camera, image_width, height), attributes)
        present = view_ids >= 0
        safe_ids = jnp.where(present, view_ids, 0)
        gathered = jnp.where(present[None], feature_table[:, safe_ids], 0.0)
        by_row = jnp.moveaxis(gathered, 1, 0)

        def render_row(row_in):
            return tile_colours(row_in[0], row_in[1], leading_columns)
        picture = to_image(lax.map(render_row, (by_row, row_starts)))

        def view_loss(values):
            return ssim_loss(jnp.pad(values, [(0, 0), (5, 5), (0, 0)]), jnp.pad(view_target, [(0, 0), (5, 5), (0, 0)]))
        _, loss_back = jax.vjp(view_loss, picture)
        picture_grad, = loss_back(jnp.ones((), jnp.float32))
        row_cots = to_tiles(picture_grad)

        def back_row(row_in):
            _, pullback = jax.vjp(lambda values: tile_colours(values, row_in[1], leading_columns), row_in[0])
            return pullback(row_in[2])[0]
        feat_grads = jnp.moveaxis(lax.map(back_row, (by_row, row_starts, row_cots)), 0, 1)
        feat_grads = jnp.where(present[None], feat_grads, 0.0)
        summed = jnp.zeros_like(feature_table).at[:, safe_ids.reshape(-1)].add(feat_grads.reshape(9, -1))
        attr_grad, = project_back(summed)
        return (grad_total + attr_grad, picture)
    grad_sum, pictures = lax.scan(one_view, jnp.zeros_like(attributes), (cameras, ordered, target))
    return (pictures, grad_sum)
```

```python
import math

import jax
import jax.numpy as jnp
from jax import lax
from jax.experimental import pallas as pl
from jax.experimental.pallas import tpu as pltpu
from jax.sharding import PartitionSpec as P

MESH = pl.DeviceIdType.MESH
peers = 64
views = 8
tile_side = 16
tiles = 8
slots = 128
lanes = 128
capacity = 16
image_width = 128.0
image_height = 1024.0
f32 = jnp.float32
window_raw = [math.exp(-((offset - 5) ** 2) / 4.5) for offset in range(11)]
window = [weight / sum(window_raw) for weight in window_raw]
sh_consts = [
    0.0,
    -0.4886025119029199,
    0.4886025119029199,
    -0.4886025119029199,
    1.0925484305920792,
    -1.0925484305920792,
    0.31539156525252005,
    -1.0925484305920792,
    0.5462742152960396,
    -0.5900435899266435,
    2.890611442640554,
    -0.4570457994644658,
    0.3731763325901154,
    -0.4570457994644658,
    1.445305721320277,
    -0.5900435899266435,
]


def unit_quat(parts):
    length_q = jnp.sqrt(
        parts[0] * parts[0] + parts[1] * parts[1] + parts[2] * parts[2] + parts[3] * parts[3]
    )
    return [part / length_q for part in parts]


def quat_matrix(quaternion):
    q_w, q_x, q_y, q_z = quaternion
    return [
        [
            1.0 - 2.0 * (q_y * q_y + q_z * q_z),
            2.0 * (q_x * q_y - q_w * q_z),
            2.0 * (q_x * q_z + q_w * q_y),
        ],
        [
            2.0 * (q_x * q_y + q_w * q_z),
            1.0 - 2.0 * (q_x * q_x + q_z * q_z),
            2.0 * (q_y * q_z - q_w * q_x),
        ],
        [
            2.0 * (q_x * q_z - q_w * q_y),
            2.0 * (q_y * q_z + q_w * q_x),
            1.0 - 2.0 * (q_x * q_x + q_y * q_y),
        ],
    ]


def camera_terms(camera):
    cam_rot = quat_matrix(unit_quat(camera[0:4]))
    shift_vec = camera[4:7]
    centre = [
        -(
            cam_rot[0][axis_col] * shift_vec[0]
            + cam_rot[1][axis_col] * shift_vec[1]
            + cam_rot[2][axis_col] * shift_vec[2]
        )
        for axis_col in range(3)
    ]
    return cam_rot, shift_vec, camera[7] * image_width, camera[7] * image_height, centre


def project(attr_rows, camera):
    cam_rot, shift_vec, horizontal_focal, focal_y, centre = camera
    position = [attr_rows[0], attr_rows[1], attr_rows[2]]
    view_pos = [
        cam_rot[axis_row][0] * position[0]
        + cam_rot[axis_row][1] * position[1]
        + cam_rot[axis_row][2] * position[2]
        + shift_vec[axis_row]
        for axis_row in range(3)
    ]
    inv_z = 1.0 / view_pos[2]
    focal_u = horizontal_focal * inv_z
    focal_v = focal_y * inv_z
    slope_u = focal_u * view_pos[0]
    slope_v = focal_v * view_pos[1]
    mean_u = 0.5 * image_width + slope_u
    mean_v = 0.5 * image_height + slope_v
    gauss_rot = quat_matrix(unit_quat([attr_rows[6], attr_rows[7], attr_rows[8], attr_rows[9]]))
    scales = [jnp.exp(attr_rows[3]), jnp.exp(attr_rows[4]), jnp.exp(attr_rows[5])]
    skew_u = slope_u * inv_z
    skew_v = slope_v * inv_z
    project_mat = [
        [focal_u * cam_rot[0][axis_col] - skew_u * cam_rot[2][axis_col] for axis_col in range(3)],
        [focal_v * cam_rot[1][axis_col] - skew_v * cam_rot[2][axis_col] for axis_col in range(3)],
    ]
    spread = [
        [
            (
                project_mat[axis_row][0] * gauss_rot[0][axis_col]
                + project_mat[axis_row][1] * gauss_rot[1][axis_col]
                + project_mat[axis_row][2] * gauss_rot[2][axis_col]
            )
            * scales[axis_col]
            for axis_col in range(3)
        ]
        for axis_row in range(2)
    ]
    cov_a = spread[0][0] * spread[0][0] + spread[0][1] * spread[0][1] + spread[0][2] * spread[0][2] + 0.3
    cov_b = spread[0][0] * spread[1][0] + spread[0][1] * spread[1][1] + spread[0][2] * spread[1][2]
    cov_c = spread[1][0] * spread[1][0] + spread[1][1] * spread[1][1] + spread[1][2] * spread[1][2] + 0.3
    inv_det = 1.0 / (cov_a * cov_c - cov_b * cov_b)
    offsets = [position[axis_col] - centre[axis_col] for axis_col in range(3)]
    distance = jnp.sqrt(offsets[0] * offsets[0] + offsets[1] * offsets[1] + offsets[2] * offsets[2])
    inv_distance = 1.0 / distance
    dir_x, dir_y, dir_z = [offset * inv_distance for offset in offsets]
    sq_x, sq_y, sq_z = (dir_x * dir_x, dir_y * dir_y, dir_z * dir_z)
    sh_basis = [
        None,
        dir_y,
        dir_z,
        dir_x,
        dir_x * dir_y,
        dir_y * dir_z,
        2.0 * sq_z - sq_x - sq_y,
        dir_x * dir_z,
        sq_x - sq_y,
        dir_y * (3.0 * sq_x - sq_y),
        dir_x * dir_y * dir_z,
        dir_y * (4.0 * sq_z - sq_x - sq_y),
        dir_z * (2.0 * sq_z - 3.0 * sq_x - 3.0 * sq_y),
        dir_x * (4.0 * sq_z - sq_x - sq_y),
        dir_z * (sq_x - sq_y),
        dir_x * (sq_x - 3.0 * sq_y),
    ]
    scaled = [None] + [sh_consts[degree] * sh_basis[degree] for degree in range(1, 16)]
    colours = []
    for channel in range(3):
        colour = 0.5 + 0.28209479177387814 * attr_rows[11 + channel]
        for degree in range(1, 16):
            colour = colour + scaled[degree] * attr_rows[11 + 3 * degree + channel]
        colours.append(colour)
    return [mean_u, mean_v, cov_c * inv_det, -cov_b * inv_det, cov_a * inv_det] + colours


def iota(shape, dim):
    return lax.broadcasted_iota(jnp.int32, shape, dim)


def lane_pick(values, index):
    return jnp.take_along_axis(values, index, axis=1, mode="promise_in_bounds")


def halves(values):
    high = values.astype(jnp.bfloat16)
    low = (values - high.astype(f32)).astype(jnp.bfloat16)
    return high, low


def dot_nt(left, right):
    return lax.dot_general(left, right, (((1,), (1,)), ((), ())), preferred_element_type=f32)


def row_sums(blocks):
    row = iota((8, lanes), 0)
    level = []
    for i in range(4):
        first, second = blocks[i], blocks[i + 4]
        level.append(
            jnp.where(row < 4, first, second)
            + pltpu.roll(jnp.where(row < 4, second, first), 4, 0)
        )
    pairs = []
    for i in range(2):
        first, second = level[i], level[i + 2]
        first = first + pltpu.roll(first, 6, 0)
        second = second + pltpu.roll(second, 2, 0)
        pairs.append(jnp.where((row & 2) == 0, first, second))
    first = pairs[0] + pltpu.roll(pairs[0], 7, 0)
    second = pairs[1] + pltpu.roll(pairs[1], 1, 0)
    return jnp.where((row & 1) == 0, first, second)


def blur_rows(ref, start, count):
    total = window[5] * ref[:, pl.ds(start + 5, count), :]
    for offset in range(5):
        total = total + window[offset] * (
            ref[:, pl.ds(start + offset, count), :]
            + ref[:, pl.ds(start + 10 - offset, count), :]
        )
    return total


def blur_columns(planes, band):
    count, rows, _ = planes.shape
    flat = planes.reshape(count * rows, lanes)
    out = jnp.dot(flat, band, preferred_element_type=f32, precision=lax.Precision.HIGHEST)
    return out.reshape(count, rows, lanes)


def step_kernel(
    attr_ref,
    cam_ref,
    ids_ref,
    order_ref,
    target_ref,
    image_ref,
    grad_ref,
    cam_row,
    cam_all,
    req_out,
    req_in,
    ans_out,
    ans_in,
    back_out,
    back_in,
    view_out,
    view_in,
    ext_x,
    ext_y,
    attr_rows,
    stack,
    wide,
    alpha_s,
    weight_s,
    sums,
    planes_y,
    planes_x,
    partials,
    send_sems,
    recv_sems,
):
    me = lax.axis_index("gauss")
    view = lax.axis_index("cam")

    def peer_at(step):
        return lax.rem(me + step, peers)

    def view_at(step):
        return lax.rem(view + step, views)

    barrier = pltpu.get_barrier_semaphore()

    def greet_peer(step, carry):
        pl.semaphore_signal(barrier, inc=1, device_id={"gauss": peer_at(step)}, device_id_type=MESH)
        return carry

    def greet_view(step, carry):
        pl.semaphore_signal(barrier, inc=1, device_id={"cam": view_at(step)}, device_id_type=MESH)
        return carry

    lax.fori_loop(1, peers, greet_peer, 0)
    lax.fori_loop(1, views, greet_view, 0)

    def remote(src, dst, phase, where):
        return pltpu.make_async_remote_copy(
            src_ref=src,
            dst_ref=dst,
            send_sem=send_sems.at[phase],
            recv_sem=recv_sems.at[phase],
            device_id=where,
            device_id_type=MESH,
        )

    def exchange(out, into, phase, axis):
        count = peers if axis == "gauss" else views
        own = me if axis == "gauss" else view

        def send(step, carry):
            other = lax.rem(own + step, count)
            remote(out.at[other], into.at[own], phase, {axis: other}).start()
            return carry

        lax.fori_loop(1, count, send, 0)
        into[pl.ds(own, 1)] = out[pl.ds(own, 1)]

    def bulk(out, into, phase, axis):
        count = peers if axis == "gauss" else views
        return remote(
            out.at[pl.ds(0, count - 1)],
            into.at[pl.ds(0, count - 1)],
            phase,
            {axis: peer_at(1) if axis == "gauss" else view_at(1)},
        )

    ids = lane_pick(ids_ref[...], order_ref[...])
    present = ids >= 0
    owner = ids >> 10
    local_id = ids & 1023
    chunk_id = (local_id >> 7).astype(f32)
    lane_id = (local_id & 127).astype(f32)
    owner_row = iota((peers, slots), 0)
    before = (iota((slots, slots), 0) < iota((slots, slots), 1)).astype(jnp.bfloat16)
    rank_rows = iota((capacity, slots), 0)
    slot_row = iota((1, slots), 1).astype(f32)
    base = jnp.zeros((peers, 1), f32)
    asked = jnp.zeros((peers, lanes), f32)
    ranks = []
    for tile in range(tiles):
        named = owner_row == owner[tile : tile + 1]
        member = jnp.where(named, 1.0, 0.0)
        earlier = jnp.dot(member.astype(jnp.bfloat16), before, preferred_element_type=f32)
        rank = jnp.sum(member * (earlier + base), axis=0, keepdims=True)
        base = base + jnp.sum(member, axis=1, keepdims=True)
        ranks.append(rank)
        hit = rank_rows == rank.astype(jnp.int32)
        terms = [
            jnp.where(hit, chunk_id[tile : tile + 1], 0.0),
            jnp.where(hit, lane_id[tile : tile + 1], 0.0),
            jnp.where(hit, 1.0, 0.0),
            jnp.where(hit, float(tile), 0.0),
            jnp.where(hit, slot_row, 0.0),
            jnp.zeros((lanes - 5 * capacity, slots), f32),
        ]
        asked = asked + dot_nt(
            member.astype(jnp.bfloat16), jnp.concatenate(terms, axis=0).astype(jnp.bfloat16)
        )
    rank = jnp.concatenate(ranks, axis=0).astype(jnp.int32)
    req_out[...] = asked.reshape(peers, 1, lanes)
    cam_row[...] = jnp.zeros((1, lanes), f32)
    cam_row[:, 0:8] = cam_ref[...]
    cam_all[pl.ds(view, 1)] = cam_row[...].reshape(1, 1, lanes)
    ext_y[:, 16:32, :] = target_ref[0]

    pl.semaphore_wait(barrier, peers + views - 2)

    exchange(req_out, req_in, 0, "gauss")
    below, above = peer_at(1), peer_at(peers - 1)
    target_down = remote(ext_y.at[:, 16:32, :], ext_y.at[:, 0:16, :], 1, {"gauss": below})
    target_up = remote(ext_y.at[:, 16:32, :], ext_y.at[:, 32:48, :], 2, {"gauss": above})
    target_down.start()
    target_up.start()

    def send_camera(step, carry):
        remote(cam_row, cam_all.at[view], 3, {"cam": view_at(step)}).start()
        return carry

    lax.fori_loop(1, views, send_camera, 0)

    for chunk in range(8):
        attr_rows[:, chunk, :] = attr_ref[:, chunk * lanes : (chunk + 1) * lanes]
    camera = [
        jnp.broadcast_to(cam_row[0:1, column : column + 1], (8, lanes)) for column in range(8)
    ]
    rows = [attr_rows[row] for row in range(59)]
    flat_features = project(rows, camera_terms(camera))
    opacity = 1.0 / (1.0 + jnp.exp(-rows[10]))
    table = flat_features[0:5] + [opacity] + flat_features[5:8]

    def by_rank(values):
        return jnp.concatenate([values, pltpu.roll(values, lanes - 8, 1)], axis=0).T

    bulk(req_out, req_in, 0, "gauss").wait_recv()
    wanted = by_rank(req_in[...].reshape(peers, lanes))
    want_chunk = wanted[0:8].astype(jnp.int32)
    want_lane = wanted[16:24].astype(jnp.int32)
    want_there = wanted[32:40]
    at_chunk = [want_chunk == chunk for chunk in range(8)]
    stack[...] = jnp.zeros((lanes, lanes), f32)
    for feature in range(9):
        picked = jnp.zeros((8, lanes), f32)
        for chunk in range(8):
            row = jnp.broadcast_to(table[feature][chunk : chunk + 1], (8, lanes))
            picked = jnp.where(at_chunk[chunk], lane_pick(row, want_lane), picked)
        stack[8 * feature : 8 * feature + 8] = picked
    turned = stack[...].T
    ans_out[:, 0, :] = turned[0:peers]
    ans_out[:, 1, :] = turned[peers:]
    exchange(ans_out, ans_in, 4, "gauss")

    outer = iota((slots, lanes), 0)
    inner = iota((slots, lanes), 1)
    band = jnp.zeros((lanes, lanes), f32)
    for offset in range(11):
        band = jnp.where(inner - outer == offset - 5, window[offset], band)
    target_down.wait_recv()
    target_up.wait_recv()
    ext_y[:, 0:16, :] = ext_y[:, 0:16, :] * jnp.where(me > 0, 1.0, 0.0)
    ext_y[:, 32:48, :] = ext_y[:, 32:48, :] * jnp.where(me < peers - 1, 1.0, 0.0)
    photo = ext_y[...]
    planes_y[0:3] = photo
    planes_y[3:6] = photo * photo
    blurred_y = blur_columns(blur_rows(planes_y, 6, 32), band)
    mean_y = blurred_y[0:3]
    var_y = blurred_y[3:6] - mean_y * mean_y

    sent = by_rank(asked)
    sent_there = sent[32:40]
    sent_tile = sent[48:56].astype(jnp.int32)
    sent_slot = sent[64:72].astype(jnp.int32)

    bulk(ans_out, ans_in, 4, "gauss").wait_recv()
    answers = jnp.concatenate([ans_in[:, 0, :], ans_in[:, 1, :]], axis=0).T
    from_lane = jnp.where(present, (rank >> 3) * peers + owner, 0)
    from_row = jnp.where(present, rank & 7, 8)
    at_row = [from_row == row for row in range(8)]
    features = []
    stack[72:128] = jnp.zeros((56, lanes), f32)
    for feature in range(9):
        picked = jnp.zeros((8, lanes), f32)
        for row in range(8):
            source = jnp.broadcast_to(
                answers[8 * feature + row : 8 * feature + row + 1], (8, lanes)
            )
            picked = jnp.where(at_row[row], lane_pick(source, from_lane), picked)
        stack[8 * feature : 8 * feature + 8] = picked
        features.append(picked)
    by_slot = stack[...].T
    spread = [lane_pick(by_slot, 8 * feature + (inner >> 4)) for feature in range(9)]
    slot_u, slot_v, conic_a, conic_b, conic_c, slot_opacity = spread[0:6]
    off_u = inner.astype(f32) + 0.5 - slot_u
    wide[0] = -0.5 * conic_a * off_u * off_u
    wide[1] = -conic_b * off_u
    wide[2] = -0.5 * conic_c
    wide[3] = slot_v
    wide[4] = slot_opacity
    wide[5] = spread[6]
    wide[6] = spread[7]
    wide[7] = spread[8]
    pixel_row = (iota((tile_side, lanes), 0) + me * tile_side).astype(f32) + 0.5

    def render(group, carry):
        transmit, red, green, blue = carry
        first = pl.multiple_of(group * 8, 8)
        block = [wide[item, pl.ds(first, 8), :] for item in range(8)]
        for i in range(8):
            flat, slope, curve, mean_v, alpha_top, c_0, c_1, c_2 = [
                item[i : i + 1] for item in block
            ]
            off_v = pixel_row - mean_v
            alpha = alpha_top * jnp.exp(flat + off_v * (slope + curve * off_v))
            weight = alpha * transmit
            transmit = transmit - weight
            red = red + weight * c_0
            green = green + weight * c_1
            blue = blue + weight * c_2
            alpha_s[first + i] = alpha
            weight_s[first + i] = weight
        return transmit, red, green, blue

    zero = jnp.zeros((tile_side, lanes), f32)
    _, red, green, blue = lax.fori_loop(0, slots // 8, render, (zero + 1.0, zero, zero, zero))
    image = jnp.stack([red, green, blue])
    ext_x[:, 16:32, :] = image
    image_down = remote(ext_x.at[:, 16:32, :], ext_x.at[:, 0:16, :], 5, {"gauss": below})
    image_up = remote(ext_x.at[:, 16:32, :], ext_x.at[:, 32:48, :], 6, {"gauss": above})
    image_down.start()
    image_up.start()
    image_ref[0] = image
    image_down.wait_recv()
    image_up.wait_recv()
    ext_x[:, 0:16, :] = ext_x[:, 0:16, :] * jnp.where(me > 0, 1.0, 0.0)
    ext_x[:, 32:48, :] = ext_x[:, 32:48, :] * jnp.where(me < peers - 1, 1.0, 0.0)

    shown = ext_x[...]
    planes_x[0:3] = shown
    planes_x[3:6] = shown * shown
    planes_x[6:9] = shown * photo
    blurred_x = blur_columns(blur_rows(planes_x, 6, 32), band)
    mean_x = blurred_x[0:3]
    var_x = blurred_x[3:6] - mean_x * mean_x
    cov_xy = blurred_x[6:9] - mean_x * mean_y
    top_1 = 2.0 * mean_x * mean_y + 0.0001
    top_2 = 2.0 * cov_xy + 0.0009
    inv_1 = 1.0 / (mean_x * mean_x + mean_y * mean_y + 0.0001)
    inv_2 = 1.0 / (var_x + var_y + 0.0009)
    inv_both = inv_1 * inv_2
    ssim = top_1 * top_2 * inv_both
    map_row = iota((3, 32, lanes), 1) + (me * tile_side - 5)
    in_view = (map_row >= 0) & (map_row < peers * tile_side)
    share = jnp.where(in_view, -0.2 / 256.0, 0.0)
    d_cov = share * 2.0 * top_1 * inv_both
    d_var = -share * ssim * inv_2
    d_mean = (
        share * (2.0 * mean_y * top_2 * inv_both - 2.0 * mean_x * ssim * inv_1)
        - 2.0 * mean_x * d_var
        - mean_y * d_cov
    )
    partials[0:3] = d_mean
    partials[3:6] = d_var
    partials[6:9] = d_cov
    pulled = blur_columns(blur_rows(partials, 0, 16), band)
    own_photo = target_ref[0]
    gap = image - own_photo
    loss_grad = (
        pulled[0:3]
        + 2.0 * image * pulled[3:6]
        + own_photo * pulled[6:9]
        + (0.8 / 256.0) * gap / jnp.sqrt(gap * gap + 0.0025)
    )
    grad_0, grad_1, grad_2 = loss_grad[0], loss_grad[1], loss_grad[2]

    def render_back(step, behind):
        first = pl.multiple_of((slots // 8 - 1 - step) * 8, 8)
        block = [wide[item, pl.ds(first, 8), :] for item in (3, 5, 6, 7)]
        kept = [[None] * 8 for _ in range(6)]
        for i in reversed(range(8)):
            mean_v, c_0, c_1, c_2 = [item[i : i + 1] for item in block]
            alpha = alpha_s[first + i]
            weight = weight_s[first + i]
            lead = grad_0 * c_0 + grad_1 * c_1 + grad_2 * c_2 - behind
            behind = behind + alpha * lead
            moment_0 = weight * lead
            off_v = pixel_row - mean_v
            moment_1 = moment_0 * off_v
            moment_2 = moment_1 * off_v
            per_slot = (
                moment_0, moment_1, moment_2, weight * grad_0, weight * grad_1, weight * grad_2
            )
            for item in range(6):
                kept[item][i] = per_slot[item][0:8] + per_slot[item][8:16]
        for item in range(6):
            sums[item, pl.ds(first, 8), :] = row_sums(kept[item])
        return behind

    lax.fori_loop(0, slots // 8, render_back, zero)

    sum_0, sum_1, sum_2 = sums[0], sums[1], sums[2]
    sum_0u = sum_0 * off_u
    quantities = [
        sum_0, sum_0u, sum_0u * off_u, sum_1, sum_1 * off_u, sum_2, sums[3], sums[4], sums[5]
    ]
    gathered = jnp.zeros((slots, lanes), f32)
    for item in range(9):
        chooser = (inner == 8 * item + (outer >> 4)).astype(jnp.bfloat16)
        for part in halves(quantities[item]):
            gathered = gathered + jnp.dot(part, chooser, preferred_element_type=f32)
    per_tile = gathered.T
    m_0, m_u, m_uu, m_v, m_uv, m_vv = [per_tile[8 * item : 8 * item + 8] for item in range(6)]
    slot_grads = [
        features[2] * m_u + features[3] * m_v,
        features[4] * m_v + features[3] * m_u,
        -0.5 * m_uu,
        -m_uv,
        -0.5 * m_vv,
        m_0,
        per_tile[48:56],
        per_tile[56:64],
        per_tile[64:72],
    ]

    at_tile = [(sent_tile == tile) & (sent_there > 0.5) for tile in range(tiles)]
    for feature in range(9):
        picked = jnp.zeros((8, lanes), f32)
        for tile in range(tiles):
            row = jnp.broadcast_to(slot_grads[feature][tile : tile + 1], (8, lanes))
            picked = jnp.where(at_tile[tile], lane_pick(row, sent_slot), picked)
        for row in range(8):
            stack[16 * row + feature : 16 * row + feature + 1] = picked[row : row + 1]
    for row in range(8):
        stack[16 * row + 9 : 16 * row + 16] = jnp.zeros((7, lanes), f32)
    turned = stack[...].T
    back_out[:, 0, :] = turned[0:peers]
    back_out[:, 1, :] = turned[peers:]
    exchange(back_out, back_in, 7, "gauss")

    bulk(back_out, back_in, 7, "gauss").wait_recv()
    returned = jnp.concatenate([back_in[:, 0, :], back_in[:, 1, :]], axis=0).T
    block_grad = jnp.zeros((views * 16, lanes), f32)
    for row in range(8):
        mine = returned[16 * row : 16 * row + 16]
        mine = jnp.where(want_there[row : row + 1] > 0.5, mine, 0.0)
        left = jnp.concatenate(
            [jnp.where(want_chunk[row : row + 1] == chunk, mine, 0.0) for chunk in range(8)], axis=0
        )
        right = (outer == want_lane[row : row + 1]).astype(jnp.bfloat16)
        for part in halves(left):
            block_grad = block_grad + dot_nt(part, right)
    view_out[...] = block_grad.reshape(views, 16, lanes)
    exchange(view_out, view_in, 8, "cam")

    bulk(cam_all, cam_all, 3, "cam").wait_recv()
    every = cam_all[...].reshape(views, lanes)
    cameras = camera_terms(
        [jnp.broadcast_to(every[:, column : column + 1], (views, lanes)) for column in range(8)]
    )
    own = attr_ref[:, pl.ds(pl.multiple_of(view * lanes, lanes), lanes)]
    own_rows = [own[row : row + 1] for row in range(59)]
    wide_rows = [jnp.broadcast_to(row, (views, lanes)) for row in own_rows]
    _, pull = jax.vjp(lambda values: project(values, cameras), wide_rows)
    bulk(view_out, view_in, 8, "cam").wait_recv()
    cots = [view_in[:, item, :] for item in range(9)]
    (row_grads,) = pull(cots[0:5] + cots[6:9])
    own_opacity = 1.0 / (1.0 + jnp.exp(-wide_rows[10]))
    row_grads[10] = cots[5] * (1.0 - own_opacity)
    for row in range(59):
        grad_ref[row : row + 1, :] = jnp.sum(row_grads[row], axis=0, keepdims=True)

    bulk(req_out, req_in, 0, "gauss").wait_send()
    bulk(ans_out, ans_in, 4, "gauss").wait_send()
    bulk(back_out, back_in, 7, "gauss").wait_send()
    bulk(view_out, view_in, 8, "cam").wait_send()
    bulk(cam_all, cam_all, 3, "cam").wait_send()
    target_down.wait_send()
    target_up.wait_send()
    image_down.wait_send()
    image_up.wait_send()


def local(attributes, cameras, tile_ids, depth_order, target):
    vmem = pl.BlockSpec(memory_space=pltpu.VMEM)
    scratch = [
        (1, lanes),
        (views, 1, lanes),
        (peers, 1, lanes),
        (peers, 1, lanes),
        (peers, 2, lanes),
        (peers, 2, lanes),
        (peers, 2, lanes),
        (peers, 2, lanes),
        (views, 16, lanes),
        (views, 16, lanes),
        (3, 48, lanes),
        (3, 48, lanes),
        (59, 8, lanes),
        (lanes, lanes),
        (8, slots, lanes),
        (slots, tile_side, lanes),
        (slots, tile_side, lanes),
        (6, slots, lanes),
        (6, 48, lanes),
        (9, 48, lanes),
        (9, 32, lanes),
    ]
    return pl.pallas_call(
        step_kernel,
        out_shape=(
            jax.ShapeDtypeStruct((1, 3, tile_side, lanes), f32),
            jax.ShapeDtypeStruct((59, lanes), f32),
        ),
        in_specs=[vmem] * 5,
        out_specs=(vmem, vmem),
        scratch_shapes=[pltpu.VMEM(shape, f32) for shape in scratch]
        + [pltpu.SemaphoreType.DMA((9,)), pltpu.SemaphoreType.DMA((9,))],
        compiler_params=pltpu.CompilerParams(
            collective_id=0, has_side_effects=True, vmem_limit_bytes=40 * 1024 * 1024
        ),
    )(attributes, cameras, tile_ids.reshape(tiles, slots), depth_order.reshape(tiles, slots), target)


def solution(mesh):
    return jax.shard_map(
        local,
        mesh=mesh,
        in_specs=(
            P(None, "gauss"),
            P("cam", None),
            P("cam", "gauss", None, None),
            P("cam", "gauss", None, None),
            P("cam", None, "gauss", None),
        ),
        out_specs=(P("cam", None, "gauss", None), P(None, ("gauss", "cam"))),
        check_vma=False,
    )
```

```python
import math

import jax
import jax.numpy as jnp
from jax import lax
from jax.experimental import pallas as pl
from jax.experimental.pallas import tpu as pltpu
from jax.sharding import PartitionSpec as P

MESH = pl.DeviceIdType.MESH
peers = 64
views = 8
tile_side = 16
tiles = 8
slots = 128
lanes = 128
capacity = 16
image_width = 128.0
image_height = 1024.0
f32 = jnp.float32
window_raw = [math.exp(-((offset - 5) ** 2) / 4.5) for offset in range(11)]
window = [weight / sum(window_raw) for weight in window_raw]
sh_consts = [
    0.0,
    -0.4886025119029199,
    0.4886025119029199,
    -0.4886025119029199,
    1.0925484305920792,
    -1.0925484305920792,
    0.31539156525252005,
    -1.0925484305920792,
    0.5462742152960396,
    -0.5900435899266435,
    2.890611442640554,
    -0.4570457994644658,
    0.3731763325901154,
    -0.4570457994644658,
    1.445305721320277,
    -0.5900435899266435,
]


def unit_quat(parts):
    length_q = jnp.sqrt(
        parts[0] * parts[0] + parts[1] * parts[1] + parts[2] * parts[2] + parts[3] * parts[3]
    )
    return [part / length_q for part in parts]


def quat_matrix(quaternion):
    q_w, q_x, q_y, q_z = quaternion
    return [
        [
            1.0 - 2.0 * (q_y * q_y + q_z * q_z),
            2.0 * (q_x * q_y - q_w * q_z),
            2.0 * (q_x * q_z + q_w * q_y),
        ],
        [
            2.0 * (q_x * q_y + q_w * q_z),
            1.0 - 2.0 * (q_x * q_x + q_z * q_z),
            2.0 * (q_y * q_z - q_w * q_x),
        ],
        [
            2.0 * (q_x * q_z - q_w * q_y),
            2.0 * (q_y * q_z + q_w * q_x),
            1.0 - 2.0 * (q_x * q_x + q_y * q_y),
        ],
    ]


def camera_terms(camera):
    cam_rot = quat_matrix(unit_quat(camera[0:4]))
    shift_vec = camera[4:7]
    centre = [
        -(
            cam_rot[0][axis_col] * shift_vec[0]
            + cam_rot[1][axis_col] * shift_vec[1]
            + cam_rot[2][axis_col] * shift_vec[2]
        )
        for axis_col in range(3)
    ]
    return cam_rot, shift_vec, camera[7] * image_width, camera[7] * image_height, centre


def project(attr_rows, camera):
    cam_rot, shift_vec, horizontal_focal, focal_y, centre = camera
    position = [attr_rows[0], attr_rows[1], attr_rows[2]]
    view_pos = [
        cam_rot[axis_row][0] * position[0]
        + cam_rot[axis_row][1] * position[1]
        + cam_rot[axis_row][2] * position[2]
        + shift_vec[axis_row]
        for axis_row in range(3)
    ]
    inv_z = 1.0 / view_pos[2]
    focal_u = horizontal_focal * inv_z
    focal_v = focal_y * inv_z
    slope_u = focal_u * view_pos[0]
    slope_v = focal_v * view_pos[1]
    mean_u = 0.5 * image_width + slope_u
    mean_v = 0.5 * image_height + slope_v
    gauss_rot = quat_matrix(unit_quat([attr_rows[6], attr_rows[7], attr_rows[8], attr_rows[9]]))
    scales = [jnp.exp(attr_rows[3]), jnp.exp(attr_rows[4]), jnp.exp(attr_rows[5])]
    skew_u = slope_u * inv_z
    skew_v = slope_v * inv_z
    project_mat = [
        [focal_u * cam_rot[0][axis_col] - skew_u * cam_rot[2][axis_col] for axis_col in range(3)],
        [focal_v * cam_rot[1][axis_col] - skew_v * cam_rot[2][axis_col] for axis_col in range(3)],
    ]
    spread = [
        [
            (
                project_mat[axis_row][0] * gauss_rot[0][axis_col]
                + project_mat[axis_row][1] * gauss_rot[1][axis_col]
                + project_mat[axis_row][2] * gauss_rot[2][axis_col]
            )
            * scales[axis_col]
            for axis_col in range(3)
        ]
        for axis_row in range(2)
    ]
    cov_a = spread[0][0] * spread[0][0] + spread[0][1] * spread[0][1] + spread[0][2] * spread[0][2] + 0.3
    cov_b = spread[0][0] * spread[1][0] + spread[0][1] * spread[1][1] + spread[0][2] * spread[1][2]
    cov_c = spread[1][0] * spread[1][0] + spread[1][1] * spread[1][1] + spread[1][2] * spread[1][2] + 0.3
    inv_det = 1.0 / (cov_a * cov_c - cov_b * cov_b)
    offsets = [position[axis_col] - centre[axis_col] for axis_col in range(3)]
    distance = jnp.sqrt(offsets[0] * offsets[0] + offsets[1] * offsets[1] + offsets[2] * offsets[2])
    inv_distance = 1.0 / distance
    dir_x, dir_y, dir_z = [offset * inv_distance for offset in offsets]
    sq_x, sq_y, sq_z = (dir_x * dir_x, dir_y * dir_y, dir_z * dir_z)
    sh_basis = [
        None,
        dir_y,
        dir_z,
        dir_x,
        dir_x * dir_y,
        dir_y * dir_z,
        2.0 * sq_z - sq_x - sq_y,
        dir_x * dir_z,
        sq_x - sq_y,
        dir_y * (3.0 * sq_x - sq_y),
        dir_x * dir_y * dir_z,
        dir_y * (4.0 * sq_z - sq_x - sq_y),
        dir_z * (2.0 * sq_z - 3.0 * sq_x - 3.0 * sq_y),
        dir_x * (4.0 * sq_z - sq_x - sq_y),
        dir_z * (sq_x - sq_y),
        dir_x * (sq_x - 3.0 * sq_y),
    ]
    scaled = [None] + [sh_consts[degree] * sh_basis[degree] for degree in range(1, 16)]
    colours = []
    for channel in range(3):
        colour = 0.5 + 0.28209479177387814 * attr_rows[11 + channel]
        for degree in range(1, 16):
            colour = colour + scaled[degree] * attr_rows[11 + 3 * degree + channel]
        colours.append(colour)
    return [mean_u, mean_v, cov_c * inv_det, -cov_b * inv_det, cov_a * inv_det] + colours


def iota(shape, dim):
    return lax.broadcasted_iota(jnp.int32, shape, dim)


def lane_pick(values, index):
    return jnp.take_along_axis(values, index, axis=1, mode="promise_in_bounds")


def halves(values):
    high = values.astype(jnp.bfloat16)
    low = (values - high.astype(f32)).astype(jnp.bfloat16)
    return high, low


def dot_nt(left, right):
    return lax.dot_general(left, right, (((1,), (1,)), ((), ())), preferred_element_type=f32)


def row_sums(blocks):
    row = iota((8, lanes), 0)
    level = []
    for i in range(4):
        first, second = blocks[i], blocks[i + 4]
        level.append(
            jnp.where(row < 4, first, second)
            + pltpu.roll(jnp.where(row < 4, second, first), 4, 0)
        )
    pairs = []
    for i in range(2):
        first, second = level[i], level[i + 2]
        first = first + pltpu.roll(first, 6, 0)
        second = second + pltpu.roll(second, 2, 0)
        pairs.append(jnp.where((row & 2) == 0, first, second))
    first = pairs[0] + pltpu.roll(pairs[0], 7, 0)
    second = pairs[1] + pltpu.roll(pairs[1], 1, 0)
    return jnp.where((row & 1) == 0, first, second)


def blur_rows(ref, start, count):
    total = window[5] * ref[:, pl.ds(start + 5, count), :]
    for offset in range(5):
        total = total + window[offset] * (
            ref[:, pl.ds(start + offset, count), :]
            + ref[:, pl.ds(start + 10 - offset, count), :]
        )
    return total


def blur_columns(planes, band):
    count, rows, _ = planes.shape
    flat = planes.reshape(count * rows, lanes)
    out = jnp.dot(flat, band, preferred_element_type=f32, precision=lax.Precision.HIGHEST)
    return out.reshape(count, rows, lanes)


def step_kernel(
    attr_hbm,
    cam_hbm,
    ids_hbm,
    order_hbm,
    target_hbm,
    image_ref,
    grad_ref,
    attr_ref,
    cam_ref,
    ids_ref,
    order_ref,
    target_ref,
    cam_row,
    cam_all,
    req_out,
    req_in,
    ans_out,
    ans_in,
    back_out,
    back_in,
    view_out,
    view_in,
    ext_x,
    ext_y,
    attr_rows,
    table_rows,
    stack,
    wide,
    alpha_s,
    weight_s,
    sums,
    planes_y,
    planes_x,
    partials,
    load_sems,
    send_sems,
    recv_sems,
):
    me = lax.axis_index("gauss")
    view = lax.axis_index("cam")
    loads = [
        pltpu.make_async_copy(source, into, load_sems.at[item])
        for item, (source, into) in enumerate(
            (
                (ids_hbm, ids_ref),
                (order_hbm, order_ref),
                (target_hbm, target_ref),
                (cam_hbm, cam_ref),
                (attr_hbm, attr_ref),
            )
        )
    ]
    for load in loads:
        load.start()

    my_z = lax.div(me, 8)
    my_y = lax.rem(me, 8)
    my_x = lax.div(view, 2)
    my_core = lax.rem(view, 2)
    along_y = [lax.rem(my_y + step, 8) for step in (4, 3, 5, 2, 6, 1, 7)]
    along_x = [lax.rem(my_x + step, 4) * 2 for step in (2, 1, 3)]

    def each_peer(visit):
        def ring(step, carry):
            from_z = 4 + (1 - 2 * lax.rem(step, 2)) * lax.div(step + 1, 2)
            first = lax.rem(my_z + from_z, 8) * 8
            for place in along_y:
                visit(first + place)
            visit(first + my_y)
            return carry

        lax.fori_loop(0, 7, ring, 0)
        for place in along_y:
            visit(my_z * 8 + place)

    def each_view(visit):
        for place in along_x:
            visit(place + my_core)
            visit(place + 1 - my_core)
        visit(my_x * 2 + 1 - my_core)

    below = lax.rem(me + 1, peers)
    above = lax.rem(me + peers - 1, peers)
    next_view = lax.rem(view + 1, views)

    barrier = pltpu.get_barrier_semaphore()

    def greet_peer(other):
        pl.semaphore_signal(barrier, inc=1, device_id={"gauss": other}, device_id_type=MESH)

    def greet_view(other):
        pl.semaphore_signal(barrier, inc=1, device_id={"cam": other}, device_id_type=MESH)

    each_peer(greet_peer)
    each_view(greet_view)

    def remote(src, dst, phase, where):
        return pltpu.make_async_remote_copy(
            src_ref=src,
            dst_ref=dst,
            send_sem=send_sems.at[phase],
            recv_sem=recv_sems.at[phase],
            device_id=where,
            device_id_type=MESH,
        )

    def exchange(out, into, phase, axis):
        own = me if axis == "gauss" else view

        def send(other):
            remote(out.at[other], into.at[own], phase, {axis: other}).start()

        if axis == "gauss":
            each_peer(send)
        else:
            each_view(send)
        into[pl.ds(own, 1)] = out[pl.ds(own, 1)]

    def bulk(out, into, phase, axis):
        count = peers if axis == "gauss" else views
        return remote(
            out.at[pl.ds(0, count - 1)],
            into.at[pl.ds(0, count - 1)],
            phase,
            {axis: below if axis == "gauss" else next_view},
        )

    loads[0].wait()
    loads[1].wait()
    ids = lane_pick(ids_ref[...], order_ref[...])
    present = ids >= 0
    owner = ids >> 10
    local_id = ids & 1023
    chunk_id = (local_id >> 7).astype(f32)
    lane_id = (local_id & 127).astype(f32)
    owner_row = iota((peers, slots), 0)
    before = (iota((slots, slots), 0) < iota((slots, slots), 1)).astype(jnp.bfloat16)
    rank_rows = iota((capacity, slots), 0)
    slot_row = iota((1, slots), 1).astype(f32)
    base = jnp.zeros((peers, 1), f32)
    asked = jnp.zeros((peers, lanes), f32)
    ranks = []
    for tile in range(tiles):
        named = owner_row == owner[tile : tile + 1]
        member = jnp.where(named, 1.0, 0.0)
        earlier = jnp.dot(member.astype(jnp.bfloat16), before, preferred_element_type=f32)
        rank = jnp.sum(member * (earlier + base), axis=0, keepdims=True)
        base = base + jnp.sum(member, axis=1, keepdims=True)
        ranks.append(rank)
        hit = rank_rows == rank.astype(jnp.int32)
        terms = [
            jnp.where(hit, chunk_id[tile : tile + 1], 0.0),
            jnp.where(hit, lane_id[tile : tile + 1], 0.0),
            jnp.where(hit, 1.0, 0.0),
            jnp.where(hit, float(tile), 0.0),
            jnp.where(hit, slot_row, 0.0),
            jnp.zeros((lanes - 5 * capacity, slots), f32),
        ]
        asked = asked + dot_nt(
            member.astype(jnp.bfloat16), jnp.concatenate(terms, axis=0).astype(jnp.bfloat16)
        )
    rank = jnp.concatenate(ranks, axis=0).astype(jnp.int32)
    req_out[...] = asked.reshape(peers, 1, lanes)
    loads[2].wait()
    loads[3].wait()
    cam_row[...] = jnp.zeros((1, lanes), f32)
    cam_row[:, 0:8] = cam_ref[...]
    cam_all[pl.ds(view, 1)] = cam_row[...].reshape(1, 1, lanes)
    ext_y[:, 16:32, :] = target_ref[0]

    pl.semaphore_wait(barrier, peers + views - 2)

    exchange(req_out, req_in, 0, "gauss")
    target_down = remote(ext_y.at[:, 16:32, :], ext_y.at[:, 0:16, :], 1, {"gauss": below})
    target_up = remote(ext_y.at[:, 16:32, :], ext_y.at[:, 32:48, :], 2, {"gauss": above})
    target_down.start()
    target_up.start()

    each_view(lambda other: remote(cam_row, cam_all.at[view], 3, {"cam": other}).start())

    loads[4].wait()
    for chunk in range(8):
        attr_rows[:, chunk, :] = attr_ref[:, chunk * lanes : (chunk + 1) * lanes]
    camera = [
        jnp.broadcast_to(cam_row[0:1, column : column + 1], (8, lanes)) for column in range(8)
    ]
    rows = [attr_rows[row] for row in range(59)]
    flat_features = project(rows, camera_terms(camera))
    opacity = 1.0 / (1.0 + jnp.exp(-rows[10]))
    table = flat_features[0:5] + [opacity] + flat_features[5:8]
    for feature in range(9):
        for chunk in range(8):
            table_rows[feature, chunk] = jnp.broadcast_to(
                table[feature][chunk : chunk + 1], (8, lanes)
            )

    def by_rank(values):
        return jnp.concatenate([values, pltpu.roll(values, lanes - 8, 1)], axis=0).T

    bulk(req_out, req_in, 0, "gauss").wait_recv()
    wanted = by_rank(req_in[...].reshape(peers, lanes))
    want_chunk = wanted[0:8].astype(jnp.int32)
    want_lane = wanted[16:24].astype(jnp.int32)
    want_there = wanted[32:40]
    at_chunk = [want_chunk == chunk for chunk in range(8)]
    stack[...] = jnp.zeros((lanes, lanes), f32)
    for feature in range(9):
        picked = jnp.zeros((8, lanes), f32)
        for chunk in range(8):
            row = table_rows[feature, chunk]
            picked = jnp.where(at_chunk[chunk], lane_pick(row, want_lane), picked)
        stack[8 * feature : 8 * feature + 8] = picked
    turned = stack[...].T
    ans_out[:, 0, :] = turned[0:peers]
    ans_out[:, 1, :] = turned[peers:]
    exchange(ans_out, ans_in, 4, "gauss")

    outer = iota((slots, lanes), 0)
    inner = iota((slots, lanes), 1)
    band = jnp.zeros((lanes, lanes), f32)
    for offset in range(11):
        band = jnp.where(inner - outer == offset - 5, window[offset], band)
    target_down.wait_recv()
    target_up.wait_recv()
    ext_y[:, 0:16, :] = ext_y[:, 0:16, :] * jnp.where(me > 0, 1.0, 0.0)
    ext_y[:, 32:48, :] = ext_y[:, 32:48, :] * jnp.where(me < peers - 1, 1.0, 0.0)
    photo = ext_y[...]
    planes_y[0:3] = photo
    planes_y[3:6] = photo * photo
    blurred_y = blur_columns(blur_rows(planes_y, 6, 32), band)
    mean_y = blurred_y[0:3]
    var_y = blurred_y[3:6] - mean_y * mean_y

    sent = by_rank(asked)
    sent_there = sent[32:40]
    sent_tile = sent[48:56].astype(jnp.int32)
    sent_slot = sent[64:72].astype(jnp.int32)

    bulk(ans_out, ans_in, 4, "gauss").wait_recv()
    answers = jnp.concatenate([ans_in[:, 0, :], ans_in[:, 1, :]], axis=0).T
    from_lane = jnp.where(present, (rank >> 3) * peers + owner, 0)
    from_row = jnp.where(present, rank & 7, 8)
    at_row = [from_row == row for row in range(8)]
    features = []
    stack[72:128] = jnp.zeros((56, lanes), f32)
    for feature in range(9):
        picked = jnp.zeros((8, lanes), f32)
        for row in range(8):
            source = jnp.broadcast_to(
                answers[8 * feature + row : 8 * feature + row + 1], (8, lanes)
            )
            picked = jnp.where(at_row[row], lane_pick(source, from_lane), picked)
        stack[8 * feature : 8 * feature + 8] = picked
        features.append(picked)
    by_slot = stack[...].T
    spread = [lane_pick(by_slot, 8 * feature + (inner >> 4)) for feature in range(9)]
    slot_u, slot_v, conic_a, conic_b, conic_c, slot_opacity = spread[0:6]
    off_u = inner.astype(f32) + 0.5 - slot_u
    wide[0] = -0.5 * conic_a * off_u * off_u
    wide[1] = -conic_b * off_u
    wide[2] = -0.5 * conic_c
    wide[3] = slot_v
    wide[4] = slot_opacity
    wide[5] = spread[6]
    wide[6] = spread[7]
    wide[7] = spread[8]
    pixel_row = (iota((tile_side, lanes), 0) + me * tile_side).astype(f32) + 0.5

    def render(group, carry):
        transmit, red, green, blue = carry
        first = pl.multiple_of(group * 8, 8)
        block = [wide[item, pl.ds(first, 8), :] for item in range(8)]
        for i in range(8):
            flat, slope, curve, mean_v, alpha_top, c_0, c_1, c_2 = [
                item[i : i + 1] for item in block
            ]
            off_v = pixel_row - mean_v
            alpha = alpha_top * jnp.exp(flat + off_v * (slope + curve * off_v))
            weight = alpha * transmit
            transmit = transmit - weight
            red = red + weight * c_0
            green = green + weight * c_1
            blue = blue + weight * c_2
            alpha_s[first + i] = alpha
            weight_s[first + i] = weight
        return transmit, red, green, blue

    zero = jnp.zeros((tile_side, lanes), f32)
    _, red, green, blue = lax.fori_loop(0, slots // 8, render, (zero + 1.0, zero, zero, zero))
    image = jnp.stack([red, green, blue])
    ext_x[:, 16:32, :] = image
    image_down = remote(ext_x.at[:, 16:32, :], ext_x.at[:, 0:16, :], 5, {"gauss": below})
    image_up = remote(ext_x.at[:, 16:32, :], ext_x.at[:, 32:48, :], 6, {"gauss": above})
    image_down.start()
    image_up.start()
    image_ref[0] = image
    image_down.wait_recv()
    image_up.wait_recv()
    ext_x[:, 0:16, :] = ext_x[:, 0:16, :] * jnp.where(me > 0, 1.0, 0.0)
    ext_x[:, 32:48, :] = ext_x[:, 32:48, :] * jnp.where(me < peers - 1, 1.0, 0.0)

    shown = ext_x[...]
    planes_x[0:3] = shown
    planes_x[3:6] = shown * shown
    planes_x[6:9] = shown * photo
    blurred_x = blur_columns(blur_rows(planes_x, 6, 32), band)
    mean_x = blurred_x[0:3]
    var_x = blurred_x[3:6] - mean_x * mean_x
    cov_xy = blurred_x[6:9] - mean_x * mean_y
    top_1 = 2.0 * mean_x * mean_y + 0.0001
    top_2 = 2.0 * cov_xy + 0.0009
    inv_1 = 1.0 / (mean_x * mean_x + mean_y * mean_y + 0.0001)
    inv_2 = 1.0 / (var_x + var_y + 0.0009)
    inv_both = inv_1 * inv_2
    ssim = top_1 * top_2 * inv_both
    map_row = iota((3, 32, lanes), 1) + (me * tile_side - 5)
    in_view = (map_row >= 0) & (map_row < peers * tile_side)
    share = jnp.where(in_view, -0.2 / 256.0, 0.0)
    d_cov = share * 2.0 * top_1 * inv_both
    d_var = -share * ssim * inv_2
    d_mean = (
        share * (2.0 * mean_y * top_2 * inv_both - 2.0 * mean_x * ssim * inv_1)
        - 2.0 * mean_x * d_var
        - mean_y * d_cov
    )
    partials[0:3] = d_mean
    partials[3:6] = d_var
    partials[6:9] = d_cov
    pulled = blur_columns(blur_rows(partials, 0, 16), band)
    own_photo = target_ref[0]
    gap = image - own_photo
    loss_grad = (
        pulled[0:3]
        + 2.0 * image * pulled[3:6]
        + own_photo * pulled[6:9]
        + (0.8 / 256.0) * gap / jnp.sqrt(gap * gap + 0.0025)
    )
    grad_0, grad_1, grad_2 = loss_grad[0], loss_grad[1], loss_grad[2]

    def render_back(step, behind):
        first = pl.multiple_of((slots // 8 - 1 - step) * 8, 8)
        block = [wide[item, pl.ds(first, 8), :] for item in (3, 5, 6, 7)]
        kept = [[None] * 8 for _ in range(6)]
        for i in reversed(range(8)):
            mean_v, c_0, c_1, c_2 = [item[i : i + 1] for item in block]
            alpha = alpha_s[first + i]
            weight = weight_s[first + i]
            lead = grad_0 * c_0 + grad_1 * c_1 + grad_2 * c_2 - behind
            behind = behind + alpha * lead
            moment_0 = weight * lead
            off_v = pixel_row - mean_v
            moment_1 = moment_0 * off_v
            moment_2 = moment_1 * off_v
            per_slot = (
                moment_0, moment_1, moment_2, weight * grad_0, weight * grad_1, weight * grad_2
            )
            for item in range(6):
                kept[item][i] = per_slot[item][0:8] + per_slot[item][8:16]
        for item in range(6):
            sums[item, pl.ds(first, 8), :] = row_sums(kept[item])
        return behind

    lax.fori_loop(0, slots // 8, render_back, zero)

    sum_0, sum_1, sum_2 = sums[0], sums[1], sums[2]
    sum_0u = sum_0 * off_u
    quantities = [
        sum_0, sum_0u, sum_0u * off_u, sum_1, sum_1 * off_u, sum_2, sums[3], sums[4], sums[5]
    ]
    gathered = jnp.zeros((slots, lanes), f32)
    for item in range(9):
        chooser = (inner == 8 * item + (outer >> 4)).astype(jnp.bfloat16)
        for part in halves(quantities[item]):
            gathered = gathered + jnp.dot(part, chooser, preferred_element_type=f32)
    per_tile = gathered.T
    m_0, m_u, m_uu, m_v, m_uv, m_vv = [per_tile[8 * item : 8 * item + 8] for item in range(6)]
    slot_grads = [
        features[2] * m_u + features[3] * m_v,
        features[4] * m_v + features[3] * m_u,
        -0.5 * m_uu,
        -m_uv,
        -0.5 * m_vv,
        m_0,
        per_tile[48:56],
        per_tile[56:64],
        per_tile[64:72],
    ]

    at_tile = [(sent_tile == tile) & (sent_there > 0.5) for tile in range(tiles)]
    for feature in range(9):
        picked = jnp.zeros((8, lanes), f32)
        for tile in range(tiles):
            row = jnp.broadcast_to(slot_grads[feature][tile : tile + 1], (8, lanes))
            picked = jnp.where(at_tile[tile], lane_pick(row, sent_slot), picked)
        for row in range(8):
            stack[16 * row + feature : 16 * row + feature + 1] = picked[row : row + 1]
    for row in range(8):
        stack[16 * row + 9 : 16 * row + 16] = jnp.zeros((7, lanes), f32)
    turned = stack[...].T
    back_out[:, 0, :] = turned[0:peers]
    back_out[:, 1, :] = turned[peers:]
    exchange(back_out, back_in, 7, "gauss")

    bulk(back_out, back_in, 7, "gauss").wait_recv()
    returned = jnp.concatenate([back_in[:, 0, :], back_in[:, 1, :]], axis=0).T
    block_grad = jnp.zeros((views * 16, lanes), f32)
    for row in range(8):
        mine = returned[16 * row : 16 * row + 16]
        mine = jnp.where(want_there[row : row + 1] > 0.5, mine, 0.0)
        left = jnp.concatenate(
            [jnp.where(want_chunk[row : row + 1] == chunk, mine, 0.0) for chunk in range(8)], axis=0
        )
        right = (outer == want_lane[row : row + 1]).astype(jnp.bfloat16)
        for part in halves(left):
            block_grad = block_grad + dot_nt(part, right)
    view_out[...] = block_grad.reshape(views, 16, lanes)
    exchange(view_out, view_in, 8, "cam")

    bulk(cam_all, cam_all, 3, "cam").wait_recv()
    every = cam_all[...].reshape(views, lanes)
    cameras = camera_terms(
        [jnp.broadcast_to(every[:, column : column + 1], (views, lanes)) for column in range(8)]
    )
    own = attr_ref[:, pl.ds(pl.multiple_of(view * lanes, lanes), lanes)]
    own_rows = [own[row : row + 1] for row in range(59)]
    wide_rows = [jnp.broadcast_to(row, (views, lanes)) for row in own_rows]
    _, pull = jax.vjp(lambda values: project(values, cameras), wide_rows)
    bulk(req_out, req_in, 0, "gauss").wait_send()
    bulk(ans_out, ans_in, 4, "gauss").wait_send()
    bulk(back_out, back_in, 7, "gauss").wait_send()
    bulk(cam_all, cam_all, 3, "cam").wait_send()
    target_down.wait_send()
    target_up.wait_send()
    image_down.wait_send()
    image_up.wait_send()
    bulk(view_out, view_in, 8, "cam").wait_recv()
    cots = [view_in[:, item, :] for item in range(9)]
    (row_grads,) = pull(cots[0:5] + cots[6:9])
    own_opacity = 1.0 / (1.0 + jnp.exp(-wide_rows[10]))
    row_grads[10] = cots[5] * (1.0 - own_opacity)
    for row in range(59):
        grad_ref[row : row + 1, :] = jnp.sum(row_grads[row], axis=0, keepdims=True)

    bulk(view_out, view_in, 8, "cam").wait_send()


def store_kernel(image_ref, grad_ref, image_out, grad_out, sems):
    store_image = pltpu.make_async_copy(image_ref, image_out, sems.at[0])
    store_grads = pltpu.make_async_copy(grad_ref, grad_out, sems.at[1])
    store_image.start()
    store_grads.start()
    store_image.wait()
    store_grads.wait()


def local(attributes, cameras, tile_ids, depth_order, target):
    vmem = pl.BlockSpec(memory_space=pltpu.VMEM)
    scratch = [
        (1, lanes),
        (views, 1, lanes),
        (peers, 1, lanes),
        (peers, 1, lanes),
        (peers, 2, lanes),
        (peers, 2, lanes),
        (peers, 2, lanes),
        (peers, 2, lanes),
        (views, 16, lanes),
        (views, 16, lanes),
        (3, 48, lanes),
        (3, 48, lanes),
        (59, 8, lanes),
        (9, 8, 8, lanes),
        (lanes, lanes),
        (8, slots, lanes),
        (slots, tile_side, lanes),
        (slots, tile_side, lanes),
        (6, slots, lanes),
        (6, 48, lanes),
        (9, 48, lanes),
        (9, 32, lanes),
    ]
    operands = (
        attributes,
        cameras,
        tile_ids.reshape(tiles, slots),
        depth_order.reshape(tiles, slots),
        target,
    )
    image, grads = pl.pallas_call(
        step_kernel,
        out_shape=(
            pltpu.VMEM((1, 3, tile_side, lanes), f32),
            pltpu.VMEM((59, lanes), f32),
        ),
        in_specs=[pl.BlockSpec(memory_space=pltpu.HBM)] * 5,
        out_specs=(vmem, vmem),
        scratch_shapes=[
            pltpu.VMEM((59, 8 * lanes), f32),
            pltpu.VMEM((1, 8), f32),
            pltpu.VMEM((tiles, slots), jnp.int32),
            pltpu.VMEM((tiles, slots), jnp.int32),
            pltpu.VMEM((1, 3, tile_side, lanes), f32),
        ]
        + [pltpu.VMEM(shape, f32) for shape in scratch]
        + [
            pltpu.SemaphoreType.DMA((5,)),
            pltpu.SemaphoreType.DMA((9,)),
            pltpu.SemaphoreType.DMA((9,)),
        ],
        compiler_params=pltpu.CompilerParams(
            collective_id=0, has_side_effects=True, vmem_limit_bytes=40 * 1024 * 1024
        ),
    )(*[pltpu.with_memory_space_constraint(operand, pltpu.HBM) for operand in operands])
    hbm = pl.BlockSpec(memory_space=pltpu.HBM)
    return pl.pallas_call(
        store_kernel,
        out_shape=(
            jax.ShapeDtypeStruct((1, 3, tile_side, lanes), f32),
            jax.ShapeDtypeStruct((59, lanes), f32),
        ),
        in_specs=[vmem, vmem],
        out_specs=(hbm, hbm),
        scratch_shapes=[pltpu.SemaphoreType.DMA((2,))],
    )(
        pltpu.with_memory_space_constraint(image, pltpu.VMEM),
        pltpu.with_memory_space_constraint(grads, pltpu.VMEM),
    )


def solution(mesh):
    return jax.shard_map(
        local,
        mesh=mesh,
        in_specs=(
            P(None, "gauss"),
            P("cam", None),
            P("cam", "gauss", None, None),
            P("cam", "gauss", None, None),
            P("cam", None, "gauss", None),
        ),
        out_specs=(P("cam", None, "gauss", None), P(None, ("gauss", "cam"))),
        check_vma=False,
    )
```

```python
import math

import jax
import jax.numpy as jnp
from jax import lax
from jax.experimental import pallas as pl
from jax.experimental.pallas import tpu as pltpu
from jax.sharding import PartitionSpec as P

MESH = pl.DeviceIdType.MESH
peers = 64
views = 8
tile_side = 16
tiles = 8
slots = 128
lanes = 128
capacity = 16
render_unroll = 16
behind_unroll = 2
back_unroll = 16
image_width = 128.0
image_height = 1024.0
f32 = jnp.float32
window_raw = [math.exp(-((offset - 5) ** 2) / 4.5) for offset in range(11)]
window = [weight / sum(window_raw) for weight in window_raw]
sh_consts = [
    0.0,
    -0.4886025119029199,
    0.4886025119029199,
    -0.4886025119029199,
    1.0925484305920792,
    -1.0925484305920792,
    0.31539156525252005,
    -1.0925484305920792,
    0.5462742152960396,
    -0.5900435899266435,
    2.890611442640554,
    -0.4570457994644658,
    0.3731763325901154,
    -0.4570457994644658,
    1.445305721320277,
    -0.5900435899266435,
]


def unit_quat(parts):
    length_q = jnp.sqrt(
        parts[0] * parts[0] + parts[1] * parts[1] + parts[2] * parts[2] + parts[3] * parts[3]
    )
    return [part / length_q for part in parts]


def quat_matrix(quaternion):
    q_w, q_x, q_y, q_z = quaternion
    return [
        [
            1.0 - 2.0 * (q_y * q_y + q_z * q_z),
            2.0 * (q_x * q_y - q_w * q_z),
            2.0 * (q_x * q_z + q_w * q_y),
        ],
        [
            2.0 * (q_x * q_y + q_w * q_z),
            1.0 - 2.0 * (q_x * q_x + q_z * q_z),
            2.0 * (q_y * q_z - q_w * q_x),
        ],
        [
            2.0 * (q_x * q_z - q_w * q_y),
            2.0 * (q_y * q_z + q_w * q_x),
            1.0 - 2.0 * (q_x * q_x + q_y * q_y),
        ],
    ]


def camera_terms(camera):
    cam_rot = quat_matrix(unit_quat(camera[0:4]))
    shift_vec = camera[4:7]
    centre = [
        -(
            cam_rot[0][axis_col] * shift_vec[0]
            + cam_rot[1][axis_col] * shift_vec[1]
            + cam_rot[2][axis_col] * shift_vec[2]
        )
        for axis_col in range(3)
    ]
    return cam_rot, shift_vec, camera[7] * image_width, camera[7] * image_height, centre


def project(attr_rows, camera):
    cam_rot, shift_vec, horizontal_focal, focal_y, centre = camera
    position = [attr_rows[0], attr_rows[1], attr_rows[2]]
    view_pos = [
        cam_rot[axis_row][0] * position[0]
        + cam_rot[axis_row][1] * position[1]
        + cam_rot[axis_row][2] * position[2]
        + shift_vec[axis_row]
        for axis_row in range(3)
    ]
    inv_z = 1.0 / view_pos[2]
    focal_u = horizontal_focal * inv_z
    focal_v = focal_y * inv_z
    slope_u = focal_u * view_pos[0]
    slope_v = focal_v * view_pos[1]
    mean_u = 0.5 * image_width + slope_u
    mean_v = 0.5 * image_height + slope_v
    gauss_rot = quat_matrix(unit_quat([attr_rows[6], attr_rows[7], attr_rows[8], attr_rows[9]]))
    scales = [jnp.exp(attr_rows[3]), jnp.exp(attr_rows[4]), jnp.exp(attr_rows[5])]
    skew_u = slope_u * inv_z
    skew_v = slope_v * inv_z
    project_mat = [
        [focal_u * cam_rot[0][axis_col] - skew_u * cam_rot[2][axis_col] for axis_col in range(3)],
        [focal_v * cam_rot[1][axis_col] - skew_v * cam_rot[2][axis_col] for axis_col in range(3)],
    ]
    spread = [
        [
            (
                project_mat[axis_row][0] * gauss_rot[0][axis_col]
                + project_mat[axis_row][1] * gauss_rot[1][axis_col]
                + project_mat[axis_row][2] * gauss_rot[2][axis_col]
            )
            * scales[axis_col]
            for axis_col in range(3)
        ]
        for axis_row in range(2)
    ]
    cov_a = spread[0][0] * spread[0][0] + spread[0][1] * spread[0][1] + spread[0][2] * spread[0][2] + 0.3
    cov_b = spread[0][0] * spread[1][0] + spread[0][1] * spread[1][1] + spread[0][2] * spread[1][2]
    cov_c = spread[1][0] * spread[1][0] + spread[1][1] * spread[1][1] + spread[1][2] * spread[1][2] + 0.3
    inv_det = 1.0 / (cov_a * cov_c - cov_b * cov_b)
    offsets = [position[axis_col] - centre[axis_col] for axis_col in range(3)]
    distance = jnp.sqrt(offsets[0] * offsets[0] + offsets[1] * offsets[1] + offsets[2] * offsets[2])
    inv_distance = 1.0 / distance
    dir_x, dir_y, dir_z = [offset * inv_distance for offset in offsets]
    sq_x, sq_y, sq_z = (dir_x * dir_x, dir_y * dir_y, dir_z * dir_z)
    sh_basis = [
        None,
        dir_y,
        dir_z,
        dir_x,
        dir_x * dir_y,
        dir_y * dir_z,
        2.0 * sq_z - sq_x - sq_y,
        dir_x * dir_z,
        sq_x - sq_y,
        dir_y * (3.0 * sq_x - sq_y),
        dir_x * dir_y * dir_z,
        dir_y * (4.0 * sq_z - sq_x - sq_y),
        dir_z * (2.0 * sq_z - 3.0 * sq_x - 3.0 * sq_y),
        dir_x * (4.0 * sq_z - sq_x - sq_y),
        dir_z * (sq_x - sq_y),
        dir_x * (sq_x - 3.0 * sq_y),
    ]
    scaled = [None] + [sh_consts[degree] * sh_basis[degree] for degree in range(1, 16)]
    colours = []
    for channel in range(3):
        colour = 0.5 + 0.28209479177387814 * attr_rows[11 + channel]
        for degree in range(1, 16):
            colour = colour + scaled[degree] * attr_rows[11 + 3 * degree + channel]
        colours.append(colour)
    return [mean_u, mean_v, cov_c * inv_det, -cov_b * inv_det, cov_a * inv_det] + colours


def iota(shape, dim):
    return lax.broadcasted_iota(jnp.int32, shape, dim)


def lane_pick(values, index):
    return jnp.take_along_axis(values, index, axis=1, mode="promise_in_bounds")


def halves(values):
    high = values.astype(jnp.bfloat16)
    low = (values - high.astype(f32)).astype(jnp.bfloat16)
    return high, low


def dot_nt(left, right):
    return lax.dot_general(left, right, (((1,), (1,)), ((), ())), preferred_element_type=f32)


def row_sums(blocks):
    row = iota((8, lanes), 0)
    level = []
    for i in range(4):
        first, second = blocks[i], blocks[i + 4]
        level.append(
            jnp.where(row < 4, first, second)
            + pltpu.roll(jnp.where(row < 4, second, first), 4, 0)
        )
    pairs = []
    for i in range(2):
        first, second = level[i], level[i + 2]
        first = first + pltpu.roll(first, 6, 0)
        second = second + pltpu.roll(second, 2, 0)
        pairs.append(jnp.where((row & 2) == 0, first, second))
    first = pairs[0] + pltpu.roll(pairs[0], 7, 0)
    second = pairs[1] + pltpu.roll(pairs[1], 1, 0)
    return jnp.where((row & 1) == 0, first, second)


def blur_rows(ref, start, count):
    total = window[5] * ref[:, pl.ds(start + 5, count), :]
    for offset in range(5):
        total = total + window[offset] * (
            ref[:, pl.ds(start + offset, count), :]
            + ref[:, pl.ds(start + 10 - offset, count), :]
        )
    return total


def blur_columns(planes, band):
    count, rows, _ = planes.shape
    flat = planes.reshape(count * rows, lanes)
    out = jnp.dot(flat, band, preferred_element_type=f32, precision=lax.Precision.HIGHEST)
    return out.reshape(count, rows, lanes)


def step_kernel(
    attr_hbm,
    cam_hbm,
    ids_hbm,
    order_hbm,
    target_hbm,
    image_ref,
    grad_ref,
    attr_ref,
    cam_ref,
    ids_ref,
    order_ref,
    target_ref,
    cam_row,
    cam_all,
    req_out,
    req_in,
    ans_out,
    ans_in,
    back_out,
    back_in,
    view_out,
    view_in,
    ext_x,
    ext_y,
    attr_rows,
    table_rows,
    stack,
    wide,
    alpha_s,
    weight_s,
    gains,
    sums,
    choosers,
    spots,
    in_chunk,
    back_stack,
    planes_y,
    planes_x,
    partials,
    load_sems,
    send_sems,
    recv_sems,
):
    me = lax.axis_index("gauss")
    view = lax.axis_index("cam")
    loads = [
        pltpu.make_async_copy(source, into, load_sems.at[item])
        for item, (source, into) in enumerate(
            (
                (ids_hbm, ids_ref),
                (order_hbm, order_ref),
                (target_hbm, target_ref),
                (cam_hbm, cam_ref),
                (attr_hbm, attr_ref),
            )
        )
    ]
    my_z = lax.div(me, 8)
    my_y = lax.rem(me, 8)
    my_x = lax.div(view, 2)
    my_core = lax.rem(view, 2)
    along_y = [lax.rem(my_y + step, 8) for step in (4, 3, 5, 2, 6, 1, 7)]
    along_x = [lax.rem(my_x + step, 4) * 2 for step in (2, 1, 3)]

    def each_peer(visit):
        def ring(step, carry):
            from_z = 4 + (1 - 2 * lax.rem(step, 2)) * lax.div(step + 1, 2)
            first = lax.rem(my_z + from_z, 8) * 8
            for place in along_y:
                visit(first + place)
            visit(first + my_y)
            return carry

        lax.fori_loop(0, 7, ring, 0)
        for place in along_y:
            visit(my_z * 8 + place)

    def each_view(visit):
        for place in along_x:
            visit(place + my_core)
            visit(place + 1 - my_core)
        visit(my_x * 2 + 1 - my_core)

    below = lax.rem(me + 1, peers)
    above = lax.rem(me + peers - 1, peers)
    next_view = lax.rem(view + 1, views)

    barrier = pltpu.get_barrier_semaphore()

    def greet_peer(other):
        pl.semaphore_signal(barrier, inc=1, device_id={"gauss": other}, device_id_type=MESH)

    def greet_view(other):
        pl.semaphore_signal(barrier, inc=1, device_id={"cam": other}, device_id_type=MESH)

    each_peer(greet_peer)
    each_view(greet_view)
    for load in loads:
        load.start()

    def remote(src, dst, phase, where):
        return pltpu.make_async_remote_copy(
            src_ref=src,
            dst_ref=dst,
            send_sem=send_sems.at[phase],
            recv_sem=recv_sems.at[phase],
            device_id=where,
            device_id_type=MESH,
        )

    def exchange(out, into, phase, axis):
        own = me if axis == "gauss" else view

        def send(other):
            remote(out.at[other], into.at[own], phase, {axis: other}).start()

        if axis == "gauss":
            each_peer(send)
        else:
            each_view(send)
        into[pl.ds(own, 1)] = out[pl.ds(own, 1)]

    def bulk(out, into, phase, axis):
        count = peers if axis == "gauss" else views
        return remote(
            out.at[pl.ds(0, count - 1)],
            into.at[pl.ds(0, count - 1)],
            phase,
            {axis: below if axis == "gauss" else next_view},
        )

    loads[0].wait()
    loads[1].wait()
    ids = lane_pick(ids_ref[...], order_ref[...])
    present = ids >= 0
    owner = ids >> 10
    local_id = ids & 1023
    chunk_id = (local_id >> 7).astype(f32)
    lane_id = (local_id & 127).astype(f32)
    owner_row = iota((peers, slots), 0)
    before = (iota((slots, slots), 0) < iota((slots, slots), 1)).astype(jnp.bfloat16)
    rank_rows = iota((capacity, slots), 0)
    slot_row = iota((1, slots), 1).astype(f32)
    base = jnp.zeros((peers, 1), f32)
    asked = jnp.zeros((peers, lanes), f32)
    ranks = []
    for tile in range(tiles):
        named = owner_row == owner[tile : tile + 1]
        member = jnp.where(named, 1.0, 0.0)
        earlier = jnp.dot(member.astype(jnp.bfloat16), before, preferred_element_type=f32)
        rank = jnp.sum(member * (earlier + base), axis=0, keepdims=True)
        base = base + jnp.sum(member, axis=1, keepdims=True)
        ranks.append(rank)
        hit = rank_rows == rank.astype(jnp.int32)
        terms = [
            jnp.where(hit, chunk_id[tile : tile + 1], 0.0),
            jnp.where(hit, lane_id[tile : tile + 1], 0.0),
            jnp.where(hit, 1.0, 0.0),
            jnp.where(hit, float(tile), 0.0),
            jnp.where(hit, slot_row, 0.0),
            jnp.zeros((lanes - 5 * capacity, slots), f32),
        ]
        asked = asked + dot_nt(
            member.astype(jnp.bfloat16), jnp.concatenate(terms, axis=0).astype(jnp.bfloat16)
        )
    rank = jnp.concatenate(ranks, axis=0).astype(jnp.int32)
    req_out[...] = asked.reshape(peers, 1, lanes)
    loads[2].wait()
    loads[3].wait()
    cam_row[...] = jnp.zeros((1, lanes), f32)
    cam_row[:, 0:8] = cam_ref[...]
    cam_all[pl.ds(view, 1)] = cam_row[...].reshape(1, 1, lanes)
    ext_y[:, 16:32, :] = target_ref[0]

    pl.semaphore_wait(barrier, peers + views - 2)

    exchange(req_out, req_in, 0, "gauss")
    target_down = remote(ext_y.at[:, 16:32, :], ext_y.at[:, 0:16, :], 1, {"gauss": below})
    target_up = remote(ext_y.at[:, 16:32, :], ext_y.at[:, 32:48, :], 2, {"gauss": above})
    target_down.start()
    target_up.start()

    each_view(lambda other: remote(cam_row, cam_all.at[view], 3, {"cam": other}).start())

    loads[4].wait()
    for chunk in range(8):
        attr_rows[:, chunk, :] = attr_ref[:, chunk * lanes : (chunk + 1) * lanes]
    camera = [
        jnp.broadcast_to(cam_row[0:1, column : column + 1], (8, lanes)) for column in range(8)
    ]
    rows = [attr_rows[row] for row in range(59)]
    flat_features = project(rows, camera_terms(camera))
    opacity = 1.0 / (1.0 + jnp.exp(-rows[10]))
    table = flat_features[0:5] + [opacity] + flat_features[5:8]
    for feature in range(9):
        for chunk in range(8):
            table_rows[feature, chunk] = jnp.broadcast_to(
                table[feature][chunk : chunk + 1], (8, lanes)
            )

    def by_rank(values):
        return jnp.concatenate([values, pltpu.roll(values, lanes - 8, 1)], axis=0).T

    bulk(req_out, req_in, 0, "gauss").wait_recv()
    wanted = by_rank(req_in[...].reshape(peers, lanes))
    want_chunk = wanted[0:8].astype(jnp.int32)
    want_lane = wanted[16:24].astype(jnp.int32)
    want_there = wanted[32:40]
    at_chunk = [want_chunk == chunk for chunk in range(8)]
    stack[...] = jnp.zeros((lanes, lanes), f32)
    for feature in range(9):
        picked = jnp.zeros((8, lanes), f32)
        for chunk in range(8):
            row = table_rows[feature, chunk]
            picked = jnp.where(at_chunk[chunk], lane_pick(row, want_lane), picked)
        stack[8 * feature : 8 * feature + 8] = picked
    turned = stack[...].T
    ans_out[:, 0, :] = turned[0:peers]
    ans_out[:, 1, :] = turned[peers:]
    exchange(ans_out, ans_in, 4, "gauss")

    outer = iota((slots, lanes), 0)
    inner = iota((slots, lanes), 1)
    band = jnp.zeros((lanes, lanes), f32)
    for offset in range(11):
        band = jnp.where(inner - outer == offset - 5, window[offset], band)
    target_down.wait_recv()
    target_up.wait_recv()
    ext_y[:, 0:16, :] = ext_y[:, 0:16, :] * jnp.where(me > 0, 1.0, 0.0)
    ext_y[:, 32:48, :] = ext_y[:, 32:48, :] * jnp.where(me < peers - 1, 1.0, 0.0)
    photo = ext_y[...]
    planes_y[0:3] = photo
    planes_y[3:6] = photo * photo
    blurred_y = blur_columns(blur_rows(planes_y, 6, 32), band)
    mean_y = blurred_y[0:3]
    var_y = blurred_y[3:6] - mean_y * mean_y

    sent = by_rank(asked)
    sent_there = sent[32:40]
    sent_tile = sent[48:56].astype(jnp.int32)
    sent_slot = sent[64:72].astype(jnp.int32)

    bulk(ans_out, ans_in, 4, "gauss").wait_recv()
    answers = jnp.concatenate([ans_in[:, 0, :], ans_in[:, 1, :]], axis=0).T
    from_lane = jnp.where(present, (rank >> 3) * peers + owner, 0)
    from_row = jnp.where(present, rank & 7, 8)
    at_row = [from_row == row for row in range(8)]
    features = []
    stack[72:128] = jnp.zeros((56, lanes), f32)
    for feature in range(9):
        picked = jnp.zeros((8, lanes), f32)
        for row in range(8):
            source = jnp.broadcast_to(
                answers[8 * feature + row : 8 * feature + row + 1], (8, lanes)
            )
            picked = jnp.where(at_row[row], lane_pick(source, from_lane), picked)
        stack[8 * feature : 8 * feature + 8] = picked
        features.append(picked)
    by_slot = stack[...].T
    spread = [lane_pick(by_slot, 8 * feature + (inner >> 4)) for feature in range(9)]
    slot_u, slot_v, conic_a, conic_b, conic_c, slot_opacity = spread[0:6]
    off_u = inner.astype(f32) + 0.5 - slot_u
    wide[0] = -0.5 * conic_a * off_u * off_u
    wide[1] = -conic_b * off_u
    wide[2] = -0.5 * conic_c
    wide[3] = slot_v
    wide[4] = slot_opacity
    wide[5] = spread[6]
    wide[6] = spread[7]
    wide[7] = spread[8]
    pixel_row = (iota((tile_side, lanes), 0) + me * tile_side).astype(f32) + 0.5

    def render(step, carry):
        transmit, red, green, blue = carry
        for part in range(render_unroll):
            first = pl.multiple_of((step * render_unroll + part) * 8, 8)
            block = [wide[item, pl.ds(first, 8), :] for item in range(8)]
            for i in range(8):
                flat, slope, curve, mean_v, alpha_top, c_0, c_1, c_2 = [
                    item[i : i + 1] for item in block
                ]
                off_v = pixel_row - mean_v
                alpha = alpha_top * jnp.exp(flat + off_v * (slope + curve * off_v))
                weight = alpha * transmit
                transmit = transmit - weight
                red = red + weight * c_0
                green = green + weight * c_1
                blue = blue + weight * c_2
                alpha_s[first + i] = alpha
                weight_s[first + i] = weight
        return transmit, red, green, blue

    zero = jnp.zeros((tile_side, lanes), f32)
    _, red, green, blue = lax.fori_loop(0, slots // 8 // render_unroll, render, (zero + 1.0, zero, zero, zero))
    image = jnp.stack([red, green, blue])
    ext_x[:, 16:32, :] = image
    image_down = remote(ext_x.at[:, 16:32, :], ext_x.at[:, 0:16, :], 5, {"gauss": below})
    image_up = remote(ext_x.at[:, 16:32, :], ext_x.at[:, 32:48, :], 6, {"gauss": above})
    image_down.start()
    image_up.start()
    image_ref[0] = image

    def look_behind(step, carry):
        behind = list(carry)
        for part in range(behind_unroll):
            first = pl.multiple_of((slots // 8 - 1 - step * behind_unroll - part) * 8, 8)
            block = [wide[item, pl.ds(first, 8), :] for item in (5, 6, 7)]
            for i in reversed(range(8)):
                alpha = alpha_s[first + i]
                weight = weight_s[first + i]
                for channel in range(3):
                    gain = block[channel][i : i + 1] - behind[channel]
                    behind[channel] = behind[channel] + alpha * gain
                    gains[channel, first + i] = weight * gain
        return tuple(behind)

    lax.fori_loop(0, slots // 8 // behind_unroll, look_behind, (zero, zero, zero))
    back_stack[...] = jnp.zeros((8, 16, lanes), f32)
    for item in range(9):
        choosers[item] = (inner == 8 * item + (outer >> 4)).astype(jnp.bfloat16)

    image_down.wait_recv()
    image_up.wait_recv()
    ext_x[:, 0:16, :] = ext_x[:, 0:16, :] * jnp.where(me > 0, 1.0, 0.0)
    ext_x[:, 32:48, :] = ext_x[:, 32:48, :] * jnp.where(me < peers - 1, 1.0, 0.0)

    shown = ext_x[...]
    planes_x[0:3] = shown
    planes_x[3:6] = shown * shown
    planes_x[6:9] = shown * photo
    blurred_x = blur_columns(blur_rows(planes_x, 6, 32), band)
    mean_x = blurred_x[0:3]
    var_x = blurred_x[3:6] - mean_x * mean_x
    cov_xy = blurred_x[6:9] - mean_x * mean_y
    top_1 = 2.0 * mean_x * mean_y + 0.0001
    top_2 = 2.0 * cov_xy + 0.0009
    inv_1 = 1.0 / (mean_x * mean_x + mean_y * mean_y + 0.0001)
    inv_2 = 1.0 / (var_x + var_y + 0.0009)
    inv_both = inv_1 * inv_2
    ssim = top_1 * top_2 * inv_both
    map_row = iota((3, 32, lanes), 1) + (me * tile_side - 5)
    in_view = (map_row >= 0) & (map_row < peers * tile_side)
    share = jnp.where(in_view, -0.2 / 256.0, 0.0)
    d_cov = share * 2.0 * top_1 * inv_both
    d_var = -share * ssim * inv_2
    d_mean = (
        share * (2.0 * mean_y * top_2 * inv_both - 2.0 * mean_x * ssim * inv_1)
        - 2.0 * mean_x * d_var
        - mean_y * d_cov
    )
    partials[0:3] = d_mean
    partials[3:6] = d_var
    partials[6:9] = d_cov
    pulled = blur_columns(blur_rows(partials, 0, 16), band)
    own_photo = target_ref[0]
    gap = image - own_photo
    loss_grad = (
        pulled[0:3]
        + 2.0 * image * pulled[3:6]
        + own_photo * pulled[6:9]
        + (0.8 / 256.0) * gap / jnp.sqrt(gap * gap + 0.0025)
    )
    grad_0, grad_1, grad_2 = loss_grad[0], loss_grad[1], loss_grad[2]

    half = tile_side // 2
    row_at = iota((half, lanes), 0).astype(f32) + (0.5 - half)
    row_high = row_at + half
    row_at_2 = row_at * row_at
    row_high_2 = row_high * row_high
    grads_low = [grad_0[:half], grad_1[:half], grad_2[:half]]
    grads_high = [grad_0[half:], grad_1[half:], grad_2[half:]]

    def render_back(step, carry):
        for part in range(back_unroll):
            first = pl.multiple_of((step * back_unroll + part) * 8, 8)
            kept = [[None] * 8 for _ in range(6)]
            for i in range(8):
                weight = weight_s[first + i]
                low, high = 0.0, 0.0
                for channel in range(3):
                    gain = gains[channel, first + i]
                    low = low + gain[:half] * grads_low[channel]
                    high = high + gain[half:] * grads_high[channel]
                    kept[3 + channel][i] = (
                        weight[:half] * grads_low[channel] + weight[half:] * grads_high[channel]
                    )
                kept[0][i] = low + high
                kept[1][i] = low * row_at + high * row_high
                kept[2][i] = low * row_at_2 + high * row_high_2
            for item in range(6):
                sums[item, pl.ds(first, 8), :] = row_sums(kept[item])
        return carry

    lax.fori_loop(0, slots // 8 // back_unroll, render_back, 0)

    to_centre = (me * tile_side + half).astype(f32) - wide[3]
    sum_0 = sums[0]
    sum_1 = sums[1] + to_centre * sum_0
    sum_2 = sums[2] + to_centre * (sums[1] + sum_1)
    sum_0u = sum_0 * off_u
    quantities = [
        sum_0, sum_0u, sum_0u * off_u, sum_1, sum_1 * off_u, sum_2, sums[3], sums[4], sums[5]
    ]
    gathered = jnp.zeros((slots, lanes), f32)
    for item in range(9):
        for part in halves(quantities[item]):
            gathered = gathered + jnp.dot(part, choosers[item], preferred_element_type=f32)
    per_tile = gathered.T
    m_0, m_u, m_uu, m_v, m_uv, m_vv = [per_tile[8 * item : 8 * item + 8] for item in range(6)]
    slot_grads = [
        features[2] * m_u + features[3] * m_v,
        features[4] * m_v + features[3] * m_u,
        -0.5 * m_uu,
        -m_uv,
        -0.5 * m_vv,
        m_0,
        per_tile[48:56],
        per_tile[56:64],
        per_tile[64:72],
    ]

    at_tile = [(sent_tile == tile) & (sent_there > 0.5) for tile in range(tiles)]
    for feature in range(9):
        picked = jnp.zeros((8, lanes), f32)
        for tile in range(tiles):
            row = jnp.broadcast_to(slot_grads[feature][tile : tile + 1], (8, lanes))
            picked = jnp.where(at_tile[tile], lane_pick(row, sent_slot), picked)
        back_stack[:, feature, :] = picked
    turned = back_stack[...].reshape(lanes, lanes).T
    back_out[:, 0, :] = turned[0:peers]
    back_out[:, 1, :] = turned[peers:]
    exchange(back_out, back_in, 7, "gauss")

    for row in range(8):
        spots[:, row * lanes : (row + 1) * lanes] = (
            outer == want_lane[row : row + 1]
        ).astype(jnp.bfloat16)
        for chunk in range(8):
            here = (want_chunk[row : row + 1] == chunk) & (want_there[row : row + 1] > 0.5)
            in_chunk[row, chunk] = jnp.broadcast_to(jnp.where(here, 1.0, 0.0), (16, lanes)).astype(
                jnp.bfloat16
            )
    bulk(back_out, back_in, 7, "gauss").wait_recv()
    returned = jnp.concatenate([back_in[:, 0, :], back_in[:, 1, :]], axis=0).T
    pieces = [[], []]
    for row in range(8):
        for part, split in enumerate(halves(returned[16 * row : 16 * row + 16])):
            pieces[part].append(
                jnp.concatenate([split * in_chunk[row, chunk] for chunk in range(8)], axis=0)
            )
    block_grad = sum(dot_nt(jnp.concatenate(piece, axis=1), spots[...]) for piece in pieces)
    view_out[...] = block_grad.reshape(views, 16, lanes)
    exchange(view_out, view_in, 8, "cam")

    bulk(cam_all, cam_all, 3, "cam").wait_recv()
    every = cam_all[...].reshape(views, lanes)
    cameras = camera_terms(
        [jnp.broadcast_to(every[:, column : column + 1], (views, lanes)) for column in range(8)]
    )
    own = attr_ref[:, pl.ds(pl.multiple_of(view * lanes, lanes), lanes)]
    own_rows = [own[row : row + 1] for row in range(59)]
    wide_rows = [jnp.broadcast_to(row, (views, lanes)) for row in own_rows]
    _, pull = jax.vjp(lambda values: project(values, cameras), wide_rows)
    bulk(req_out, req_in, 0, "gauss").wait_send()
    bulk(ans_out, ans_in, 4, "gauss").wait_send()
    bulk(back_out, back_in, 7, "gauss").wait_send()
    bulk(cam_all, cam_all, 3, "cam").wait_send()
    target_down.wait_send()
    target_up.wait_send()
    image_down.wait_send()
    image_up.wait_send()
    bulk(view_out, view_in, 8, "cam").wait_recv()
    cots = [view_in[:, item, :] for item in range(9)]
    (row_grads,) = pull(cots[0:5] + cots[6:9])
    own_opacity = 1.0 / (1.0 + jnp.exp(-wide_rows[10]))
    row_grads[10] = cots[5] * (1.0 - own_opacity)
    row_grads = row_grads + [jnp.zeros((views, lanes), f32)] * 5
    for first in range(0, 64, 8):
        count = min(8, 59 - first)
        grad_ref[first : first + count, :] = row_sums(row_grads[first : first + 8])[:count]
    bulk(view_out, view_in, 8, "cam").wait_send()


def store_kernel(image_ref, grad_ref, image_out, grad_out, sems):
    store_image = pltpu.make_async_copy(image_ref, image_out, sems.at[0])
    store_grads = pltpu.make_async_copy(grad_ref, grad_out, sems.at[1])
    store_image.start()
    store_grads.start()
    store_image.wait()
    store_grads.wait()


def local(attributes, cameras, tile_ids, depth_order, target):
    vmem = pl.BlockSpec(memory_space=pltpu.VMEM)
    scratch = [
        (1, lanes),
        (views, 1, lanes),
        (peers, 1, lanes),
        (peers, 1, lanes),
        (peers, 2, lanes),
        (peers, 2, lanes),
        (peers, 2, lanes),
        (peers, 2, lanes),
        (views, 16, lanes),
        (views, 16, lanes),
        (3, 48, lanes),
        (3, 48, lanes),
        (59, 8, lanes),
        (9, 8, 8, lanes),
        (lanes, lanes),
        (8, slots, lanes),
        (slots, tile_side, lanes),
        (slots, tile_side, lanes),
        (3, slots, tile_side, lanes),
        (6, slots, lanes),
        (9, slots, lanes, jnp.bfloat16),
        (lanes, 8 * lanes, jnp.bfloat16),
        (8, 8, 16, lanes, jnp.bfloat16),
        (8, 16, lanes),
        (6, 48, lanes),
        (9, 48, lanes),
        (9, 32, lanes),
    ]
    operands = (
        attributes,
        cameras,
        tile_ids.reshape(tiles, slots),
        depth_order.reshape(tiles, slots),
        target,
    )
    image, grads = pl.pallas_call(
        step_kernel,
        out_shape=(
            pltpu.VMEM((1, 3, tile_side, lanes), f32),
            pltpu.VMEM((59, lanes), f32),
        ),
        in_specs=[pl.BlockSpec(memory_space=pltpu.HBM)] * 5,
        out_specs=(vmem, vmem),
        scratch_shapes=[
            pltpu.VMEM((59, 8 * lanes), f32),
            pltpu.VMEM((1, 8), f32),
            pltpu.VMEM((tiles, slots), jnp.int32),
            pltpu.VMEM((tiles, slots), jnp.int32),
            pltpu.VMEM((1, 3, tile_side, lanes), f32),
        ]
        + [
            pltpu.VMEM(shape, f32)
            if isinstance(shape[-1], int)
            else pltpu.VMEM(shape[:-1], shape[-1])
            for shape in scratch
        ]
        + [
            pltpu.SemaphoreType.DMA((5,)),
            pltpu.SemaphoreType.DMA((9,)),
            pltpu.SemaphoreType.DMA((9,)),
        ],
        compiler_params=pltpu.CompilerParams(
            collective_id=0, has_side_effects=True, vmem_limit_bytes=40 * 1024 * 1024
        ),
    )(*[pltpu.with_memory_space_constraint(operand, pltpu.HBM) for operand in operands])
    hbm = pl.BlockSpec(memory_space=pltpu.HBM)
    return pl.pallas_call(
        store_kernel,
        out_shape=(
            jax.ShapeDtypeStruct((1, 3, tile_side, lanes), f32),
            jax.ShapeDtypeStruct((59, lanes), f32),
        ),
        in_specs=[vmem, vmem],
        out_specs=(hbm, hbm),
        scratch_shapes=[pltpu.SemaphoreType.DMA((2,))],
    )(
        pltpu.with_memory_space_constraint(image, pltpu.VMEM),
        pltpu.with_memory_space_constraint(grads, pltpu.VMEM),
    )


def solution(mesh):
    return jax.shard_map(
        local,
        mesh=mesh,
        in_specs=(
            P(None, "gauss"),
            P("cam", None),
            P("cam", "gauss", None, None),
            P("cam", "gauss", None, None),
            P("cam", None, "gauss", None),
        ),
        out_specs=(P("cam", None, "gauss", None), P(None, ("gauss", "cam"))),
        check_vma=False,
    )
```

```python
import math

import jax
import jax.numpy as jnp
from jax import lax
from jax.experimental import pallas as pl
from jax.experimental.pallas import tpu as pltpu
from jax.sharding import PartitionSpec as P

MESH = pl.DeviceIdType.MESH
peers = 64
hubs = 32
views = 8
tile_side = 16
tiles = 8
slots = 128
lanes = 128
capacity = 16
render_unroll = 16
behind_unroll = 2
back_unroll = 16
image_width = 128.0
image_height = 1024.0
f32 = jnp.float32
window_raw = [math.exp(-((offset - 5) ** 2) / 4.5) for offset in range(11)]
window = [weight / sum(window_raw) for weight in window_raw]
sh_consts = [
    0.0,
    -0.4886025119029199,
    0.4886025119029199,
    -0.4886025119029199,
    1.0925484305920792,
    -1.0925484305920792,
    0.31539156525252005,
    -1.0925484305920792,
    0.5462742152960396,
    -0.5900435899266435,
    2.890611442640554,
    -0.4570457994644658,
    0.3731763325901154,
    -0.4570457994644658,
    1.445305721320277,
    -0.5900435899266435,
]


def unit_quat(parts):
    length_q = jnp.sqrt(
        parts[0] * parts[0] + parts[1] * parts[1] + parts[2] * parts[2] + parts[3] * parts[3]
    )
    return [part / length_q for part in parts]


def quat_matrix(quaternion):
    q_w, q_x, q_y, q_z = quaternion
    return [
        [
            1.0 - 2.0 * (q_y * q_y + q_z * q_z),
            2.0 * (q_x * q_y - q_w * q_z),
            2.0 * (q_x * q_z + q_w * q_y),
        ],
        [
            2.0 * (q_x * q_y + q_w * q_z),
            1.0 - 2.0 * (q_x * q_x + q_z * q_z),
            2.0 * (q_y * q_z - q_w * q_x),
        ],
        [
            2.0 * (q_x * q_z - q_w * q_y),
            2.0 * (q_y * q_z + q_w * q_x),
            1.0 - 2.0 * (q_x * q_x + q_y * q_y),
        ],
    ]


def camera_terms(camera):
    cam_rot = quat_matrix(unit_quat(camera[0:4]))
    shift_vec = camera[4:7]
    centre = [
        -(
            cam_rot[0][axis_col] * shift_vec[0]
            + cam_rot[1][axis_col] * shift_vec[1]
            + cam_rot[2][axis_col] * shift_vec[2]
        )
        for axis_col in range(3)
    ]
    return cam_rot, shift_vec, camera[7] * image_width, camera[7] * image_height, centre


def project(attr_rows, camera):
    cam_rot, shift_vec, horizontal_focal, focal_y, centre = camera
    position = [attr_rows[0], attr_rows[1], attr_rows[2]]
    view_pos = [
        cam_rot[axis_row][0] * position[0]
        + cam_rot[axis_row][1] * position[1]
        + cam_rot[axis_row][2] * position[2]
        + shift_vec[axis_row]
        for axis_row in range(3)
    ]
    inv_z = 1.0 / view_pos[2]
    focal_u = horizontal_focal * inv_z
    focal_v = focal_y * inv_z
    slope_u = focal_u * view_pos[0]
    slope_v = focal_v * view_pos[1]
    mean_u = 0.5 * image_width + slope_u
    mean_v = 0.5 * image_height + slope_v
    gauss_rot = quat_matrix(unit_quat([attr_rows[6], attr_rows[7], attr_rows[8], attr_rows[9]]))
    scales = [jnp.exp(attr_rows[3]), jnp.exp(attr_rows[4]), jnp.exp(attr_rows[5])]
    skew_u = slope_u * inv_z
    skew_v = slope_v * inv_z
    project_mat = [
        [focal_u * cam_rot[0][axis_col] - skew_u * cam_rot[2][axis_col] for axis_col in range(3)],
        [focal_v * cam_rot[1][axis_col] - skew_v * cam_rot[2][axis_col] for axis_col in range(3)],
    ]
    spread = [
        [
            (
                project_mat[axis_row][0] * gauss_rot[0][axis_col]
                + project_mat[axis_row][1] * gauss_rot[1][axis_col]
                + project_mat[axis_row][2] * gauss_rot[2][axis_col]
            )
            * scales[axis_col]
            for axis_col in range(3)
        ]
        for axis_row in range(2)
    ]
    cov_a = spread[0][0] * spread[0][0] + spread[0][1] * spread[0][1] + spread[0][2] * spread[0][2] + 0.3
    cov_b = spread[0][0] * spread[1][0] + spread[0][1] * spread[1][1] + spread[0][2] * spread[1][2]
    cov_c = spread[1][0] * spread[1][0] + spread[1][1] * spread[1][1] + spread[1][2] * spread[1][2] + 0.3
    inv_det = 1.0 / (cov_a * cov_c - cov_b * cov_b)
    offsets = [position[axis_col] - centre[axis_col] for axis_col in range(3)]
    distance = jnp.sqrt(offsets[0] * offsets[0] + offsets[1] * offsets[1] + offsets[2] * offsets[2])
    inv_distance = 1.0 / distance
    dir_x, dir_y, dir_z = [offset * inv_distance for offset in offsets]
    sq_x, sq_y, sq_z = (dir_x * dir_x, dir_y * dir_y, dir_z * dir_z)
    sh_basis = [
        None,
        dir_y,
        dir_z,
        dir_x,
        dir_x * dir_y,
        dir_y * dir_z,
        2.0 * sq_z - sq_x - sq_y,
        dir_x * dir_z,
        sq_x - sq_y,
        dir_y * (3.0 * sq_x - sq_y),
        dir_x * dir_y * dir_z,
        dir_y * (4.0 * sq_z - sq_x - sq_y),
        dir_z * (2.0 * sq_z - 3.0 * sq_x - 3.0 * sq_y),
        dir_x * (4.0 * sq_z - sq_x - sq_y),
        dir_z * (sq_x - sq_y),
        dir_x * (sq_x - 3.0 * sq_y),
    ]
    scaled = [None] + [sh_consts[degree] * sh_basis[degree] for degree in range(1, 16)]
    colours = []
    for channel in range(3):
        colour = 0.5 + 0.28209479177387814 * attr_rows[11 + channel]
        for degree in range(1, 16):
            colour = colour + scaled[degree] * attr_rows[11 + 3 * degree + channel]
        colours.append(colour)
    return [mean_u, mean_v, cov_c * inv_det, -cov_b * inv_det, cov_a * inv_det] + colours


def iota(shape, dim):
    return lax.broadcasted_iota(jnp.int32, shape, dim)


def lane_pick(values, index):
    return jnp.take_along_axis(values, index, axis=1, mode="promise_in_bounds")


def halves(values):
    high = values.astype(jnp.bfloat16)
    low = (values - high.astype(f32)).astype(jnp.bfloat16)
    return high, low


def dot_nt(left, right):
    return lax.dot_general(left, right, (((1,), (1,)), ((), ())), preferred_element_type=f32)


def row_sums(blocks):
    row = iota((8, lanes), 0)
    level = []
    for i in range(4):
        first, second = blocks[i], blocks[i + 4]
        level.append(
            jnp.where(row < 4, first, second)
            + pltpu.roll(jnp.where(row < 4, second, first), 4, 0)
        )
    pairs = []
    for i in range(2):
        first, second = level[i], level[i + 2]
        first = first + pltpu.roll(first, 6, 0)
        second = second + pltpu.roll(second, 2, 0)
        pairs.append(jnp.where((row & 2) == 0, first, second))
    first = pairs[0] + pltpu.roll(pairs[0], 7, 0)
    second = pairs[1] + pltpu.roll(pairs[1], 1, 0)
    return jnp.where((row & 1) == 0, first, second)


def blur_rows(ref, start, count):
    total = window[5] * ref[:, pl.ds(start + 5, count), :]
    for offset in range(5):
        total = total + window[offset] * (
            ref[:, pl.ds(start + offset, count), :]
            + ref[:, pl.ds(start + 10 - offset, count), :]
        )
    return total


def blur_columns(planes, band):
    count, rows, _ = planes.shape
    flat = planes.reshape(count * rows, lanes)
    out = jnp.dot(flat, band, preferred_element_type=f32, precision=lax.Precision.HIGHEST)
    return out.reshape(count, rows, lanes)


def step_kernel(
    attr_hbm,
    cam_hbm,
    ids_hbm,
    order_hbm,
    target_hbm,
    image_ref,
    grad_ref,
    attr_ref,
    cam_ref,
    ids_ref,
    order_ref,
    target_ref,
    cam_row,
    cam_all,
    req_out,
    req_in,
    ids_out,
    ids_own,
    table_own,
    table_in,
    ans_out,
    ans_in,
    back_out,
    back_in,
    view_out,
    view_in,
    ext_x,
    ext_y,
    attr_rows,
    stack,
    wide,
    alpha_s,
    weight_s,
    gains,
    sums,
    choosers,
    spots,
    in_chunk,
    back_stack,
    planes_y,
    planes_x,
    partials,
    load_sems,
    send_sems,
    recv_sems,
):
    me = lax.axis_index("gauss")
    view = lax.axis_index("cam")
    loads = [
        pltpu.make_async_copy(source, into, load_sems.at[item])
        for item, (source, into) in enumerate(
            (
                (ids_hbm, ids_ref),
                (order_hbm, order_ref),
                (target_hbm, target_ref),
                (cam_hbm, cam_ref),
                (attr_hbm, attr_ref),
            )
        )
    ]
    my_z = lax.div(me, 8)
    my_y = lax.rem(me, 8)
    my_x = lax.div(view, 2)
    my_core = lax.rem(view, 2)
    along_y = [lax.rem(my_y + step, 8) for step in (4, 3, 5, 2, 6, 1, 7)]
    along_x = [lax.rem(my_x + step, 4) * 2 for step in (2, 1, 3)]

    def each_peer(visit):
        def ring(step, carry):
            from_z = 4 + (1 - 2 * lax.rem(step, 2)) * lax.div(step + 1, 2)
            first = lax.rem(my_z + from_z, 8) * 8
            for place in along_y:
                visit(first + place)
            visit(first + my_y)
            return carry

        lax.fori_loop(0, 7, ring, 0)
        for place in along_y:
            visit(my_z * 8 + place)

    hub = my_z < 4
    partner = (7 - my_z) * 8 + my_y

    def each_hub(visit):
        def ring(step, carry):
            for place in along_y:
                visit(step * 8 + place)

            @pl.when(step != my_z)
            def _():
                visit(step * 8 + my_y)

            return carry

        lax.fori_loop(0, 4, ring, 0)

    def each_view(visit):
        for place in along_x:
            visit(place + my_core)
            visit(place + 1 - my_core)
        visit(my_x * 2 + 1 - my_core)

    below = lax.rem(me + 1, peers)
    above = lax.rem(me + peers - 1, peers)
    next_view = lax.rem(view + 1, views)

    barrier = pltpu.get_barrier_semaphore()

    def greet_peer(other):
        pl.semaphore_signal(barrier, inc=1, device_id={"gauss": other}, device_id_type=MESH)

    def greet_view(other):
        pl.semaphore_signal(barrier, inc=1, device_id={"cam": other}, device_id_type=MESH)

    @pl.when(hub)
    def _():
        each_peer(greet_peer)

    each_view(greet_view)
    for load in loads:
        load.start()

    def remote(src, dst, phase, where):
        return pltpu.make_async_remote_copy(
            src_ref=src,
            dst_ref=dst,
            send_sem=send_sems.at[phase],
            recv_sem=recv_sems.at[phase],
            device_id=where,
            device_id_type=MESH,
        )

    def exchange(out, into, phase, axis):
        own = me if axis == "gauss" else view

        def send(other):
            remote(out.at[other], into.at[own], phase, {axis: other}).start()

        if axis == "gauss":
            each_peer(send)
        else:
            each_view(send)
        into[pl.ds(own, 1)] = out[pl.ds(own, 1)]

    def bulk(out, into, phase, axis):
        count = peers if axis == "gauss" else views
        return remote(
            out.at[pl.ds(0, count - 1)],
            into.at[pl.ds(0, count - 1)],
            phase,
            {axis: below if axis == "gauss" else next_view},
        )

    loads[0].wait()
    loads[1].wait()
    ids = lane_pick(ids_ref[...], order_ref[...])
    present = ids >= 0
    owner = ids >> 10
    local_id = ids & 1023
    chunk_id = (local_id >> 7).astype(f32)
    lane_id = (local_id & 127).astype(f32)
    owner_row = iota((peers, slots), 0)
    before = (iota((slots, slots), 0) < iota((slots, slots), 1)).astype(jnp.bfloat16)
    rank_rows = iota((capacity, slots), 0)
    slot_row = iota((1, slots), 1).astype(f32)
    base = jnp.zeros((peers, 1), f32)
    asked = jnp.zeros((peers, lanes), f32)
    ranks = []
    for tile in range(tiles):
        named = owner_row == owner[tile : tile + 1]
        member = jnp.where(named, 1.0, 0.0)
        earlier = jnp.dot(member.astype(jnp.bfloat16), before, preferred_element_type=f32)
        rank = jnp.sum(member * (earlier + base), axis=0, keepdims=True)
        base = base + jnp.sum(member, axis=1, keepdims=True)
        ranks.append(rank)
        hit = rank_rows == rank.astype(jnp.int32)
        terms = [
            jnp.where(hit, chunk_id[tile : tile + 1], 0.0),
            jnp.where(hit, lane_id[tile : tile + 1], 0.0),
            jnp.where(hit, 1.0, 0.0),
            jnp.where(hit, float(tile), 0.0),
            jnp.where(hit, slot_row, 0.0),
            jnp.zeros((lanes - 5 * capacity, slots), f32),
        ]
        asked = asked + dot_nt(
            member.astype(jnp.bfloat16), jnp.concatenate(terms, axis=0).astype(jnp.bfloat16)
        )
    rank = jnp.concatenate(ranks, axis=0).astype(jnp.int32)
    req_out[:, 0, :] = asked[0:32]
    req_out[:, 1, :] = jnp.concatenate([asked[first : first + 8] for first in (56, 48, 40, 32)])
    loads[2].wait()
    loads[3].wait()
    cam_row[...] = jnp.zeros((1, lanes), f32)
    cam_row[:, 0:8] = cam_ref[...]
    cam_all[pl.ds(view, 1)] = cam_row[...].reshape(1, 1, lanes)
    ext_y[:, 16:32, :] = target_ref[0]

    pl.semaphore_wait(barrier, hubs + views - 1 - jnp.where(hub, 1, 0))

    each_hub(
        lambda other: remote(req_out.at[other], req_in.at[me], 0, {"gauss": other}).start()
    )
    target_down = remote(ext_y.at[:, 16:32, :], ext_y.at[:, 0:16, :], 1, {"gauss": below})
    target_up = remote(ext_y.at[:, 16:32, :], ext_y.at[:, 32:48, :], 2, {"gauss": above})

    each_view(lambda other: remote(cam_row, cam_all.at[view], 3, {"cam": other}).start())

    loads[4].wait()
    for chunk in range(8):
        attr_rows[:, chunk, :] = attr_ref[:, chunk * lanes : (chunk + 1) * lanes]
    camera = [
        jnp.broadcast_to(cam_row[0:1, column : column + 1], (8, lanes)) for column in range(8)
    ]
    rows = [attr_rows[row] for row in range(59)]
    flat_features = project(rows, camera_terms(camera))
    opacity = 1.0 / (1.0 + jnp.exp(-rows[10]))
    table = flat_features[0:5] + [opacity] + flat_features[5:8]
    for feature in range(9):
        table_own[feature] = table[feature]
    push = remote(table_own, table_in, 9, {"gauss": partner})
    name = remote(ids_out, ids_own, 10, {"gauss": partner})

    @pl.when(jnp.logical_not(hub))
    def _():
        push.start()

    def by_rank(values):
        return jnp.concatenate([values, pltpu.roll(values, lanes - 8, 1)], axis=0).T

    some = {"gauss": below}

    def hub_step():
        req_in[pl.ds(me, 1)] = req_out[pl.ds(me, 1)]
        remote(req_in.at[pl.ds(0, 63)], req_in.at[pl.ds(0, 63)], 0, some).wait_recv()
        stack[...] = jnp.zeros((lanes, lanes), f32)
        for block, features_ref in enumerate((table_own, table_in)):
            asked_here = by_rank(req_in[:, block, :])
            asked_chunk = asked_here[0:8].astype(jnp.int32)
            asked_lane = asked_here[16:24].astype(jnp.int32)
            at_chunk = [asked_chunk == chunk for chunk in range(8)]
            if block == 1:
                push.wait_recv()
            for feature in range(9):
                picked = jnp.zeros((8, lanes), f32)
                for chunk in range(8):
                    row = jnp.broadcast_to(features_ref[feature, chunk : chunk + 1], (8, lanes))
                    picked = jnp.where(at_chunk[chunk], lane_pick(row, asked_lane), picked)
                stack[8 * feature : 8 * feature + 8] = picked
            turned = stack[...].T
            ans_out[:, 2 * block, :] = turned[0:peers]
            ans_out[:, 2 * block + 1, :] = turned[peers:]
        each_peer(
            lambda other: remote(ans_out.at[other], ans_in.at[me], 4, {"gauss": other}).start()
        )
        ans_in[pl.ds(me, 1)] = ans_out[pl.ds(me, 1)]
        ids_out[...] = req_in[:, 1, :].reshape(peers, 1, lanes)
        name.start()
        ids_own[...] = req_in[:, 0, :].reshape(peers, 1, lanes)

    pl.when(hub)(hub_step)

    outer = iota((slots, lanes), 0)
    inner = iota((slots, lanes), 1)
    band = jnp.zeros((lanes, lanes), f32)
    for offset in range(11):
        band = jnp.where(inner - outer == offset - 5, window[offset], band)
    sent = by_rank(asked)
    sent_there = sent[32:40]
    sent_tile = sent[48:56].astype(jnp.int32)
    sent_slot = sent[64:72].astype(jnp.int32)

    @pl.when(hub)
    def _():
        remote(ans_in.at[pl.ds(0, hubs - 1)], ans_in.at[pl.ds(0, hubs - 1)], 4, some).wait_recv()

    @pl.when(jnp.logical_not(hub))
    def _():
        remote(ans_in, ans_in, 4, some).wait_recv()

    target_down.start()
    target_up.start()
    by_owner = []
    for row in range(2):
        by_owner.append(ans_in[:, row, :])
        partners = ans_in[:, 2 + row, :]
        by_owner += [partners[first : first + 8] for first in (24, 16, 8, 0)]
    answers = jnp.concatenate(by_owner, axis=0).T
    from_lane = jnp.where(present, (rank >> 3) * peers + owner, 0)
    from_row = jnp.where(present, rank & 7, 8)
    at_row = [from_row == row for row in range(8)]
    features = []
    stack[72:128] = jnp.zeros((56, lanes), f32)
    for feature in range(9):
        picked = jnp.zeros((8, lanes), f32)
        for row in range(8):
            source = jnp.broadcast_to(
                answers[8 * feature + row : 8 * feature + row + 1], (8, lanes)
            )
            picked = jnp.where(at_row[row], lane_pick(source, from_lane), picked)
        stack[8 * feature : 8 * feature + 8] = picked
        features.append(picked)
    by_slot = stack[...].T
    spread = [lane_pick(by_slot, 8 * feature + (inner >> 4)) for feature in range(9)]
    slot_u, slot_v, conic_a, conic_b, conic_c, slot_opacity = spread[0:6]
    off_u = inner.astype(f32) + 0.5 - slot_u
    wide[0] = -0.5 * conic_a * off_u * off_u
    wide[1] = -conic_b * off_u
    wide[2] = -0.5 * conic_c
    wide[3] = slot_v
    wide[4] = slot_opacity
    wide[5] = spread[6]
    wide[6] = spread[7]
    wide[7] = spread[8]
    pixel_row = (iota((tile_side, lanes), 0) + me * tile_side).astype(f32) + 0.5

    def render(step, carry):
        transmit, red, green, blue = carry
        for part in range(render_unroll):
            first = pl.multiple_of((step * render_unroll + part) * 8, 8)
            block = [wide[item, pl.ds(first, 8), :] for item in range(8)]
            for i in range(8):
                flat, slope, curve, mean_v, alpha_top, c_0, c_1, c_2 = [
                    item[i : i + 1] for item in block
                ]
                off_v = pixel_row - mean_v
                alpha = alpha_top * jnp.exp(flat + off_v * (slope + curve * off_v))
                weight = alpha * transmit
                transmit = transmit - weight
                red = red + weight * c_0
                green = green + weight * c_1
                blue = blue + weight * c_2
                alpha_s[first + i] = alpha
                weight_s[first + i] = weight
        return transmit, red, green, blue

    zero = jnp.zeros((tile_side, lanes), f32)
    _, red, green, blue = lax.fori_loop(0, slots // 8 // render_unroll, render, (zero + 1.0, zero, zero, zero))
    image = jnp.stack([red, green, blue])
    ext_x[:, 16:32, :] = image
    image_down = remote(ext_x.at[:, 16:32, :], ext_x.at[:, 0:16, :], 5, {"gauss": below})
    image_up = remote(ext_x.at[:, 16:32, :], ext_x.at[:, 32:48, :], 6, {"gauss": above})
    image_down.start()
    image_up.start()
    image_ref[0] = image

    def look_behind(step, carry):
        behind = list(carry)
        for part in range(behind_unroll):
            first = pl.multiple_of((slots // 8 - 1 - step * behind_unroll - part) * 8, 8)
            block = [wide[item, pl.ds(first, 8), :] for item in (5, 6, 7)]
            for i in reversed(range(8)):
                alpha = alpha_s[first + i]
                weight = weight_s[first + i]
                for channel in range(3):
                    gain = block[channel][i : i + 1] - behind[channel]
                    behind[channel] = behind[channel] + alpha * gain
                    gains[channel, first + i] = weight * gain
        return tuple(behind)

    lax.fori_loop(0, slots // 8 // behind_unroll, look_behind, (zero, zero, zero))
    target_down.wait_recv()
    target_up.wait_recv()
    ext_y[:, 0:16, :] = ext_y[:, 0:16, :] * jnp.where(me > 0, 1.0, 0.0)
    ext_y[:, 32:48, :] = ext_y[:, 32:48, :] * jnp.where(me < peers - 1, 1.0, 0.0)
    photo = ext_y[...]
    planes_y[0:3] = photo
    planes_y[3:6] = photo * photo
    blurred_y = blur_columns(blur_rows(planes_y, 6, 32), band)
    mean_y = blurred_y[0:3]
    var_y = blurred_y[3:6] - mean_y * mean_y

    back_stack[...] = jnp.zeros((8, 16, lanes), f32)
    for item in range(9):
        choosers[item] = (inner == 8 * item + (outer >> 4)).astype(jnp.bfloat16)

    image_down.wait_recv()
    image_up.wait_recv()
    ext_x[:, 0:16, :] = ext_x[:, 0:16, :] * jnp.where(me > 0, 1.0, 0.0)
    ext_x[:, 32:48, :] = ext_x[:, 32:48, :] * jnp.where(me < peers - 1, 1.0, 0.0)

    shown = ext_x[...]
    planes_x[0:3] = shown
    planes_x[3:6] = shown * shown
    planes_x[6:9] = shown * photo
    blurred_x = blur_columns(blur_rows(planes_x, 6, 32), band)
    mean_x = blurred_x[0:3]
    var_x = blurred_x[3:6] - mean_x * mean_x
    cov_xy = blurred_x[6:9] - mean_x * mean_y
    top_1 = 2.0 * mean_x * mean_y + 0.0001
    top_2 = 2.0 * cov_xy + 0.0009
    inv_1 = 1.0 / (mean_x * mean_x + mean_y * mean_y + 0.0001)
    inv_2 = 1.0 / (var_x + var_y + 0.0009)
    inv_both = inv_1 * inv_2
    ssim = top_1 * top_2 * inv_both
    map_row = iota((3, 32, lanes), 1) + (me * tile_side - 5)
    in_view = (map_row >= 0) & (map_row < peers * tile_side)
    share = jnp.where(in_view, -0.2 / 256.0, 0.0)
    d_cov = share * 2.0 * top_1 * inv_both
    d_var = -share * ssim * inv_2
    d_mean = (
        share * (2.0 * mean_y * top_2 * inv_both - 2.0 * mean_x * ssim * inv_1)
        - 2.0 * mean_x * d_var
        - mean_y * d_cov
    )
    partials[0:3] = d_mean
    partials[3:6] = d_var
    partials[6:9] = d_cov
    pulled = blur_columns(blur_rows(partials, 0, 16), band)
    own_photo = target_ref[0]
    gap = image - own_photo
    loss_grad = (
        pulled[0:3]
        + 2.0 * image * pulled[3:6]
        + own_photo * pulled[6:9]
        + (0.8 / 256.0) * gap / jnp.sqrt(gap * gap + 0.0025)
    )
    grad_0, grad_1, grad_2 = loss_grad[0], loss_grad[1], loss_grad[2]

    half = tile_side // 2
    row_at = iota((half, lanes), 0).astype(f32) + (0.5 - half)
    row_high = row_at + half
    row_at_2 = row_at * row_at
    row_high_2 = row_high * row_high
    grads_low = [grad_0[:half], grad_1[:half], grad_2[:half]]
    grads_high = [grad_0[half:], grad_1[half:], grad_2[half:]]

    def render_back(step, carry):
        for part in range(back_unroll):
            first = pl.multiple_of((step * back_unroll + part) * 8, 8)
            kept = [[None] * 8 for _ in range(6)]
            for i in range(8):
                weight = weight_s[first + i]
                low, high = 0.0, 0.0
                for channel in range(3):
                    gain = gains[channel, first + i]
                    low = low + gain[:half] * grads_low[channel]
                    high = high + gain[half:] * grads_high[channel]
                    kept[3 + channel][i] = (
                        weight[:half] * grads_low[channel] + weight[half:] * grads_high[channel]
                    )
                kept[0][i] = low + high
                kept[1][i] = low * row_at + high * row_high
                kept[2][i] = low * row_at_2 + high * row_high_2
            for item in range(6):
                sums[item, pl.ds(first, 8), :] = row_sums(kept[item])
        return carry

    lax.fori_loop(0, slots // 8 // back_unroll, render_back, 0)

    to_centre = (me * tile_side + half).astype(f32) - wide[3]
    sum_0 = sums[0]
    sum_1 = sums[1] + to_centre * sum_0
    sum_2 = sums[2] + to_centre * (sums[1] + sum_1)
    sum_0u = sum_0 * off_u
    quantities = [
        sum_0, sum_0u, sum_0u * off_u, sum_1, sum_1 * off_u, sum_2, sums[3], sums[4], sums[5]
    ]
    gathered = jnp.zeros((slots, lanes), f32)
    for item in range(9):
        for part in halves(quantities[item]):
            gathered = gathered + jnp.dot(part, choosers[item], preferred_element_type=f32)
    per_tile = gathered.T
    m_0, m_u, m_uu, m_v, m_uv, m_vv = [per_tile[8 * item : 8 * item + 8] for item in range(6)]
    slot_grads = [
        features[2] * m_u + features[3] * m_v,
        features[4] * m_v + features[3] * m_u,
        -0.5 * m_uu,
        -m_uv,
        -0.5 * m_vv,
        m_0,
        per_tile[48:56],
        per_tile[56:64],
        per_tile[64:72],
    ]

    at_tile = [(sent_tile == tile) & (sent_there > 0.5) for tile in range(tiles)]
    for feature in range(9):
        picked = jnp.zeros((8, lanes), f32)
        for tile in range(tiles):
            row = jnp.broadcast_to(slot_grads[feature][tile : tile + 1], (8, lanes))
            picked = jnp.where(at_tile[tile], lane_pick(row, sent_slot), picked)
        back_stack[:, feature, :] = picked
    turned = back_stack[...].reshape(lanes, lanes).T
    back_out[:, 0, :] = turned[0:peers]
    back_out[:, 1, :] = turned[peers:]
    exchange(back_out, back_in, 7, "gauss")

    @pl.when(jnp.logical_not(hub))
    def _():
        name.wait_recv()

    wanted = by_rank(ids_own[...].reshape(peers, lanes))
    want_chunk = wanted[0:8].astype(jnp.int32)
    want_lane = wanted[16:24].astype(jnp.int32)
    want_there = wanted[32:40]
    for row in range(8):
        spots[:, row * lanes : (row + 1) * lanes] = (
            outer == want_lane[row : row + 1]
        ).astype(jnp.bfloat16)
        for chunk in range(8):
            here = (want_chunk[row : row + 1] == chunk) & (want_there[row : row + 1] > 0.5)
            in_chunk[row, chunk] = jnp.broadcast_to(jnp.where(here, 1.0, 0.0), (16, lanes)).astype(
                jnp.bfloat16
            )
    bulk(back_out, back_in, 7, "gauss").wait_recv()
    returned = jnp.concatenate([back_in[:, 0, :], back_in[:, 1, :]], axis=0).T
    pieces = [[], []]
    for row in range(8):
        for part, split in enumerate(halves(returned[16 * row : 16 * row + 16])):
            pieces[part].append(
                jnp.concatenate([split * in_chunk[row, chunk] for chunk in range(8)], axis=0)
            )
    block_grad = sum(dot_nt(jnp.concatenate(piece, axis=1), spots[...]) for piece in pieces)
    view_out[...] = block_grad.reshape(views, 16, lanes)
    exchange(view_out, view_in, 8, "cam")

    bulk(cam_all, cam_all, 3, "cam").wait_recv()
    every = cam_all[...].reshape(views, lanes)
    cameras = camera_terms(
        [jnp.broadcast_to(every[:, column : column + 1], (views, lanes)) for column in range(8)]
    )
    own = attr_ref[:, pl.ds(pl.multiple_of(view * lanes, lanes), lanes)]
    own_rows = [own[row : row + 1] for row in range(59)]
    wide_rows = [jnp.broadcast_to(row, (views, lanes)) for row in own_rows]
    _, pull = jax.vjp(lambda values: project(values, cameras), wide_rows)
    @pl.when(hub)
    def _():
        remote(req_out.at[pl.ds(0, 31)], req_out.at[pl.ds(0, 31)], 0, some).wait_send()
        remote(ans_out.at[pl.ds(0, 63)], ans_out.at[pl.ds(0, 63)], 4, some).wait_send()
        name.wait_send()

    @pl.when(jnp.logical_not(hub))
    def _():
        remote(req_out, req_out, 0, some).wait_send()
        push.wait_send()

    bulk(back_out, back_in, 7, "gauss").wait_send()
    bulk(cam_all, cam_all, 3, "cam").wait_send()
    target_down.wait_send()
    target_up.wait_send()
    image_down.wait_send()
    image_up.wait_send()
    bulk(view_out, view_in, 8, "cam").wait_recv()
    cots = [view_in[:, item, :] for item in range(9)]
    (row_grads,) = pull(cots[0:5] + cots[6:9])
    own_opacity = 1.0 / (1.0 + jnp.exp(-wide_rows[10]))
    row_grads[10] = cots[5] * (1.0 - own_opacity)
    row_grads = row_grads + [jnp.zeros((views, lanes), f32)] * 5
    for first in range(0, 64, 8):
        count = min(8, 59 - first)
        grad_ref[first : first + count, :] = row_sums(row_grads[first : first + 8])[:count]
    bulk(view_out, view_in, 8, "cam").wait_send()


def store_kernel(image_ref, grad_ref, image_out, grad_out, sems):
    store_image = pltpu.make_async_copy(image_ref, image_out, sems.at[0])
    store_grads = pltpu.make_async_copy(grad_ref, grad_out, sems.at[1])
    store_image.start()
    store_grads.start()
    store_image.wait()
    store_grads.wait()


def local(attributes, cameras, tile_ids, depth_order, target):
    vmem = pl.BlockSpec(memory_space=pltpu.VMEM)
    scratch = [
        (1, lanes),
        (views, 1, lanes),
        (hubs, 2, lanes),
        (peers, 2, lanes),
        (peers, 1, lanes),
        (peers, 1, lanes),
        (9, 8, lanes),
        (9, 8, lanes),
        (peers, 4, lanes),
        (hubs, 4, lanes),
        (peers, 2, lanes),
        (peers, 2, lanes),
        (views, 16, lanes),
        (views, 16, lanes),
        (3, 48, lanes),
        (3, 48, lanes),
        (59, 8, lanes),
        (lanes, lanes),
        (8, slots, lanes),
        (slots, tile_side, lanes),
        (slots, tile_side, lanes),
        (3, slots, tile_side, lanes),
        (6, slots, lanes),
        (9, slots, lanes, jnp.bfloat16),
        (lanes, 8 * lanes, jnp.bfloat16),
        (8, 8, 16, lanes, jnp.bfloat16),
        (8, 16, lanes),
        (6, 48, lanes),
        (9, 48, lanes),
        (9, 32, lanes),
    ]
    operands = (
        attributes,
        cameras,
        tile_ids.reshape(tiles, slots),
        depth_order.reshape(tiles, slots),
        target,
    )
    image, grads = pl.pallas_call(
        step_kernel,
        out_shape=(
            pltpu.VMEM((1, 3, tile_side, lanes), f32),
            pltpu.VMEM((59, lanes), f32),
        ),
        in_specs=[pl.BlockSpec(memory_space=pltpu.HBM)] * 5,
        out_specs=(vmem, vmem),
        scratch_shapes=[
            pltpu.VMEM((59, 8 * lanes), f32),
            pltpu.VMEM((1, 8), f32),
            pltpu.VMEM((tiles, slots), jnp.int32),
            pltpu.VMEM((tiles, slots), jnp.int32),
            pltpu.VMEM((1, 3, tile_side, lanes), f32),
        ]
        + [
            pltpu.VMEM(shape, f32)
            if isinstance(shape[-1], int)
            else pltpu.VMEM(shape[:-1], shape[-1])
            for shape in scratch
        ]
        + [
            pltpu.SemaphoreType.DMA((5,)),
            pltpu.SemaphoreType.DMA((11,)),
            pltpu.SemaphoreType.DMA((11,)),
        ],
        compiler_params=pltpu.CompilerParams(
            collective_id=0, has_side_effects=True, vmem_limit_bytes=40 * 1024 * 1024
        ),
    )(*[pltpu.with_memory_space_constraint(operand, pltpu.HBM) for operand in operands])
    hbm = pl.BlockSpec(memory_space=pltpu.HBM)
    return pl.pallas_call(
        store_kernel,
        out_shape=(
            jax.ShapeDtypeStruct((1, 3, tile_side, lanes), f32),
            jax.ShapeDtypeStruct((59, lanes), f32),
        ),
        in_specs=[vmem, vmem],
        out_specs=(hbm, hbm),
        scratch_shapes=[pltpu.SemaphoreType.DMA((2,))],
    )(
        pltpu.with_memory_space_constraint(image, pltpu.VMEM),
        pltpu.with_memory_space_constraint(grads, pltpu.VMEM),
    )


def solution(mesh):
    return jax.shard_map(
        local,
        mesh=mesh,
        in_specs=(
            P(None, "gauss"),
            P("cam", None),
            P("cam", "gauss", None, None),
            P("cam", "gauss", None, None),
            P("cam", None, "gauss", None),
        ),
        out_specs=(P("cam", None, "gauss", None), P(None, ("gauss", "cam"))),
        check_vma=False,
    )
```

```python
import math

import jax
import jax.numpy as jnp
from jax import lax
from jax.experimental import pallas as pl
from jax.experimental.pallas import tpu as pltpu
from jax.sharding import PartitionSpec as P

MESH = pl.DeviceIdType.MESH
peers = 64
views = 8
tile_side = 16
tiles = 8
slots = 128
lanes = 128
capacity = 16
render_unroll = 16
behind_unroll = 2
back_unroll = 16
image_width = 128.0
image_height = 1024.0
f32 = jnp.float32
window_raw = [math.exp(-((offset - 5) ** 2) / 4.5) for offset in range(11)]
window = [weight / sum(window_raw) for weight in window_raw]
sh_consts = [
    0.0,
    -0.4886025119029199,
    0.4886025119029199,
    -0.4886025119029199,
    1.0925484305920792,
    -1.0925484305920792,
    0.31539156525252005,
    -1.0925484305920792,
    0.5462742152960396,
    -0.5900435899266435,
    2.890611442640554,
    -0.4570457994644658,
    0.3731763325901154,
    -0.4570457994644658,
    1.445305721320277,
    -0.5900435899266435,
]


def unit_quat(parts):
    length_q = jnp.sqrt(
        parts[0] * parts[0] + parts[1] * parts[1] + parts[2] * parts[2] + parts[3] * parts[3]
    )
    return [part / length_q for part in parts]


def quat_matrix(quaternion):
    q_w, q_x, q_y, q_z = quaternion
    return [
        [
            1.0 - 2.0 * (q_y * q_y + q_z * q_z),
            2.0 * (q_x * q_y - q_w * q_z),
            2.0 * (q_x * q_z + q_w * q_y),
        ],
        [
            2.0 * (q_x * q_y + q_w * q_z),
            1.0 - 2.0 * (q_x * q_x + q_z * q_z),
            2.0 * (q_y * q_z - q_w * q_x),
        ],
        [
            2.0 * (q_x * q_z - q_w * q_y),
            2.0 * (q_y * q_z + q_w * q_x),
            1.0 - 2.0 * (q_x * q_x + q_y * q_y),
        ],
    ]


def camera_terms(camera):
    cam_rot = quat_matrix(unit_quat(camera[0:4]))
    shift_vec = camera[4:7]
    centre = [
        -(
            cam_rot[0][axis_col] * shift_vec[0]
            + cam_rot[1][axis_col] * shift_vec[1]
            + cam_rot[2][axis_col] * shift_vec[2]
        )
        for axis_col in range(3)
    ]
    return cam_rot, shift_vec, camera[7] * image_width, camera[7] * image_height, centre


def project(attr_rows, camera):
    cam_rot, shift_vec, horizontal_focal, focal_y, centre = camera
    position = [attr_rows[0], attr_rows[1], attr_rows[2]]
    view_pos = [
        cam_rot[axis_row][0] * position[0]
        + cam_rot[axis_row][1] * position[1]
        + cam_rot[axis_row][2] * position[2]
        + shift_vec[axis_row]
        for axis_row in range(3)
    ]
    inv_z = 1.0 / view_pos[2]
    focal_u = horizontal_focal * inv_z
    focal_v = focal_y * inv_z
    slope_u = focal_u * view_pos[0]
    slope_v = focal_v * view_pos[1]
    mean_u = 0.5 * image_width + slope_u
    mean_v = 0.5 * image_height + slope_v
    gauss_rot = quat_matrix(unit_quat([attr_rows[6], attr_rows[7], attr_rows[8], attr_rows[9]]))
    scales = [jnp.exp(attr_rows[3]), jnp.exp(attr_rows[4]), jnp.exp(attr_rows[5])]
    skew_u = slope_u * inv_z
    skew_v = slope_v * inv_z
    project_mat = [
        [focal_u * cam_rot[0][axis_col] - skew_u * cam_rot[2][axis_col] for axis_col in range(3)],
        [focal_v * cam_rot[1][axis_col] - skew_v * cam_rot[2][axis_col] for axis_col in range(3)],
    ]
    spread = [
        [
            (
                project_mat[axis_row][0] * gauss_rot[0][axis_col]
                + project_mat[axis_row][1] * gauss_rot[1][axis_col]
                + project_mat[axis_row][2] * gauss_rot[2][axis_col]
            )
            * scales[axis_col]
            for axis_col in range(3)
        ]
        for axis_row in range(2)
    ]
    cov_a = spread[0][0] * spread[0][0] + spread[0][1] * spread[0][1] + spread[0][2] * spread[0][2] + 0.3
    cov_b = spread[0][0] * spread[1][0] + spread[0][1] * spread[1][1] + spread[0][2] * spread[1][2]
    cov_c = spread[1][0] * spread[1][0] + spread[1][1] * spread[1][1] + spread[1][2] * spread[1][2] + 0.3
    inv_det = 1.0 / (cov_a * cov_c - cov_b * cov_b)
    offsets = [position[axis_col] - centre[axis_col] for axis_col in range(3)]
    distance = jnp.sqrt(offsets[0] * offsets[0] + offsets[1] * offsets[1] + offsets[2] * offsets[2])
    inv_distance = 1.0 / distance
    dir_x, dir_y, dir_z = [offset * inv_distance for offset in offsets]
    sq_x, sq_y, sq_z = (dir_x * dir_x, dir_y * dir_y, dir_z * dir_z)
    sh_basis = [
        None,
        dir_y,
        dir_z,
        dir_x,
        dir_x * dir_y,
        dir_y * dir_z,
        2.0 * sq_z - sq_x - sq_y,
        dir_x * dir_z,
        sq_x - sq_y,
        dir_y * (3.0 * sq_x - sq_y),
        dir_x * dir_y * dir_z,
        dir_y * (4.0 * sq_z - sq_x - sq_y),
        dir_z * (2.0 * sq_z - 3.0 * sq_x - 3.0 * sq_y),
        dir_x * (4.0 * sq_z - sq_x - sq_y),
        dir_z * (sq_x - sq_y),
        dir_x * (sq_x - 3.0 * sq_y),
    ]
    scaled = [None] + [sh_consts[degree] * sh_basis[degree] for degree in range(1, 16)]
    colours = []
    for channel in range(3):
        colour = 0.5 + 0.28209479177387814 * attr_rows[11 + channel]
        for degree in range(1, 16):
            colour = colour + scaled[degree] * attr_rows[11 + 3 * degree + channel]
        colours.append(colour)
    return [mean_u, mean_v, cov_c * inv_det, -cov_b * inv_det, cov_a * inv_det] + colours


def iota(shape, dim):
    return lax.broadcasted_iota(jnp.int32, shape, dim)


def lane_pick(values, index):
    return jnp.take_along_axis(values, index, axis=1, mode="promise_in_bounds")


def halves(values):
    high = values.astype(jnp.bfloat16)
    low = (values - high.astype(f32)).astype(jnp.bfloat16)
    return high, low


def dot_nt(left, right):
    return lax.dot_general(left, right, (((1,), (1,)), ((), ())), preferred_element_type=f32)


def row_sums(blocks):
    row = iota((8, lanes), 0)
    level = []
    for i in range(4):
        first, second = blocks[i], blocks[i + 4]
        level.append(
            jnp.where(row < 4, first, second)
            + pltpu.roll(jnp.where(row < 4, second, first), 4, 0)
        )
    pairs = []
    for i in range(2):
        first, second = level[i], level[i + 2]
        first = first + pltpu.roll(first, 6, 0)
        second = second + pltpu.roll(second, 2, 0)
        pairs.append(jnp.where((row & 2) == 0, first, second))
    first = pairs[0] + pltpu.roll(pairs[0], 7, 0)
    second = pairs[1] + pltpu.roll(pairs[1], 1, 0)
    return jnp.where((row & 1) == 0, first, second)


def blur_rows(ref, start, count):
    total = window[5] * ref[:, pl.ds(start + 5, count), :]
    for offset in range(5):
        total = total + window[offset] * (
            ref[:, pl.ds(start + offset, count), :]
            + ref[:, pl.ds(start + 10 - offset, count), :]
        )
    return total


def blur_columns(planes, band):
    count, rows, _ = planes.shape
    flat = planes.reshape(count * rows, lanes)
    out = jnp.dot(flat, band, preferred_element_type=f32, precision=lax.Precision.HIGHEST)
    return out.reshape(count, rows, lanes)


def step_kernel(
    attr_hbm,
    cam_hbm,
    ids_hbm,
    order_hbm,
    target_hbm,
    image_ref,
    grad_ref,
    attr_ref,
    cam_ref,
    ids_ref,
    order_ref,
    target_ref,
    cam_row,
    cam_all,
    req_out,
    req_in,
    ids_out,
    ids_own,
    asked_rows,
    table_in,
    table_rows,
    ans_out,
    ans_in,
    back_out,
    back_in,
    view_out,
    view_in,
    ext_x,
    ext_y,
    attr_rows,
    stack,
    wide,
    alpha_s,
    weight_s,
    gains,
    sums,
    choosers,
    spots,
    in_chunk,
    back_stack,
    planes_y,
    planes_x,
    partials,
    load_sems,
    send_sems,
    recv_sems,
):
    me = lax.axis_index("gauss")
    view = lax.axis_index("cam")
    loads = [
        pltpu.make_async_copy(source, into, load_sems.at[item])
        for item, (source, into) in enumerate(
            (
                (ids_hbm, ids_ref),
                (order_hbm, order_ref),
                (target_hbm, target_ref),
                (cam_hbm, cam_ref),
                (attr_hbm, attr_ref),
            )
        )
    ]
    my_z = lax.div(me, 8)
    my_y = lax.rem(me, 8)
    my_x = lax.div(view, 2)
    my_core = lax.rem(view, 2)
    along_y = [lax.rem(my_y + step, 8) for step in (4, 3, 5, 2, 6, 1, 7)]
    along_x = [lax.rem(my_x + step, 4) * 2 for step in (2, 1, 3)]

    def each_peer(visit):
        def ring(step, carry):
            from_z = 4 + (1 - 2 * lax.rem(step, 2)) * lax.div(step + 1, 2)
            first = lax.rem(my_z + from_z, 8) * 8
            for place in along_y:
                visit(first + place)
            visit(first + my_y)
            return carry

        lax.fori_loop(0, 7, ring, 0)
        for place in along_y:
            visit(my_z * 8 + place)

    hub = my_z < 4
    near = [lax.rem(my_y + step, 8) for step in (7, 0, 1, 2)]
    clients = [lax.rem(my_y + step, 8) for step in (1, 0, 7, 6)]
    far_y = lax.rem(my_y + 4, 8)
    low_z = jnp.where(hub, my_z, 7 - my_z)

    def each_hub(visit):
        def ring(step, carry):
            for place in (3, 0, 2):
                visit(step * 8 + near[place], step * 4 + place)

            @pl.when(step != my_z)
            def _():
                visit(step * 8 + my_y, step * 4 + 1)

            return carry

        lax.fori_loop(0, 4, ring, 0)

    def each_client(visit):
        def ring(step, carry):
            from_z = 4 + (1 - 2 * lax.rem(step, 2)) * lax.div(step + 1, 2)
            its_z = lax.rem(my_z + from_z, 8)
            for place in (3, 0, 2, 1):
                visit(its_z * 8 + clients[place], its_z * 4 + place)
            return carry

        lax.fori_loop(0, 7, ring, 0)
        for place in (3, 0, 2):
            visit(my_z * 8 + clients[place], my_z * 4 + place)

    def seen_from(other):
        turn = lax.rem(lax.rem(other, 8) - my_y + 9, 8)
        return lax.div(turn, 4) * 32 + my_z * 4 + lax.rem(turn, 4)

    def each_view(visit):
        for place in along_x:
            visit(place + my_core)
            visit(place + 1 - my_core)
        visit(my_x * 2 + 1 - my_core)

    below = lax.rem(me + 1, peers)
    above = lax.rem(me + peers - 1, peers)
    next_view = lax.rem(view + 1, views)

    barrier = pltpu.get_barrier_semaphore()

    def greet_peer(other):
        pl.semaphore_signal(barrier, inc=1, device_id={"gauss": other}, device_id_type=MESH)

    def greet_view(other):
        pl.semaphore_signal(barrier, inc=1, device_id={"cam": other}, device_id_type=MESH)

    @pl.when(hub)
    def _():
        greet_peer((7 - my_z) * 8 + far_y)
        greet_peer(my_z * 8 + far_y)
        each_client(lambda other, place: greet_peer(other))

    each_view(greet_view)
    for load in (loads[0], loads[1], loads[3], loads[4], loads[2]):
        load.start()

    def remote(src, dst, phase, where):
        return pltpu.make_async_remote_copy(
            src_ref=src,
            dst_ref=dst,
            send_sem=send_sems.at[phase],
            recv_sem=recv_sems.at[phase],
            device_id=where,
            device_id_type=MESH,
        )

    def exchange(out, into, phase, axis):
        own = me if axis == "gauss" else view

        def send(other):
            place = seen_from(other) if axis == "gauss" else own
            remote(out.at[other], into.at[place], phase, {axis: other}).start()

        if axis == "gauss":
            each_peer(send)
        else:
            each_view(send)
        into[pl.ds(seen_from(me) if axis == "gauss" else own, 1)] = out[pl.ds(own, 1)]

    def bulk(out, into, phase, axis):
        count = peers if axis == "gauss" else views
        return remote(
            out.at[pl.ds(0, count - 1)],
            into.at[pl.ds(0, count - 1)],
            phase,
            {axis: below if axis == "gauss" else next_view},
        )

    loads[0].wait()
    loads[1].wait()
    ids = lane_pick(ids_ref[...], order_ref[...])
    present = ids >= 0
    owner = ids >> 10
    local_id = ids & 1023
    chunk_id = (local_id >> 7).astype(f32)
    lane_id = (local_id & 127).astype(f32)
    owner_row = iota((peers, slots), 0)
    before = (iota((slots, slots), 0) < iota((slots, slots), 1)).astype(jnp.bfloat16)
    rank_rows = iota((capacity, slots), 0)
    slot_row = iota((1, slots), 1).astype(f32)
    base = jnp.zeros((peers, 1), f32)
    asked = jnp.zeros((peers, lanes), f32)
    ranks = []
    for tile in range(tiles):
        named = owner_row == owner[tile : tile + 1]
        member = jnp.where(named, 1.0, 0.0)
        earlier = jnp.dot(member.astype(jnp.bfloat16), before, preferred_element_type=f32)
        rank = jnp.sum(member * (earlier + base), axis=0, keepdims=True)
        base = base + jnp.sum(member, axis=1, keepdims=True)
        ranks.append(rank)
        hit = rank_rows == rank.astype(jnp.int32)
        terms = [
            jnp.where(hit, chunk_id[tile : tile + 1], 0.0),
            jnp.where(hit, lane_id[tile : tile + 1], 0.0),
            jnp.where(hit, 1.0, 0.0),
            jnp.where(hit, float(tile), 0.0),
            jnp.where(hit, slot_row, 0.0),
            jnp.zeros((lanes - 5 * capacity, slots), f32),
        ]
        asked = asked + dot_nt(
            member.astype(jnp.bfloat16), jnp.concatenate(terms, axis=0).astype(jnp.bfloat16)
        )
    rank = jnp.concatenate(ranks, axis=0).astype(jnp.int32)
    asked_rows[...] = asked.reshape(peers, 1, lanes)
    for step in range(4):
        for place in range(4):
            across = lax.rem(near[place] + 4, 8)
            blocks = (
                step * 8 + near[place],
                step * 8 + across,
                (7 - step) * 8 + near[place],
                (7 - step) * 8 + across,
            )
            for item, block in enumerate(blocks):
                req_out[4 * step + place, item : item + 1] = asked_rows[block]
    loads[2].wait()
    loads[3].wait()
    cam_row[...] = jnp.zeros((1, lanes), f32)
    cam_row[:, 0:8] = cam_ref[...]
    cam_all[pl.ds(view, 1)] = cam_row[...].reshape(1, 1, lanes)
    ext_y[:, 16:32, :] = target_ref[0]

    loads[4].wait()
    for chunk in range(8):
        attr_rows[:, chunk, :] = attr_ref[:, chunk * lanes : (chunk + 1) * lanes]
    camera = [
        jnp.broadcast_to(cam_row[0:1, column : column + 1], (8, lanes)) for column in range(8)
    ]
    rows = [attr_rows[row] for row in range(59)]
    flat_features = project(rows, camera_terms(camera))
    opacity = 1.0 / (1.0 + jnp.exp(-rows[10]))
    table = flat_features[0:5] + [opacity] + flat_features[5:8]
    for feature in range(9):
        table_in[0, feature] = table[feature]
    pl.semaphore_wait(barrier, 17 + views - 1 - jnp.where(hub, 1, 0))

    each_hub(
        lambda other, place: remote(
            req_out.at[place], req_in.at[my_z * 4 + lax.rem(place, 4)], 0, {"gauss": other}
        ).start()
    )
    push_near = remote(table_in.at[0], table_in.at[2], 9, {"gauss": low_z * 8 + my_y})
    push_far = remote(table_in.at[0], table_in.at[3], 9, {"gauss": low_z * 8 + far_y})
    push_across = remote(table_in.at[0], table_in.at[1], 9, {"gauss": low_z * 8 + far_y})
    names = [
        remote(ids_out.at[item], ids_own.at[item % 2], 10, {"gauss": block})
        for item, block in (
            (1, low_z * 8 + far_y),
            (2, (7 - low_z) * 8 + my_y),
            (3, (7 - low_z) * 8 + far_y),
        )
    ]

    @pl.when(jnp.logical_not(hub))
    def _():
        push_near.start()
        push_far.start()

    @pl.when(hub)
    def _():
        push_across.start()

    target_down = remote(ext_y.at[:, 16:32, :], ext_y.at[:, 0:16, :], 1, {"gauss": below})
    target_up = remote(ext_y.at[:, 16:32, :], ext_y.at[:, 32:48, :], 2, {"gauss": above})

    each_view(lambda other: remote(cam_row, cam_all.at[view], 3, {"cam": other}).start())

    def by_rank(values):
        return jnp.concatenate([values, pltpu.roll(values, lanes - 8, 1)], axis=0).T

    some = {"gauss": below}

    def hub_step():
        own_place = my_z * 4 + 1
        req_in[pl.ds(own_place, 1)] = req_out[pl.ds(own_place, 1)]
        stack[...] = jnp.zeros((lanes, lanes), f32)
        remote(table_in.at[pl.ds(1, 3)], table_in.at[pl.ds(1, 3)], 9, some).wait_recv()
        upper = iota((8, lanes), 0) < 4
        for pair in range(2):
            for feature in range(9):
                for chunk in range(8):
                    table_rows[pair, feature, chunk] = jnp.where(
                        upper,
                        table_in[2 * pair, feature, chunk : chunk + 1],
                        table_in[2 * pair + 1, feature, chunk : chunk + 1],
                    )
        remote(req_in.at[pl.ds(0, 31)], req_in.at[pl.ds(0, 31)], 0, some).wait_recv()
        first_block = (iota((32, lanes), 1) & 4) == 0
        for pair in range(2):
            near_rows, far_rows = req_in[:, 2 * pair, :], req_in[:, 2 * pair + 1, :]
            asked_here = jnp.concatenate(
                [
                    jnp.where(
                        first_block,
                        pltpu.roll(near_rows, (lanes - 4 * part) % lanes, 1),
                        pltpu.roll(far_rows, (lanes + 4 - 4 * part) % lanes, 1),
                    )
                    for part in range(4)
                ],
                axis=0,
            ).T
            asked_chunk = asked_here[0:8].astype(jnp.int32)
            asked_lane = asked_here[16:24].astype(jnp.int32)
            at_chunk = [asked_chunk == chunk for chunk in range(8)]
            for feature in range(9):
                picked = jnp.zeros((8, lanes), f32)
                for chunk in range(8):
                    row = table_rows[pair, feature, chunk]
                    picked = jnp.where(at_chunk[chunk], lane_pick(row, asked_lane), picked)
                stack[8 * feature : 8 * feature + 8] = picked
            turned = stack[...].T
            for part in range(4):
                ans_out[:, 4 * pair + part, :] = turned[32 * part : 32 * part + 32]
        each_client(
            lambda other, place: remote(
                ans_out.at[place], ans_in.at[my_z * 4 + lax.rem(place, 4)], 4, {"gauss": other}
            ).start()
        )
        ans_in[pl.ds(own_place, 1)] = ans_out[pl.ds(own_place, 1)]
        for block in range(4):
            ids_out[block] = req_in[:, block, :].reshape(32, 1, lanes)
        for name in names:
            name.start()
        ids_own[0] = ids_out[0]

    pl.when(hub)(hub_step)

    outer = iota((slots, lanes), 0)
    inner = iota((slots, lanes), 1)
    band = jnp.zeros((lanes, lanes), f32)
    for offset in range(11):
        band = jnp.where(inner - outer == offset - 5, window[offset], band)
    sent = by_rank(asked)
    sent_there = sent[32:40]
    sent_tile = sent[48:56].astype(jnp.int32)
    sent_slot = sent[64:72].astype(jnp.int32)

    @pl.when(hub)
    def _():
        remote(ans_in.at[pl.ds(0, 15)], ans_in.at[pl.ds(0, 15)], 4, some).wait_recv()

    @pl.when(jnp.logical_not(hub))
    def _():
        remote(ans_in, ans_in, 4, some).wait_recv()

    target_down.start()
    target_up.start()
    by_owner = [ans_in[:, row, :] for row in range(8)]
    answers = jnp.concatenate(by_owner, axis=0).T
    owner_z, owner_y = owner >> 3, owner & 7
    turn = (owner_y - my_y + 9) & 7
    beyond = owner_z >= 4
    from_hub = jnp.where(beyond, 7 - owner_z, owner_z) * 4 + (turn & 3)
    from_lane = jnp.where(present, (jnp.where(beyond, 4, 0) + (rank >> 2)) * 16 + from_hub, 0)
    from_row = jnp.where(present, (turn >> 2) * 4 + (rank & 3), 8)
    at_row = [from_row == row for row in range(8)]
    features = []
    stack[72:128] = jnp.zeros((56, lanes), f32)
    for feature in range(9):
        picked = jnp.zeros((8, lanes), f32)
        for row in range(8):
            source = jnp.broadcast_to(
                answers[8 * feature + row : 8 * feature + row + 1], (8, lanes)
            )
            picked = jnp.where(at_row[row], lane_pick(source, from_lane), picked)
        stack[8 * feature : 8 * feature + 8] = picked
        features.append(picked)
    by_slot = stack[...].T
    spread = [lane_pick(by_slot, 8 * feature + (inner >> 4)) for feature in range(9)]
    slot_u, slot_v, conic_a, conic_b, conic_c, slot_opacity = spread[0:6]
    off_u = inner.astype(f32) + 0.5 - slot_u
    wide[0] = -0.5 * conic_a * off_u * off_u
    wide[1] = -conic_b * off_u
    wide[2] = -0.5 * conic_c
    wide[3] = slot_v
    wide[4] = slot_opacity
    wide[5] = spread[6]
    wide[6] = spread[7]
    wide[7] = spread[8]
    pixel_row = (iota((tile_side, lanes), 0) + me * tile_side).astype(f32) + 0.5

    def render(step, carry):
        transmit, red, green, blue = carry
        for part in range(render_unroll):
            first = pl.multiple_of((step * render_unroll + part) * 8, 8)
            block = [wide[item, pl.ds(first, 8), :] for item in range(8)]
            for i in range(8):
                flat, slope, curve, mean_v, alpha_top, c_0, c_1, c_2 = [
                    item[i : i + 1] for item in block
                ]
                off_v = pixel_row - mean_v
                alpha = alpha_top * jnp.exp(flat + off_v * (slope + curve * off_v))
                weight = alpha * transmit
                transmit = transmit - weight
                red = red + weight * c_0
                green = green + weight * c_1
                blue = blue + weight * c_2
                alpha_s[first + i] = alpha
                weight_s[first + i] = weight
        return transmit, red, green, blue

    zero = jnp.zeros((tile_side, lanes), f32)
    _, red, green, blue = lax.fori_loop(0, slots // 8 // render_unroll, render, (zero + 1.0, zero, zero, zero))
    image = jnp.stack([red, green, blue])
    ext_x[:, 16:32, :] = image
    image_down = remote(ext_x.at[:, 16:32, :], ext_x.at[:, 0:16, :], 5, {"gauss": below})
    image_up = remote(ext_x.at[:, 16:32, :], ext_x.at[:, 32:48, :], 6, {"gauss": above})
    image_down.start()
    image_up.start()
    image_ref[0] = image

    def look_behind(step, carry):
        behind = list(carry)
        for part in range(behind_unroll):
            first = pl.multiple_of((slots // 8 - 1 - step * behind_unroll - part) * 8, 8)
            block = [wide[item, pl.ds(first, 8), :] for item in (5, 6, 7)]
            for i in reversed(range(8)):
                alpha = alpha_s[first + i]
                weight = weight_s[first + i]
                for channel in range(3):
                    gain = block[channel][i : i + 1] - behind[channel]
                    behind[channel] = behind[channel] + alpha * gain
                    gains[channel, first + i] = weight * gain
        return tuple(behind)

    lax.fori_loop(0, slots // 8 // behind_unroll, look_behind, (zero, zero, zero))
    target_down.wait_recv()
    target_up.wait_recv()
    ext_y[:, 0:16, :] = ext_y[:, 0:16, :] * jnp.where(me > 0, 1.0, 0.0)
    ext_y[:, 32:48, :] = ext_y[:, 32:48, :] * jnp.where(me < peers - 1, 1.0, 0.0)
    photo = ext_y[...]
    planes_y[0:3] = photo
    planes_y[3:6] = photo * photo
    blurred_y = blur_columns(blur_rows(planes_y, 6, 32), band)
    mean_y = blurred_y[0:3]
    var_y = blurred_y[3:6] - mean_y * mean_y

    back_stack[...] = jnp.zeros((8, 16, lanes), f32)
    for item in range(9):
        choosers[item] = (inner == 8 * item + (outer >> 4)).astype(jnp.bfloat16)

    image_down.wait_recv()
    image_up.wait_recv()
    ext_x[:, 0:16, :] = ext_x[:, 0:16, :] * jnp.where(me > 0, 1.0, 0.0)
    ext_x[:, 32:48, :] = ext_x[:, 32:48, :] * jnp.where(me < peers - 1, 1.0, 0.0)

    shown = ext_x[...]
    planes_x[0:3] = shown
    planes_x[3:6] = shown * shown
    planes_x[6:9] = shown * photo
    blurred_x = blur_columns(blur_rows(planes_x, 6, 32), band)
    mean_x = blurred_x[0:3]
    var_x = blurred_x[3:6] - mean_x * mean_x
    cov_xy = blurred_x[6:9] - mean_x * mean_y
    top_1 = 2.0 * mean_x * mean_y + 0.0001
    top_2 = 2.0 * cov_xy + 0.0009
    inv_1 = 1.0 / (mean_x * mean_x + mean_y * mean_y + 0.0001)
    inv_2 = 1.0 / (var_x + var_y + 0.0009)
    inv_both = inv_1 * inv_2
    ssim = top_1 * top_2 * inv_both
    map_row = iota((3, 32, lanes), 1) + (me * tile_side - 5)
    in_view = (map_row >= 0) & (map_row < peers * tile_side)
    share = jnp.where(in_view, -0.2 / 256.0, 0.0)
    d_cov = share * 2.0 * top_1 * inv_both
    d_var = -share * ssim * inv_2
    d_mean = (
        share * (2.0 * mean_y * top_2 * inv_both - 2.0 * mean_x * ssim * inv_1)
        - 2.0 * mean_x * d_var
        - mean_y * d_cov
    )
    partials[0:3] = d_mean
    partials[3:6] = d_var
    partials[6:9] = d_cov
    pulled = blur_columns(blur_rows(partials, 0, 16), band)
    own_photo = target_ref[0]
    gap = image - own_photo
    loss_grad = (
        pulled[0:3]
        + 2.0 * image * pulled[3:6]
        + own_photo * pulled[6:9]
        + (0.8 / 256.0) * gap / jnp.sqrt(gap * gap + 0.0025)
    )
    grad_0, grad_1, grad_2 = loss_grad[0], loss_grad[1], loss_grad[2]

    half = tile_side // 2
    row_at = iota((half, lanes), 0).astype(f32) + (0.5 - half)
    row_high = row_at + half
    row_at_2 = row_at * row_at
    row_high_2 = row_high * row_high
    grads_low = [grad_0[:half], grad_1[:half], grad_2[:half]]
    grads_high = [grad_0[half:], grad_1[half:], grad_2[half:]]

    def render_back(step, carry):
        for part in range(back_unroll):
            first = pl.multiple_of((step * back_unroll + part) * 8, 8)
            kept = [[None] * 8 for _ in range(6)]
            for i in range(8):
                weight = weight_s[first + i]
                low, high = 0.0, 0.0
                for channel in range(3):
                    gain = gains[channel, first + i]
                    low = low + gain[:half] * grads_low[channel]
                    high = high + gain[half:] * grads_high[channel]
                    kept[3 + channel][i] = (
                        weight[:half] * grads_low[channel] + weight[half:] * grads_high[channel]
                    )
                kept[0][i] = low + high
                kept[1][i] = low * row_at + high * row_high
                kept[2][i] = low * row_at_2 + high * row_high_2
            for item in range(6):
                sums[item, pl.ds(first, 8), :] = row_sums(kept[item])
        return carry

    lax.fori_loop(0, slots // 8 // back_unroll, render_back, 0)

    to_centre = (me * tile_side + half).astype(f32) - wide[3]
    sum_0 = sums[0]
    sum_1 = sums[1] + to_centre * sum_0
    sum_2 = sums[2] + to_centre * (sums[1] + sum_1)
    sum_0u = sum_0 * off_u
    quantities = [
        sum_0, sum_0u, sum_0u * off_u, sum_1, sum_1 * off_u, sum_2, sums[3], sums[4], sums[5]
    ]
    gathered = jnp.zeros((slots, lanes), f32)
    for item in range(9):
        for part in halves(quantities[item]):
            gathered = gathered + jnp.dot(part, choosers[item], preferred_element_type=f32)
    per_tile = gathered.T
    m_0, m_u, m_uu, m_v, m_uv, m_vv = [per_tile[8 * item : 8 * item + 8] for item in range(6)]
    slot_grads = [
        features[2] * m_u + features[3] * m_v,
        features[4] * m_v + features[3] * m_u,
        -0.5 * m_uu,
        -m_uv,
        -0.5 * m_vv,
        m_0,
        per_tile[48:56],
        per_tile[56:64],
        per_tile[64:72],
    ]

    at_tile = [(sent_tile == tile) & (sent_there > 0.5) for tile in range(tiles)]
    for feature in range(9):
        picked = jnp.zeros((8, lanes), f32)
        for tile in range(tiles):
            row = jnp.broadcast_to(slot_grads[feature][tile : tile + 1], (8, lanes))
            picked = jnp.where(at_tile[tile], lane_pick(row, sent_slot), picked)
        back_stack[:, feature, :] = picked
    turned = back_stack[...].reshape(lanes, lanes).T
    back_out[:, 0, :] = turned[0:peers]
    back_out[:, 1, :] = turned[peers:]
    exchange(back_out, back_in, 7, "gauss")

    @pl.when(jnp.logical_not(hub))
    def _():
        remote(ids_own, ids_own, 10, some).wait_recv()

    @pl.when(hub)
    def _():
        names[0].wait_recv()

    wanted = by_rank(ids_own[...].reshape(peers, lanes))
    want_chunk = wanted[0:8].astype(jnp.int32)
    want_lane = wanted[16:24].astype(jnp.int32)
    want_there = wanted[32:40]
    for row in range(8):
        spots[:, row * lanes : (row + 1) * lanes] = (
            outer == want_lane[row : row + 1]
        ).astype(jnp.bfloat16)
        for chunk in range(8):
            here = (want_chunk[row : row + 1] == chunk) & (want_there[row : row + 1] > 0.5)
            in_chunk[row, chunk] = jnp.broadcast_to(jnp.where(here, 1.0, 0.0), (16, lanes)).astype(
                jnp.bfloat16
            )
    bulk(back_out, back_in, 7, "gauss").wait_recv()
    returned = jnp.concatenate([back_in[:, 0, :], back_in[:, 1, :]], axis=0).T
    pieces = [[], []]
    for row in range(8):
        for part, split in enumerate(halves(returned[16 * row : 16 * row + 16])):
            pieces[part].append(
                jnp.concatenate([split * in_chunk[row, chunk] for chunk in range(8)], axis=0)
            )
    block_grad = sum(dot_nt(jnp.concatenate(piece, axis=1), spots[...]) for piece in pieces)
    view_out[...] = block_grad.reshape(views, 16, lanes)
    exchange(view_out, view_in, 8, "cam")

    bulk(cam_all, cam_all, 3, "cam").wait_recv()
    every = cam_all[...].reshape(views, lanes)
    cameras = camera_terms(
        [jnp.broadcast_to(every[:, column : column + 1], (views, lanes)) for column in range(8)]
    )
    own = attr_ref[:, pl.ds(pl.multiple_of(view * lanes, lanes), lanes)]
    own_rows = [own[row : row + 1] for row in range(59)]
    wide_rows = [jnp.broadcast_to(row, (views, lanes)) for row in own_rows]
    _, pull = jax.vjp(lambda values: project(values, cameras), wide_rows)
    @pl.when(hub)
    def _():
        remote(req_out.at[pl.ds(0, 15)], req_out.at[pl.ds(0, 15)], 0, some).wait_send()
        remote(ans_out.at[pl.ds(0, 31)], ans_out.at[pl.ds(0, 31)], 4, some).wait_send()
        remote(ids_out.at[pl.ds(1, 3)], ids_out.at[pl.ds(1, 3)], 10, some).wait_send()
        push_across.wait_send()

    @pl.when(jnp.logical_not(hub))
    def _():
        remote(req_out, req_out, 0, some).wait_send()
        remote(table_in.at[pl.ds(0, 2)], table_in.at[pl.ds(0, 2)], 9, some).wait_send()

    bulk(back_out, back_in, 7, "gauss").wait_send()
    bulk(cam_all, cam_all, 3, "cam").wait_send()
    target_down.wait_send()
    target_up.wait_send()
    image_down.wait_send()
    image_up.wait_send()
    bulk(view_out, view_in, 8, "cam").wait_recv()
    cots = [view_in[:, item, :] for item in range(9)]
    (row_grads,) = pull(cots[0:5] + cots[6:9])
    own_opacity = 1.0 / (1.0 + jnp.exp(-wide_rows[10]))
    row_grads[10] = cots[5] * (1.0 - own_opacity)
    row_grads = row_grads + [jnp.zeros((views, lanes), f32)] * 5
    for first in range(0, 64, 8):
        count = min(8, 59 - first)
        grad_ref[first : first + count, :] = row_sums(row_grads[first : first + 8])[:count]
    bulk(view_out, view_in, 8, "cam").wait_send()


def store_kernel(image_ref, grad_ref, image_out, grad_out, sems):
    store_image = pltpu.make_async_copy(image_ref, image_out, sems.at[0])
    store_grads = pltpu.make_async_copy(grad_ref, grad_out, sems.at[1])
    store_image.start()
    store_grads.start()
    store_image.wait()
    store_grads.wait()


def local(attributes, cameras, tile_ids, depth_order, target):
    vmem = pl.BlockSpec(memory_space=pltpu.VMEM)
    scratch = [
        (1, lanes),
        (views, 1, lanes),
        (16, 4, lanes),
        (32, 4, lanes),
        (4, 32, 1, lanes),
        (2, 32, 1, lanes),
        (peers, 1, lanes),
        (4, 9, 8, lanes),
        (2, 9, 8, 8, lanes),
        (32, 8, lanes),
        (16, 8, lanes),
        (peers, 2, lanes),
        (peers, 2, lanes),
        (views, 16, lanes),
        (views, 16, lanes),
        (3, 48, lanes),
        (3, 48, lanes),
        (59, 8, lanes),
        (lanes, lanes),
        (8, slots, lanes),
        (slots, tile_side, lanes),
        (slots, tile_side, lanes),
        (3, slots, tile_side, lanes),
        (6, slots, lanes),
        (9, slots, lanes, jnp.bfloat16),
        (lanes, 8 * lanes, jnp.bfloat16),
        (8, 8, 16, lanes, jnp.bfloat16),
        (8, 16, lanes),
        (6, 48, lanes),
        (9, 48, lanes),
        (9, 32, lanes),
    ]
    operands = (
        attributes,
        cameras,
        tile_ids.reshape(tiles, slots),
        depth_order.reshape(tiles, slots),
        target,
    )
    image, grads = pl.pallas_call(
        step_kernel,
        out_shape=(
            pltpu.VMEM((1, 3, tile_side, lanes), f32),
            pltpu.VMEM((59, lanes), f32),
        ),
        in_specs=[pl.BlockSpec(memory_space=pltpu.HBM)] * 5,
        out_specs=(vmem, vmem),
        scratch_shapes=[
            pltpu.VMEM((59, 8 * lanes), f32),
            pltpu.VMEM((1, 8), f32),
            pltpu.VMEM((tiles, slots), jnp.int32),
            pltpu.VMEM((tiles, slots), jnp.int32),
            pltpu.VMEM((1, 3, tile_side, lanes), f32),
        ]
        + [
            pltpu.VMEM(shape, f32)
            if isinstance(shape[-1], int)
            else pltpu.VMEM(shape[:-1], shape[-1])
            for shape in scratch
        ]
        + [
            pltpu.SemaphoreType.DMA((5,)),
            pltpu.SemaphoreType.DMA((11,)),
            pltpu.SemaphoreType.DMA((11,)),
        ],
        compiler_params=pltpu.CompilerParams(
            collective_id=0, has_side_effects=True, vmem_limit_bytes=40 * 1024 * 1024
        ),
    )(*[pltpu.with_memory_space_constraint(operand, pltpu.HBM) for operand in operands])
    hbm = pl.BlockSpec(memory_space=pltpu.HBM)
    return pl.pallas_call(
        store_kernel,
        out_shape=(
            jax.ShapeDtypeStruct((1, 3, tile_side, lanes), f32),
            jax.ShapeDtypeStruct((59, lanes), f32),
        ),
        in_specs=[vmem, vmem],
        out_specs=(hbm, hbm),
        scratch_shapes=[pltpu.SemaphoreType.DMA((2,))],
    )(
        pltpu.with_memory_space_constraint(image, pltpu.VMEM),
        pltpu.with_memory_space_constraint(grads, pltpu.VMEM),
    )


def solution(mesh):
    return jax.shard_map(
        local,
        mesh=mesh,
        in_specs=(
            P(None, "gauss"),
            P("cam", None),
            P("cam", "gauss", None, None),
            P("cam", "gauss", None, None),
            P("cam", None, "gauss", None),
        ),
        out_specs=(P("cam", None, "gauss", None), P(None, ("gauss", "cam"))),
        check_vma=False,
    )
```

```python
import math

import jax
import jax.numpy as jnp
from jax import lax
from jax.experimental import pallas as pl
from jax.experimental.pallas import tpu as pltpu
from jax.sharding import PartitionSpec as P

MESH = pl.DeviceIdType.MESH
peers = 64
views = 8
tile_side = 16
tiles = 8
slots = 128
lanes = 128
capacity = 16
render_unroll = 16
behind_unroll = 2
back_unroll = 16
image_width = 128.0
image_height = 1024.0
f32 = jnp.float32
window_raw = [math.exp(-((offset - 5) ** 2) / 4.5) for offset in range(11)]
window = [weight / sum(window_raw) for weight in window_raw]
sh_consts = [
    0.0,
    -0.4886025119029199,
    0.4886025119029199,
    -0.4886025119029199,
    1.0925484305920792,
    -1.0925484305920792,
    0.31539156525252005,
    -1.0925484305920792,
    0.5462742152960396,
    -0.5900435899266435,
    2.890611442640554,
    -0.4570457994644658,
    0.3731763325901154,
    -0.4570457994644658,
    1.445305721320277,
    -0.5900435899266435,
]


def unit_quat(parts):
    length_q = jnp.sqrt(
        parts[0] * parts[0] + parts[1] * parts[1] + parts[2] * parts[2] + parts[3] * parts[3]
    )
    return [part / length_q for part in parts]


def quat_matrix(quaternion):
    q_w, q_x, q_y, q_z = quaternion
    return [
        [
            1.0 - 2.0 * (q_y * q_y + q_z * q_z),
            2.0 * (q_x * q_y - q_w * q_z),
            2.0 * (q_x * q_z + q_w * q_y),
        ],
        [
            2.0 * (q_x * q_y + q_w * q_z),
            1.0 - 2.0 * (q_x * q_x + q_z * q_z),
            2.0 * (q_y * q_z - q_w * q_x),
        ],
        [
            2.0 * (q_x * q_z - q_w * q_y),
            2.0 * (q_y * q_z + q_w * q_x),
            1.0 - 2.0 * (q_x * q_x + q_y * q_y),
        ],
    ]


def camera_terms(camera):
    cam_rot = quat_matrix(unit_quat(camera[0:4]))
    shift_vec = camera[4:7]
    centre = [
        -(
            cam_rot[0][axis_col] * shift_vec[0]
            + cam_rot[1][axis_col] * shift_vec[1]
            + cam_rot[2][axis_col] * shift_vec[2]
        )
        for axis_col in range(3)
    ]
    return cam_rot, shift_vec, camera[7] * image_width, camera[7] * image_height, centre


def project(attr_rows, camera):
    cam_rot, shift_vec, horizontal_focal, focal_y, centre = camera
    position = [attr_rows[0], attr_rows[1], attr_rows[2]]
    view_pos = [
        cam_rot[axis_row][0] * position[0]
        + cam_rot[axis_row][1] * position[1]
        + cam_rot[axis_row][2] * position[2]
        + shift_vec[axis_row]
        for axis_row in range(3)
    ]
    inv_z = 1.0 / view_pos[2]
    focal_u = horizontal_focal * inv_z
    focal_v = focal_y * inv_z
    slope_u = focal_u * view_pos[0]
    slope_v = focal_v * view_pos[1]
    mean_u = 0.5 * image_width + slope_u
    mean_v = 0.5 * image_height + slope_v
    gauss_rot = quat_matrix(unit_quat([attr_rows[6], attr_rows[7], attr_rows[8], attr_rows[9]]))
    scales = [jnp.exp(attr_rows[3]), jnp.exp(attr_rows[4]), jnp.exp(attr_rows[5])]
    skew_u = slope_u * inv_z
    skew_v = slope_v * inv_z
    project_mat = [
        [focal_u * cam_rot[0][axis_col] - skew_u * cam_rot[2][axis_col] for axis_col in range(3)],
        [focal_v * cam_rot[1][axis_col] - skew_v * cam_rot[2][axis_col] for axis_col in range(3)],
    ]
    spread = [
        [
            (
                project_mat[axis_row][0] * gauss_rot[0][axis_col]
                + project_mat[axis_row][1] * gauss_rot[1][axis_col]
                + project_mat[axis_row][2] * gauss_rot[2][axis_col]
            )
            * scales[axis_col]
            for axis_col in range(3)
        ]
        for axis_row in range(2)
    ]
    cov_a = spread[0][0] * spread[0][0] + spread[0][1] * spread[0][1] + spread[0][2] * spread[0][2] + 0.3
    cov_b = spread[0][0] * spread[1][0] + spread[0][1] * spread[1][1] + spread[0][2] * spread[1][2]
    cov_c = spread[1][0] * spread[1][0] + spread[1][1] * spread[1][1] + spread[1][2] * spread[1][2] + 0.3
    inv_det = 1.0 / (cov_a * cov_c - cov_b * cov_b)
    offsets = [position[axis_col] - centre[axis_col] for axis_col in range(3)]
    distance = jnp.sqrt(offsets[0] * offsets[0] + offsets[1] * offsets[1] + offsets[2] * offsets[2])
    inv_distance = 1.0 / distance
    dir_x, dir_y, dir_z = [offset * inv_distance for offset in offsets]
    sq_x, sq_y, sq_z = (dir_x * dir_x, dir_y * dir_y, dir_z * dir_z)
    sh_basis = [
        None,
        dir_y,
        dir_z,
        dir_x,
        dir_x * dir_y,
        dir_y * dir_z,
        2.0 * sq_z - sq_x - sq_y,
        dir_x * dir_z,
        sq_x - sq_y,
        dir_y * (3.0 * sq_x - sq_y),
        dir_x * dir_y * dir_z,
        dir_y * (4.0 * sq_z - sq_x - sq_y),
        dir_z * (2.0 * sq_z - 3.0 * sq_x - 3.0 * sq_y),
        dir_x * (4.0 * sq_z - sq_x - sq_y),
        dir_z * (sq_x - sq_y),
        dir_x * (sq_x - 3.0 * sq_y),
    ]
    scaled = [None] + [sh_consts[degree] * sh_basis[degree] for degree in range(1, 16)]
    colours = []
    for channel in range(3):
        colour = 0.5 + 0.28209479177387814 * attr_rows[11 + channel]
        for degree in range(1, 16):
            colour = colour + scaled[degree] * attr_rows[11 + 3 * degree + channel]
        colours.append(colour)
    return [mean_u, mean_v, cov_c * inv_det, -cov_b * inv_det, cov_a * inv_det] + colours


def iota(shape, dim):
    return lax.broadcasted_iota(jnp.int32, shape, dim)


def lane_pick(values, index):
    return jnp.take_along_axis(values, index, axis=1, mode="promise_in_bounds")


def halves(values):
    high = values.astype(jnp.bfloat16)
    low = (values - high.astype(f32)).astype(jnp.bfloat16)
    return high, low


def dot_nt(left, right):
    return lax.dot_general(left, right, (((1,), (1,)), ((), ())), preferred_element_type=f32)


def row_sums(blocks):
    row = iota((8, lanes), 0)
    level = []
    for i in range(4):
        first, second = blocks[i], blocks[i + 4]
        level.append(
            jnp.where(row < 4, first, second)
            + pltpu.roll(jnp.where(row < 4, second, first), 4, 0)
        )
    pairs = []
    for i in range(2):
        first, second = level[i], level[i + 2]
        first = first + pltpu.roll(first, 6, 0)
        second = second + pltpu.roll(second, 2, 0)
        pairs.append(jnp.where((row & 2) == 0, first, second))
    first = pairs[0] + pltpu.roll(pairs[0], 7, 0)
    second = pairs[1] + pltpu.roll(pairs[1], 1, 0)
    return jnp.where((row & 1) == 0, first, second)


def blur_rows(ref, start, count):
    total = window[5] * ref[:, pl.ds(start + 5, count), :]
    for offset in range(5):
        total = total + window[offset] * (
            ref[:, pl.ds(start + offset, count), :]
            + ref[:, pl.ds(start + 10 - offset, count), :]
        )
    return total


def blur_columns(planes, band):
    count, rows, _ = planes.shape
    flat = planes.reshape(count * rows, lanes)
    out = jnp.dot(flat, band, preferred_element_type=f32, precision=lax.Precision.HIGHEST)
    return out.reshape(count, rows, lanes)


def step_kernel(
    attr_hbm,
    cam_hbm,
    ids_hbm,
    order_hbm,
    target_hbm,
    image_ref,
    grad_ref,
    attr_ref,
    cam_ref,
    ids_ref,
    order_ref,
    target_ref,
    cam_row,
    cam_all,
    req_out,
    req_in,
    ids_out,
    ids_own,
    asked_rows,
    table_in,
    table_rows,
    ans_out,
    ans_in,
    back_out,
    back_in,
    view_out,
    view_in,
    ext_x,
    ext_y,
    attr_rows,
    stack,
    wide,
    alpha_s,
    weight_s,
    gains,
    sums,
    choosers,
    spots,
    in_chunk,
    back_stack,
    planes_y,
    planes_x,
    partials,
    load_sems,
    send_sems,
    recv_sems,
):
    me = lax.axis_index("gauss")
    view = lax.axis_index("cam")
    loads = [
        pltpu.make_async_copy(source, into, load_sems.at[item])
        for item, (source, into) in enumerate(
            (
                (ids_hbm, ids_ref),
                (order_hbm, order_ref),
                (target_hbm, target_ref),
                (cam_hbm, cam_ref),
                (attr_hbm, attr_ref),
            )
        )
    ]
    my_z = lax.div(me, 8)
    my_y = lax.rem(me, 8)
    my_x = lax.div(view, 2)
    my_core = lax.rem(view, 2)
    along_y = [lax.rem(my_y + step, 8) for step in (4, 3, 5, 2, 6, 1, 7)]
    along_x = [lax.rem(my_x + step, 4) * 2 for step in (2, 1, 3)]

    def each_peer(visit):
        def ring(step, carry):
            from_z = 4 + (1 - 2 * lax.rem(step, 2)) * lax.div(step + 1, 2)
            first = lax.rem(my_z + from_z, 8) * 8
            for place in along_y:
                visit(first + place)
            visit(first + my_y)
            return carry

        lax.fori_loop(0, 7, ring, 0)
        for place in along_y:
            visit(my_z * 8 + place)

    hub = my_z < 4
    near = [lax.rem(my_y + step, 8) for step in (7, 0, 1, 2)]
    clients = [lax.rem(my_y + step, 8) for step in (1, 0, 7, 6)]
    far_y = lax.rem(my_y + 4, 8)
    low_z = jnp.where(hub, my_z, 7 - my_z)

    def each_hub(visit):
        def ring(step, carry):
            for place in (3, 0, 2):
                visit(step * 8 + near[place], step * 4 + place)

            @pl.when(step != my_z)
            def _():
                visit(step * 8 + my_y, step * 4 + 1)

            return carry

        lax.fori_loop(0, 4, ring, 0)

    def each_client(visit):
        def ring(step, carry):
            from_z = 4 + (1 - 2 * lax.rem(step, 2)) * lax.div(step + 1, 2)
            its_z = lax.rem(my_z + from_z, 8)
            for place in (3, 0, 2, 1):
                visit(its_z * 8 + clients[place], its_z * 4 + place)
            return carry

        lax.fori_loop(0, 7, ring, 0)
        for place in (3, 0, 2):
            visit(my_z * 8 + clients[place], my_z * 4 + place)

    def seen_from(other):
        turn = lax.rem(lax.rem(other, 8) - my_y + 9, 8)
        return lax.div(turn, 4) * 32 + my_z * 4 + lax.rem(turn, 4)

    def each_view(visit):
        for place in along_x:
            visit(place + my_core)
            visit(place + 1 - my_core)
        visit(my_x * 2 + 1 - my_core)

    below = lax.rem(me + 1, peers)
    above = lax.rem(me + peers - 1, peers)
    next_view = lax.rem(view + 1, views)

    barrier = pltpu.get_barrier_semaphore()

    def greet_peer(other):
        pl.semaphore_signal(barrier, inc=1, device_id={"gauss": other}, device_id_type=MESH)

    def greet_view(other):
        pl.semaphore_signal(barrier, inc=1, device_id={"cam": other}, device_id_type=MESH)

    @pl.when(hub)
    def _():
        greet_peer((7 - my_z) * 8 + far_y)
        greet_peer(my_z * 8 + far_y)
        each_client(lambda other, place: greet_peer(other))

    each_view(greet_view)
    for load in (loads[0], loads[1], loads[3], loads[4], loads[2]):
        load.start()

    def remote(src, dst, phase, where):
        return pltpu.make_async_remote_copy(
            src_ref=src,
            dst_ref=dst,
            send_sem=send_sems.at[phase],
            recv_sem=recv_sems.at[phase],
            device_id=where,
            device_id_type=MESH,
        )

    def exchange(out, into, phase, axis):
        own = me if axis == "gauss" else view

        def send(other):
            place = seen_from(other) if axis == "gauss" else own
            remote(out.at[other], into.at[place], phase, {axis: other}).start()

        if axis == "gauss":
            each_peer(send)
        else:
            each_view(send)
        into[pl.ds(seen_from(me) if axis == "gauss" else own, 1)] = out[pl.ds(own, 1)]

    def bulk(out, into, phase, axis):
        count = peers if axis == "gauss" else views
        return remote(
            out.at[pl.ds(0, count - 1)],
            into.at[pl.ds(0, count - 1)],
            phase,
            {axis: below if axis == "gauss" else next_view},
        )

    loads[0].wait()
    loads[1].wait()
    ids = lane_pick(ids_ref[...], order_ref[...])
    present = ids >= 0
    owner = ids >> 10
    local_id = ids & 1023
    chunk_id = (local_id >> 7).astype(f32)
    lane_id = (local_id & 127).astype(f32)
    owner_row = iota((peers, slots), 0)
    before = (iota((slots, slots), 0) < iota((slots, slots), 1)).astype(jnp.bfloat16)
    rank_rows = iota((capacity, slots), 0)
    slot_row = iota((1, slots), 1).astype(f32)
    base = jnp.zeros((peers, 1), f32)
    asked = jnp.zeros((peers, lanes), f32)
    ranks = []
    for tile in range(tiles):
        named = owner_row == owner[tile : tile + 1]
        member = jnp.where(named, 1.0, 0.0)
        earlier = jnp.dot(member.astype(jnp.bfloat16), before, preferred_element_type=f32)
        rank = jnp.sum(member * (earlier + base), axis=0, keepdims=True)
        base = base + jnp.sum(member, axis=1, keepdims=True)
        ranks.append(rank)
        hit = rank_rows == rank.astype(jnp.int32)
        terms = [
            jnp.where(hit, chunk_id[tile : tile + 1], 0.0),
            jnp.where(hit, lane_id[tile : tile + 1], 0.0),
            jnp.where(hit, 1.0, 0.0),
            jnp.where(hit, float(tile), 0.0),
            jnp.where(hit, slot_row, 0.0),
            jnp.zeros((lanes - 5 * capacity, slots), f32),
        ]
        asked = asked + dot_nt(
            member.astype(jnp.bfloat16), jnp.concatenate(terms, axis=0).astype(jnp.bfloat16)
        )
    rank = jnp.concatenate(ranks, axis=0).astype(jnp.int32)
    asked_rows[...] = asked.reshape(peers, 1, lanes)
    for step in range(4):
        for place in range(4):
            across = lax.rem(near[place] + 4, 8)
            blocks = (
                step * 8 + near[place],
                step * 8 + across,
                (7 - step) * 8 + near[place],
                (7 - step) * 8 + across,
            )
            for item, block in enumerate(blocks):
                req_out[4 * step + place, item : item + 1] = asked_rows[block]
    loads[2].wait()
    loads[3].wait()
    cam_row[...] = jnp.zeros((1, lanes), f32)
    cam_row[:, 0:8] = cam_ref[...]
    cam_all[pl.ds(view, 1)] = cam_row[...].reshape(1, 1, lanes)
    ext_y[:, 16:32, :] = target_ref[0]

    loads[4].wait()
    for chunk in range(8):
        attr_rows[:, chunk, :] = attr_ref[:, chunk * lanes : (chunk + 1) * lanes]
    camera = [
        jnp.broadcast_to(cam_row[0:1, column : column + 1], (8, lanes)) for column in range(8)
    ]
    rows = [attr_rows[row] for row in range(59)]
    flat_features = project(rows, camera_terms(camera))
    opacity = 1.0 / (1.0 + jnp.exp(-rows[10]))
    table = flat_features[0:5] + [opacity] + flat_features[5:8]
    for feature in range(9):
        table_in[0, feature] = table[feature]
    pl.semaphore_wait(barrier, 17 + views - 1 - jnp.where(hub, 1, 0))

    each_hub(
        lambda other, place: remote(
            req_out.at[place], req_in.at[my_z * 4 + lax.rem(place, 4)], 0, {"gauss": other}
        ).start()
    )
    push_near = remote(table_in.at[0], table_in.at[2], 9, {"gauss": low_z * 8 + my_y})
    push_far = remote(table_in.at[0], table_in.at[3], 9, {"gauss": low_z * 8 + far_y})
    push_across = remote(table_in.at[0], table_in.at[1], 9, {"gauss": low_z * 8 + far_y})
    names = [
        remote(ids_out.at[item], ids_own.at[item % 2], 10, {"gauss": block})
        for item, block in (
            (1, low_z * 8 + far_y),
            (2, (7 - low_z) * 8 + my_y),
            (3, (7 - low_z) * 8 + far_y),
        )
    ]

    @pl.when(jnp.logical_not(hub))
    def _():
        push_near.start()
        push_far.start()

    @pl.when(hub)
    def _():
        push_across.start()

    target_down = remote(ext_y.at[:, 16:32, :], ext_y.at[:, 0:16, :], 1, {"gauss": below})
    target_up = remote(ext_y.at[:, 16:32, :], ext_y.at[:, 32:48, :], 2, {"gauss": above})

    each_view(lambda other: remote(cam_row, cam_all.at[view], 3, {"cam": other}).start())

    def by_rank(values):
        return jnp.concatenate([values, pltpu.roll(values, lanes - 8, 1)], axis=0).T

    some = {"gauss": below}

    def hub_step():
        own_place = my_z * 4 + 1
        req_in[pl.ds(own_place, 1)] = req_out[pl.ds(own_place, 1)]
        stack[...] = jnp.zeros((lanes, lanes), f32)
        remote(table_in.at[pl.ds(1, 3)], table_in.at[pl.ds(1, 3)], 9, some).wait_recv()
        upper = iota((8, lanes), 0) < 4
        for pair in range(2):
            for feature in range(9):
                for chunk in range(8):
                    table_rows[pair, feature, chunk] = jnp.where(
                        upper,
                        table_in[2 * pair, feature, chunk : chunk + 1],
                        table_in[2 * pair + 1, feature, chunk : chunk + 1],
                    )
        remote(req_in.at[pl.ds(0, 31)], req_in.at[pl.ds(0, 31)], 0, some).wait_recv()
        first_block = (iota((32, lanes), 1) & 4) == 0
        for pair in range(2):
            near_rows, far_rows = req_in[:, 2 * pair, :], req_in[:, 2 * pair + 1, :]
            asked_here = jnp.concatenate(
                [
                    jnp.where(
                        first_block,
                        pltpu.roll(near_rows, (lanes - 4 * part) % lanes, 1),
                        pltpu.roll(far_rows, (lanes + 4 - 4 * part) % lanes, 1),
                    )
                    for part in range(4)
                ],
                axis=0,
            ).T
            asked_chunk = asked_here[0:8].astype(jnp.int32)
            asked_lane = asked_here[16:24].astype(jnp.int32)
            at_chunk = [asked_chunk == chunk for chunk in range(8)]
            for feature in range(9):
                picked = jnp.zeros((8, lanes), f32)
                for chunk in range(8):
                    row = table_rows[pair, feature, chunk]
                    picked = jnp.where(at_chunk[chunk], lane_pick(row, asked_lane), picked)
                stack[8 * feature : 8 * feature + 8] = picked
            turned = stack[...].T
            for part in range(4):
                ans_out[:, 4 * pair + part, :] = turned[32 * part : 32 * part + 32]
        each_client(
            lambda other, place: remote(
                ans_out.at[place], ans_in.at[my_z * 4 + lax.rem(place, 4)], 4, {"gauss": other}
            ).start()
        )
        ans_in[pl.ds(own_place, 1)] = ans_out[pl.ds(own_place, 1)]
        for block in range(4):
            ids_out[block] = req_in[:, block, :].reshape(32, 1, lanes)
        for name in names:
            name.start()
        ids_own[0] = ids_out[0]

    pl.when(hub)(hub_step)

    outer = iota((slots, lanes), 0)
    inner = iota((slots, lanes), 1)
    band = jnp.zeros((lanes, lanes), f32)
    for offset in range(11):
        band = jnp.where(inner - outer == offset - 5, window[offset], band)
    sent = by_rank(asked)
    sent_there = sent[32:40]
    sent_tile = sent[48:56].astype(jnp.int32)
    sent_slot = sent[64:72].astype(jnp.int32)

    @pl.when(hub)
    def _():
        remote(ans_in.at[pl.ds(0, 15)], ans_in.at[pl.ds(0, 15)], 4, some).wait_recv()

    @pl.when(jnp.logical_not(hub))
    def _():
        remote(ans_in, ans_in, 4, some).wait_recv()

    target_down.start()
    target_up.start()
    by_owner = [ans_in[:, row, :] for row in range(8)]
    answers = jnp.concatenate(by_owner, axis=0).T
    owner_z, owner_y = owner >> 3, owner & 7
    turn = (owner_y - my_y + 9) & 7
    beyond = owner_z >= 4
    from_hub = jnp.where(beyond, 7 - owner_z, owner_z) * 4 + (turn & 3)
    from_lane = jnp.where(present, (jnp.where(beyond, 4, 0) + (rank >> 2)) * 16 + from_hub, 0)
    from_row = jnp.where(present, (turn >> 2) * 4 + (rank & 3), 8)
    at_row = [from_row == row for row in range(8)]
    features = []
    stack[72:128] = jnp.zeros((56, lanes), f32)
    for feature in range(9):
        picked = jnp.zeros((8, lanes), f32)
        for row in range(8):
            source = jnp.broadcast_to(
                answers[8 * feature + row : 8 * feature + row + 1], (8, lanes)
            )
            picked = jnp.where(at_row[row], lane_pick(source, from_lane), picked)
        stack[8 * feature : 8 * feature + 8] = picked
        features.append(picked)
    by_slot = stack[...].T
    spread = [lane_pick(by_slot, 8 * feature + (inner >> 4)) for feature in range(9)]
    slot_u, slot_v, conic_a, conic_b, conic_c, slot_opacity = spread[0:6]
    off_u = inner.astype(f32) + 0.5 - slot_u
    wide[0] = -0.5 * conic_a * off_u * off_u
    wide[1] = -conic_b * off_u
    wide[2] = -0.5 * conic_c
    wide[3] = slot_v
    wide[4] = slot_opacity
    wide[5] = spread[6]
    wide[6] = spread[7]
    wide[7] = spread[8]
    pixel_row = (iota((tile_side, lanes), 0) + me * tile_side).astype(f32) + 0.5

    def render(step, carry):
        transmit, red, green, blue = carry
        for part in range(render_unroll):
            first = pl.multiple_of((step * render_unroll + part) * 8, 8)
            block = [wide[item, pl.ds(first, 8), :] for item in range(8)]
            for i in range(8):
                flat, slope, curve, mean_v, alpha_top, c_0, c_1, c_2 = [
                    item[i : i + 1] for item in block
                ]
                off_v = pixel_row - mean_v
                alpha = alpha_top * jnp.exp(flat + off_v * (slope + curve * off_v))
                weight = alpha * transmit
                transmit = transmit - weight
                red = red + weight * c_0
                green = green + weight * c_1
                blue = blue + weight * c_2
                alpha_s[first + i] = alpha
                weight_s[first + i] = weight
        return transmit, red, green, blue

    zero = jnp.zeros((tile_side, lanes), f32)
    _, red, green, blue = lax.fori_loop(0, slots // 8 // render_unroll, render, (zero + 1.0, zero, zero, zero))
    image = jnp.stack([red, green, blue])
    ext_x[:, 16:32, :] = image
    image_down = remote(ext_x.at[:, 16:32, :], ext_x.at[:, 0:16, :], 5, {"gauss": below})
    image_up = remote(ext_x.at[:, 16:32, :], ext_x.at[:, 32:48, :], 6, {"gauss": above})
    image_down.start()
    image_up.start()
    image_ref[0] = image

    def look_behind(step, carry):
        behind = list(carry)
        for part in range(behind_unroll):
            first = pl.multiple_of((slots // 8 - 1 - step * behind_unroll - part) * 8, 8)
            block = [wide[item, pl.ds(first, 8), :] for item in (5, 6, 7)]
            for i in reversed(range(8)):
                alpha = alpha_s[first + i]
                weight = weight_s[first + i]
                for channel in range(3):
                    gain = block[channel][i : i + 1] - behind[channel]
                    behind[channel] = behind[channel] + alpha * gain
                    gains[channel, first + i] = weight * gain
        return tuple(behind)

    lax.fori_loop(0, slots // 8 // behind_unroll, look_behind, (zero, zero, zero))
    target_down.wait_recv()
    target_up.wait_recv()
    ext_y[:, 0:16, :] = ext_y[:, 0:16, :] * jnp.where(me > 0, 1.0, 0.0)
    ext_y[:, 32:48, :] = ext_y[:, 32:48, :] * jnp.where(me < peers - 1, 1.0, 0.0)
    photo = ext_y[...]
    planes_y[0:3] = photo
    planes_y[3:6] = photo * photo
    blurred_y = blur_columns(blur_rows(planes_y, 6, 32), band)
    mean_y = blurred_y[0:3]
    var_y = blurred_y[3:6] - mean_y * mean_y

    back_stack[...] = jnp.zeros((8, 16, lanes), f32)
    for item in range(9):
        choosers[item] = (inner == 8 * item + (outer >> 4)).astype(jnp.bfloat16)

    band_high, band_low = halves(band)
    planes_x[0:3, 16:32, :] = image
    planes_x[3:6, 16:32, :] = image * image
    planes_x[6:9, 16:32, :] = image * photo[:, 16:32]

    image_down.wait_recv()
    image_up.wait_recv()
    for first, inside in ((0, me > 0), (32, me < peers - 1)):
        shown = ext_x[:, first : first + 16, :] * jnp.where(inside, 1.0, 0.0)
        planes_x[0:3, first : first + 16, :] = shown
        planes_x[3:6, first : first + 16, :] = shown * shown
        planes_x[6:9, first : first + 16, :] = shown * photo[:, first : first + 16]

    blurred_x = blur_columns(blur_rows(planes_x, 6, 32), band)
    mean_x = blurred_x[0:3]
    var_x = blurred_x[3:6] - mean_x * mean_x
    cov_xy = blurred_x[6:9] - mean_x * mean_y
    top_1 = 2.0 * mean_x * mean_y + 0.0001
    top_2 = 2.0 * cov_xy + 0.0009
    inv_1 = 1.0 / (mean_x * mean_x + mean_y * mean_y + 0.0001)
    inv_2 = 1.0 / (var_x + var_y + 0.0009)
    inv_both = inv_1 * inv_2
    ssim = top_1 * top_2 * inv_both
    map_row = iota((3, 32, lanes), 1) + (me * tile_side - 5)
    in_view = (map_row >= 0) & (map_row < peers * tile_side)
    share = jnp.where(in_view, -0.2 / 256.0, 0.0)
    d_cov = share * 2.0 * top_1 * inv_both
    d_var = -share * ssim * inv_2
    d_mean = (
        share * (2.0 * mean_y * top_2 * inv_both - 2.0 * mean_x * ssim * inv_1)
        - 2.0 * mean_x * d_var
        - mean_y * d_cov
    )
    partials[0:3] = d_mean
    partials[3:6] = d_var
    partials[6:9] = d_cov
    pulled_high, pulled_low = halves(blur_rows(partials, 0, 16).reshape(9 * tile_side, lanes))
    pulled = (
        jnp.dot(pulled_high, band_high, preferred_element_type=f32)
        + jnp.dot(pulled_high, band_low, preferred_element_type=f32)
        + jnp.dot(pulled_low, band_high, preferred_element_type=f32)
    ).reshape(9, tile_side, lanes)
    own_photo = target_ref[0]
    gap = image - own_photo
    loss_grad = (
        pulled[0:3]
        + 2.0 * image * pulled[3:6]
        + own_photo * pulled[6:9]
        + (0.8 / 256.0) * gap / jnp.sqrt(gap * gap + 0.0025)
    )
    grad_0, grad_1, grad_2 = loss_grad[0], loss_grad[1], loss_grad[2]

    half = tile_side // 2
    row_at = iota((half, lanes), 0).astype(f32) + (0.5 - half)
    row_high = row_at + half
    row_at_2 = row_at * row_at
    row_high_2 = row_high * row_high
    grads_low = [grad_0[:half], grad_1[:half], grad_2[:half]]
    grads_high = [grad_0[half:], grad_1[half:], grad_2[half:]]

    def render_back(step, carry):
        for part in range(back_unroll):
            first = pl.multiple_of((step * back_unroll + part) * 8, 8)
            kept = [[None] * 8 for _ in range(6)]
            for i in range(8):
                weight = weight_s[first + i]
                low, high = 0.0, 0.0
                for channel in range(3):
                    gain = gains[channel, first + i]
                    low = low + gain[:half] * grads_low[channel]
                    high = high + gain[half:] * grads_high[channel]
                    kept[3 + channel][i] = (
                        weight[:half] * grads_low[channel] + weight[half:] * grads_high[channel]
                    )
                kept[0][i] = low + high
                kept[1][i] = low * row_at + high * row_high
                kept[2][i] = low * row_at_2 + high * row_high_2
            for item in range(6):
                sums[item, pl.ds(first, 8), :] = row_sums(kept[item])
        return carry

    lax.fori_loop(0, slots // 8 // back_unroll, render_back, 0)

    to_centre = (me * tile_side + half).astype(f32) - wide[3]
    sum_0 = sums[0]
    sum_1 = sums[1] + to_centre * sum_0
    sum_2 = sums[2] + to_centre * (sums[1] + sum_1)
    sum_0u = sum_0 * off_u
    quantities = [
        sum_0, sum_0u, sum_0u * off_u, sum_1, sum_1 * off_u, sum_2, sums[3], sums[4], sums[5]
    ]
    gathered = jnp.zeros((slots, lanes), f32)
    for item in range(9):
        for part in halves(quantities[item]):
            gathered = gathered + jnp.dot(part, choosers[item], preferred_element_type=f32)
    per_tile = gathered.T
    m_0, m_u, m_uu, m_v, m_uv, m_vv = [per_tile[8 * item : 8 * item + 8] for item in range(6)]
    slot_grads = [
        features[2] * m_u + features[3] * m_v,
        features[4] * m_v + features[3] * m_u,
        -0.5 * m_uu,
        -m_uv,
        -0.5 * m_vv,
        m_0,
        per_tile[48:56],
        per_tile[56:64],
        per_tile[64:72],
    ]

    at_tile = [(sent_tile == tile) & (sent_there > 0.5) for tile in range(tiles)]
    for feature in range(9):
        picked = jnp.zeros((8, lanes), f32)
        for tile in range(tiles):
            row = jnp.broadcast_to(slot_grads[feature][tile : tile + 1], (8, lanes))
            picked = jnp.where(at_tile[tile], lane_pick(row, sent_slot), picked)
        back_stack[:, feature, :] = picked
    turned = back_stack[...].reshape(lanes, lanes).T
    back_out[:, 0, :] = turned[0:peers]
    back_out[:, 1, :] = turned[peers:]
    exchange(back_out, back_in, 7, "gauss")

    @pl.when(jnp.logical_not(hub))
    def _():
        remote(ids_own, ids_own, 10, some).wait_recv()

    @pl.when(hub)
    def _():
        names[0].wait_recv()

    wanted = by_rank(ids_own[...].reshape(peers, lanes))
    want_chunk = wanted[0:8].astype(jnp.int32)
    want_lane = wanted[16:24].astype(jnp.int32)
    want_there = wanted[32:40]
    for row in range(8):
        spots[:, row * lanes : (row + 1) * lanes] = (
            outer == want_lane[row : row + 1]
        ).astype(jnp.bfloat16)
        for chunk in range(8):
            here = (want_chunk[row : row + 1] == chunk) & (want_there[row : row + 1] > 0.5)
            in_chunk[row, chunk] = jnp.broadcast_to(jnp.where(here, 1.0, 0.0), (16, lanes)).astype(
                jnp.bfloat16
            )
    bulk(back_out, back_in, 7, "gauss").wait_recv()
    returned = jnp.concatenate([back_in[:, 0, :], back_in[:, 1, :]], axis=0).T
    pieces = [[], []]
    for row in range(8):
        for part, split in enumerate(halves(returned[16 * row : 16 * row + 16])):
            pieces[part].append(
                jnp.concatenate([split * in_chunk[row, chunk] for chunk in range(8)], axis=0)
            )
    block_grad = sum(dot_nt(jnp.concatenate(piece, axis=1), spots[...]) for piece in pieces)
    view_out[...] = block_grad.reshape(views, 16, lanes)
    exchange(view_out, view_in, 8, "cam")

    bulk(cam_all, cam_all, 3, "cam").wait_recv()
    every = cam_all[...].reshape(views, lanes)
    cameras = camera_terms(
        [jnp.broadcast_to(every[:, column : column + 1], (views, lanes)) for column in range(8)]
    )
    own = attr_ref[:, pl.ds(pl.multiple_of(view * lanes, lanes), lanes)]
    own_rows = [own[row : row + 1] for row in range(59)]
    wide_rows = [jnp.broadcast_to(row, (views, lanes)) for row in own_rows]
    _, pull = jax.vjp(lambda values: project(values, cameras), wide_rows)
    @pl.when(hub)
    def _():
        remote(req_out.at[pl.ds(0, 15)], req_out.at[pl.ds(0, 15)], 0, some).wait_send()
        remote(ans_out.at[pl.ds(0, 31)], ans_out.at[pl.ds(0, 31)], 4, some).wait_send()
        remote(ids_out.at[pl.ds(1, 3)], ids_out.at[pl.ds(1, 3)], 10, some).wait_send()
        push_across.wait_send()

    @pl.when(jnp.logical_not(hub))
    def _():
        remote(req_out, req_out, 0, some).wait_send()
        remote(table_in.at[pl.ds(0, 2)], table_in.at[pl.ds(0, 2)], 9, some).wait_send()

    bulk(back_out, back_in, 7, "gauss").wait_send()
    bulk(cam_all, cam_all, 3, "cam").wait_send()
    target_down.wait_send()
    target_up.wait_send()
    image_down.wait_send()
    image_up.wait_send()
    bulk(view_out, view_in, 8, "cam").wait_recv()
    cots = [view_in[:, item, :] for item in range(9)]
    (row_grads,) = pull(cots[0:5] + cots[6:9])
    own_opacity = 1.0 / (1.0 + jnp.exp(-wide_rows[10]))
    row_grads[10] = cots[5] * (1.0 - own_opacity)
    row_grads = row_grads + [jnp.zeros((views, lanes), f32)] * 5
    for first in range(0, 64, 8):
        count = min(8, 59 - first)
        grad_ref[first : first + count, :] = row_sums(row_grads[first : first + 8])[:count]
    bulk(view_out, view_in, 8, "cam").wait_send()


def store_kernel(image_ref, grad_ref, image_out, grad_out, sems):
    store_image = pltpu.make_async_copy(image_ref, image_out, sems.at[0])
    store_grads = pltpu.make_async_copy(grad_ref, grad_out, sems.at[1])
    store_image.start()
    store_grads.start()
    store_image.wait()
    store_grads.wait()


def local(attributes, cameras, tile_ids, depth_order, target):
    vmem = pl.BlockSpec(memory_space=pltpu.VMEM)
    scratch = [
        (1, lanes),
        (views, 1, lanes),
        (16, 4, lanes),
        (32, 4, lanes),
        (4, 32, 1, lanes),
        (2, 32, 1, lanes),
        (peers, 1, lanes),
        (4, 9, 8, lanes),
        (2, 9, 8, 8, lanes),
        (32, 8, lanes),
        (16, 8, lanes),
        (peers, 2, lanes),
        (peers, 2, lanes),
        (views, 16, lanes),
        (views, 16, lanes),
        (3, 48, lanes),
        (3, 48, lanes),
        (59, 8, lanes),
        (lanes, lanes),
        (8, slots, lanes),
        (slots, tile_side, lanes),
        (slots, tile_side, lanes),
        (3, slots, tile_side, lanes),
        (6, slots, lanes),
        (9, slots, lanes, jnp.bfloat16),
        (lanes, 8 * lanes, jnp.bfloat16),
        (8, 8, 16, lanes, jnp.bfloat16),
        (8, 16, lanes),
        (6, 48, lanes),
        (9, 48, lanes),
        (9, 32, lanes),
    ]
    operands = (
        attributes,
        cameras,
        tile_ids.reshape(tiles, slots),
        depth_order.reshape(tiles, slots),
        target,
    )
    image, grads = pl.pallas_call(
        step_kernel,
        out_shape=(
            pltpu.VMEM((1, 3, tile_side, lanes), f32),
            pltpu.VMEM((59, lanes), f32),
        ),
        in_specs=[pl.BlockSpec(memory_space=pltpu.HBM)] * 5,
        out_specs=(vmem, vmem),
        scratch_shapes=[
            pltpu.VMEM((59, 8 * lanes), f32),
            pltpu.VMEM((1, 8), f32),
            pltpu.VMEM((tiles, slots), jnp.int32),
            pltpu.VMEM((tiles, slots), jnp.int32),
            pltpu.VMEM((1, 3, tile_side, lanes), f32),
        ]
        + [
            pltpu.VMEM(shape, f32)
            if isinstance(shape[-1], int)
            else pltpu.VMEM(shape[:-1], shape[-1])
            for shape in scratch
        ]
        + [
            pltpu.SemaphoreType.DMA((5,)),
            pltpu.SemaphoreType.DMA((11,)),
            pltpu.SemaphoreType.DMA((11,)),
        ],
        compiler_params=pltpu.CompilerParams(
            collective_id=0, has_side_effects=True, vmem_limit_bytes=40 * 1024 * 1024
        ),
    )(*[pltpu.with_memory_space_constraint(operand, pltpu.HBM) for operand in operands])
    hbm = pl.BlockSpec(memory_space=pltpu.HBM)
    return pl.pallas_call(
        store_kernel,
        out_shape=(
            jax.ShapeDtypeStruct((1, 3, tile_side, lanes), f32),
            jax.ShapeDtypeStruct((59, lanes), f32),
        ),
        in_specs=[vmem, vmem],
        out_specs=(hbm, hbm),
        scratch_shapes=[pltpu.SemaphoreType.DMA((2,))],
    )(
        pltpu.with_memory_space_constraint(image, pltpu.VMEM),
        pltpu.with_memory_space_constraint(grads, pltpu.VMEM),
    )


def solution(mesh):
    return jax.shard_map(
        local,
        mesh=mesh,
        in_specs=(
            P(None, "gauss"),
            P("cam", None),
            P("cam", "gauss", None, None),
            P("cam", "gauss", None, None),
            P("cam", None, "gauss", None),
        ),
        out_specs=(P("cam", None, "gauss", None), P(None, ("gauss", "cam"))),
        check_vma=False,
    )
```
